32 devices in a mesh: groups: 2 (over x), row: 4 (over y, core), col: 4 (over z).
Axes of the slice: x: 2, y: 2, z: 4, core: 2. Of those that a mesh axis runs over, the one named last changes fastest.
Arguments:
- positions: float32 [3, 16384], P(None, ('groups', 'row', 'col')), parts along dimension 1, may hold values from 0 to 1
- targets: float32 [64, 16384], P(None, ('groups', 'row', 'col')), parts along dimension 1, may hold values from -0.5 to 2
- pairs: int32 [2, 768], P(None, ('groups', 'row', 'col')), parts along dimension 1, may hold values from 0 to 7, as said below
- counts: int32 [32], P(('groups', 'row', 'col')), parts along dimension 0, may hold values from 2 to 24, as said below
Outputs:
- weights: float32 [64, 16384], P(None, ('groups', 'row', 'col')), parts along dimension 1
- residual: float32 [64, 16384], P(None, ('groups', 'row', 'col')), parts along dimension 1
The draws below stay inside these ranges and needn't reach their ends.
There are 2 independent parts, one for each index of `groups`. The reference program is written for one: setup_inputs(seed, part) draws one part's arguments, and reference() takes and returns one part's arrays. A program takes and returns all parts, laid end to end along the dimension named above; each array names one. Nothing has to cross between parts.
Inputs may be any that keep to these rules, and one draw needn't show every extreme that they name: `pairs`: row 0 entries of a device's list lie below 8, row 1 entries below 8. Entries s < 2 of device d name its own block d * 2 + s twice; every other entry names two blocks of different devices. Entries may repeat. `counts`: some device uses all its entries.
All inputs are finite; a program needn't handle non-finite values.
Results may differ from the reference program's by a relative error of at most 0.0003.
Values sent between devices are 32-bit elements; how exact they have to be, the bound alone decides.
No kernel may reach another device: no remote copies, remote signals or barrier semaphores. Data moves between devices by JAX's collectives and lax.ppermute only.
A program may use at most 64 MiB of HBM per device.

```python
import jax
import jax.numpy as jnp
from jax import lax

BLOCK = 256
BLOCK_DEV = 2
TARGET_COLS = 64
ITERS = 3
PAIRS_DEV = 24
BLOCKS = 32
POINTS = 8192
N_ROW = 4
N_COL = 4


def draw_pairs(key, part):
    key = jax.random.fold_in(key, 11)
    devices = N_ROW * N_COL
    first_key, second_key, third_key = jax.random.split(key, 3)
    device_ids = jnp.arange(devices, dtype=jnp.int32)[:, None]
    entry_ids = jnp.arange(PAIRS_DEV, dtype=jnp.int32)[None, :]
    row_of = device_ids // N_COL
    col_of = device_ids % N_COL
    row_ids = jax.random.randint(first_key, (devices, PAIRS_DEV), 0, N_COL * BLOCK_DEV, dtype=jnp.int32)
    other_row = (row_of + 1 + jax.random.randint(second_key, (devices, PAIRS_DEV), 0, N_ROW - 1, dtype=jnp.int32)) % N_ROW
    col_ids = other_row * BLOCK_DEV + jax.random.randint(third_key, (devices, PAIRS_DEV), 0, BLOCK_DEV, dtype=jnp.int32)
    own_entry = entry_ids < BLOCK_DEV
    row_ids = jnp.where(own_entry, col_of * BLOCK_DEV + entry_ids, row_ids)
    col_ids = jnp.where(own_entry, row_of * BLOCK_DEV + entry_ids, col_ids)
    return jnp.stack([row_ids.reshape(-1), col_ids.reshape(-1)]).astype(jnp.int32)


def draw_counts(key, part):
    key = jax.random.fold_in(key, 23)
    devices = N_ROW * N_COL
    headroom = PAIRS_DEV - BLOCK_DEV
    first_key, second_key = jax.random.split(key, 2)
    drawn_level = jax.random.randint(first_key, (devices,), 0, headroom + 1, dtype=jnp.int32)
    surplus = drawn_level * drawn_level // headroom
    busiest = jax.random.randint(second_key, (), 0, devices, dtype=jnp.int32)
    surplus = jnp.where(jnp.arange(devices, dtype=jnp.int32) == busiest, headroom, surplus)
    return (BLOCK_DEV + surplus).astype(jnp.int32)


def steps_of(rng, shape, cuts, low, high):
    gain, own = 1.0, jax.random.fold_in(rng, 6)
    for dim, shards_of in cuts:
        heights = jnp.exp(jax.random.uniform(jax.random.fold_in(own, dim), (shards_of,), jnp.float32, low / len(cuts), high / len(cuts)))
        gain = gain * jnp.repeat(heights, shape[dim] // shards_of).reshape([-1 if axis == dim else 1 for axis in range(len(shape))])
    return gain


def setup_inputs(seed: int = 0, part: int = 0) -> dict:
    splits = jax.random.split(jax.random.key(seed), 5)
    own_keys = jax.random.split(jax.random.fold_in(splits[4], part), 5)
    positions = jnp.clip(1.0 * jax.random.uniform(own_keys[0], (3, POINTS), jnp.float32) ** steps_of(own_keys[0], (3, POINTS), ((1, 16),), -0.2, 0.2), 0.0, 1.0)
    targets = jnp.clip(-0.5 + 2.5 * jax.random.uniform(own_keys[1], (TARGET_COLS, POINTS), jnp.float32) ** steps_of(own_keys[1], (TARGET_COLS, POINTS), ((1, 16),), -0.2, 0.2), -0.5, 2.0)
    pairs = draw_pairs(jax.random.fold_in(jax.random.fold_in(splits[4], part), 71), part)
    counts = draw_counts(jax.random.fold_in(jax.random.fold_in(splits[4], part), 71), part)
    return {"positions": positions, "targets": targets, "pairs": pairs, "counts": counts}


support_radius = 0.5
ridge_shift = 1.5

def wendland(left_points, right_points):
    delta_x = left_points[0][:, None] - right_points[0][None, :]
    delta_y = left_points[1][:, None] - right_points[1][None, :]
    delta_z = left_points[2][:, None] - right_points[2][None, :]
    scaled = jnp.sqrt(delta_x * delta_x + delta_y * delta_y + delta_z * delta_z) * (1.0 / support_radius)
    remain = jnp.maximum(1.0 - scaled, 0.0)
    return remain * remain * remain * remain * (4.0 * scaled + 1.0)

def pair_table(pairs, counts):
    devices = N_ROW * N_COL
    row_ids = pairs[0].reshape(devices, PAIRS_DEV)
    col_ids = pairs[1].reshape(devices, PAIRS_DEV)
    device_ids = jnp.arange(devices, dtype=jnp.int32)
    row_of = (device_ids // N_COL)[:, None]
    col_of = (device_ids % N_COL)[:, None]
    row_global = row_of * (N_COL * BLOCK_DEV) + row_ids
    col_global = (col_ids // BLOCK_DEV * N_COL + col_of) * BLOCK_DEV + col_ids % BLOCK_DEV
    in_list = (jnp.arange(PAIRS_DEV, dtype=jnp.int32)[None, :] < counts[:, None]).astype(jnp.float32)
    mirrored = in_list * (row_global != col_global).astype(jnp.float32)
    return (row_global, col_global, in_list, mirrored)

def degrees(blocks, table):

    def accumulate(totals, entries):
        row_ids, col_ids, live_rows, mirror_rows = entries
        tiles = jax.vmap(wendland)(blocks[row_ids], blocks[col_ids])
        totals = totals.at[row_ids].add(lax.optimization_barrier(jnp.sum(tiles, axis=2)) * live_rows[:, None])
        totals = totals.at[col_ids].add(lax.optimization_barrier(jnp.sum(tiles, axis=1)) * mirror_rows[:, None])
        return (totals, None)
    totals, unused = lax.scan(accumulate, jnp.zeros((BLOCKS, BLOCK), jnp.float32), table)
    return totals.reshape(-1)

def kernel_product(blocks, table, vector):
    vector_blocks = vector.reshape(TARGET_COLS, BLOCKS, BLOCK).transpose(1, 0, 2)

    def accumulate(totals, entries):
        row_ids, col_ids, live_rows, mirror_rows = entries
        tiles = jax.vmap(wendland)(blocks[row_ids], blocks[col_ids])
        row_add = jnp.einsum('pab,pqb->pqa', tiles, vector_blocks[col_ids], precision=lax.Precision.HIGHEST)
        col_add = jnp.einsum('pab,pqa->pqb', tiles, vector_blocks[row_ids], precision=lax.Precision.HIGHEST)
        totals = totals.at[row_ids].add(row_add * live_rows[:, None, None])
        totals = totals.at[col_ids].add(col_add * mirror_rows[:, None, None])
        return (totals, None)
    totals, unused = lax.scan(accumulate, jnp.zeros((BLOCKS, TARGET_COLS, BLOCK), jnp.float32), table)
    return totals.transpose(1, 0, 2).reshape(TARGET_COLS, POINTS)

def reference(positions, targets, pairs, counts):
    blocks = positions.reshape(3, BLOCKS, BLOCK).transpose(1, 0, 2)
    table = pair_table(pairs, counts)
    largest = jnp.max(degrees(blocks, table))
    weights = jnp.zeros_like(targets)
    residual = targets
    direction = targets
    norm_now = lax.optimization_barrier(jnp.sum(residual * residual, axis=1))
    for iteration in range(ITERS):
        applied = ridge_shift * direction + kernel_product(blocks, table, direction) / largest
        step_size = norm_now / lax.optimization_barrier(jnp.sum(direction * applied, axis=1))
        weights = weights + step_size[:, None] * direction
        residual = residual - step_size[:, None] * applied
        norm_next = lax.optimization_barrier(jnp.sum(residual * residual, axis=1))
        direction = residual + (norm_next / norm_now)[:, None] * direction
        norm_now = norm_next
    return (weights, residual)
```

```python
import functools

import jax
import jax.numpy as jnp
from jax import lax
from jax.experimental import pallas as pl
from jax.experimental.pallas import tpu as pltpu
from jax.sharding import PartitionSpec as P

BLOCK = 256
BLOCK_DEV = 2
LANES = 128
ROWS = 8
PIECE_DEPTH = 64
GROUP = 4
STORED_MAX = 192

support_radius = 0.5
ridge_shift = 1.5
f32 = jnp.float32
bf16 = jnp.bfloat16


def pack_kernel(n_row, n_col, targets_ref, positions_ref, pairs_ref, counts_ref, out_ref, extra_ref):
    entries = pairs_ref.shape[1]
    group_rows = targets_ref.shape[0] // (n_row // 2 * n_col)
    lane = lax.broadcasted_iota(jnp.int32, (1, LANES), 1)
    for half in range(BLOCK_DEV):
        extra_ref[half] = jnp.zeros((ROWS, LANES), f32)
        for part in range(2):
            start = half * BLOCK + part * LANES
            extra_ref[half, 4 * part : 4 * part + 3, :] = positions_ref[:, start : start + LANES]
        extra_ref[half, 3:4, :] = jnp.where(lane == LANES - 1, counts_ref[0], 0).astype(f32)
        extra_ref[half, 3:4, 0:entries] = pairs_ref[0:1, :].astype(f32)
        extra_ref[half, 7:8, 0:entries] = pairs_ref[1:2, :].astype(f32)
    for row in range(n_row):
        for col in range(n_col):
            device = row * n_col + col
            group = row // 2 * n_col + col
            half = row % 2
            if group_rows < ROWS:
                out_ref[device, :, 0:BLOCK] = jnp.zeros((ROWS, BLOCK), f32)
            out_ref[device, 0:group_rows, 0:BLOCK] = targets_ref[
                group * group_rows : (group + 1) * group_rows, half * BLOCK : (half + 1) * BLOCK
            ]
            out_ref[device, :, BLOCK : BLOCK + LANES] = extra_ref[half]


def split(value, pieces):
    found = []
    for _ in range(pieces):
        piece = value.astype(bf16).astype(f32)
        found.append(piece)
        value = value - piece
    return found


def point_factors(extra):
    row = lax.broadcasted_iota(jnp.int32, (ROWS, BLOCK), 0)
    coords = jnp.concatenate([extra, pltpu.roll(extra, 4, 0)], axis=1)
    coords = jnp.where(row < 3, (coords - 0.5) * (1.0 / support_radius), 0.0)
    first, second, third = split(coords, 3)
    norm = jnp.sum(coords * coords, axis=0, keepdims=True)
    norm_pieces = split(jnp.broadcast_to(norm, (ROWS, BLOCK)), 3)
    zero = jnp.zeros((ROWS, BLOCK), f32)
    norms = jnp.where(
        row == 0, norm_pieces[0], jnp.where(row == 1, norm_pieces[1], jnp.where(row == 2, norm_pieces[2], zero))
    )
    ones = jnp.where(row < 3, 1.0, 0.0).astype(f32)
    left = jnp.concatenate([first, first, second, second, first, third, norms, ones], axis=0)
    right = jnp.concatenate(
        [-2.0 * piece for piece in (first, second, first, second, third, first)] + [ones, norms], axis=0
    )
    return left, right


def form_tile(left, right):
    square = jnp.maximum(jnp.dot(left, right, preferred_element_type=f32), 1e-30)
    remain = jnp.maximum(1.0 - square * lax.rsqrt(square), 0.0)
    remain_two = remain * remain
    tile = remain_two * remain_two * (1.25 - remain)
    head = tile.astype(bf16)
    return head, (tile - head.astype(f32)).astype(bf16)


def tile_products(row_vector, col_vector, head, tail):
    over_rows = (((1,), (0,)), ((), ()))
    over_cols = (((1,), (1,)), ((), ()))
    to_cols = lax.dot_general(row_vector, head, over_rows, preferred_element_type=f32) + lax.dot_general(
        row_vector, tail, over_rows, preferred_element_type=f32
    )
    to_rows = lax.dot_general(col_vector, head, over_cols, preferred_element_type=f32) + lax.dot_general(
        col_vector, tail, over_cols, preferred_element_type=f32
    )
    return to_cols, to_rows


def store_pieces(vector_ref, block, value, with_ones):
    head, tail = split(value, 2)
    parts = [head, tail]
    if with_ones:
        row = lax.broadcasted_iota(jnp.int32, (2 * ROWS, BLOCK), 0)
        parts.append(jnp.where(row == 0, 1.0, 0.0).astype(f32))
    vector_ref[block] = jnp.concatenate(parts, axis=0).astype(bf16)


def form_kernel(n_row, n_col, stored, mine_ref, other_ref, list_ref, base_ref, partial_ref, *rest):
    if stored:
        tiles_ref, meta_ref, meta_sem, vector_ref, total_ref, left_ref, right_ref = rest
    else:
        left_ref, right_ref, meta_ref, meta_sem, vector_ref, total_ref = rest
    n_dev = n_row * n_col
    blocks = n_dev * BLOCK_DEV
    core = lax.rem(lax.axis_index("row"), 2)
    meta_copy = pltpu.make_async_copy(mine_ref.at[:, :, BLOCK : BLOCK + LANES], meta_ref, meta_sem)
    meta_copy.start()

    def assemble(device, carry):
        for source, half in ((mine_ref, core), (other_ref, 1 - core)):
            block = BLOCK_DEV * device + half
            values = source[device, :, 0:BLOCK]
            base_ref[block] = values
            store_pieces(vector_ref, block, values, True)
            left, right = point_factors(source[device, :, BLOCK : BLOCK + LANES])
            left_ref[block] = left.T.astype(bf16)
            right_ref[block] = right.astype(bf16)
        return carry

    lax.fori_loop(0, n_dev, assemble, 0, unroll=2)
    total_ref[...] = jnp.zeros_like(total_ref)
    meta_copy.wait()

    def put(slot, row_block, col_block, row_to, col_to):
        list_ref[1 + 4 * slot] = row_block
        list_ref[2 + 4 * slot] = col_block
        list_ref[3 + 4 * slot] = row_to
        list_ref[4 + 4 * slot] = col_to

    def read_device(device, carry):
        seen, held = carry
        row = device // n_col
        col = lax.rem(device, n_col)
        count = meta_ref[device, 3, LANES - 1].astype(jnp.int32)
        first = lax.rem(seen + core, 2)
        taken = (count - first + 1) // 2

        def read_entry(index, carry):
            slot = first + 2 * index
            row_id = meta_ref[device, 3, slot].astype(jnp.int32)
            col_id = meta_ref[device, 7, slot].astype(jnp.int32)
            row_block = row * (n_col * BLOCK_DEV) + row_id
            col_block = ((col_id // BLOCK_DEV) * n_col + col) * BLOCK_DEV + lax.rem(col_id, BLOCK_DEV)
            row_to = jnp.where(row_block == col_block, blocks, row_block)
            put(held + index, row_block, col_block, row_to, col_block)
            return carry

        lax.fori_loop(0, taken, read_entry, 0)
        return seen + count, held + taken

    _, held = lax.fori_loop(0, n_dev, read_device, (0, 0))
    groups = (held + GROUP - 1) // GROUP

    def pad(slot, carry):
        put(slot, 0, 0, blocks, blocks)
        return carry

    lax.fori_loop(held, groups * GROUP, pad, 0)
    list_ref[0] = groups

    def run_group(group, carry):
        for place in range(GROUP):
            slot = group * GROUP + place
            row_block = list_ref[1 + 4 * slot]
            col_block = list_ref[2 + 4 * slot]
            head, tail = form_tile(left_ref[row_block], right_ref[col_block])
            if stored:
                tiles_ref[slot, 0] = head
                tiles_ref[slot, 1] = tail
            to_cols, to_rows = tile_products(vector_ref[row_block], vector_ref[col_block], head, tail)
            row_to = list_ref[3 + 4 * slot]
            col_to = list_ref[4 + 4 * slot]
            total_ref[col_to] += to_cols
            total_ref[row_to] += to_rows
        return carry

    lax.fori_loop(0, groups, run_group, 0)
    for block in range(blocks):
        partial_ref[block] = total_ref[block, 0:ROWS] + total_ref[block, ROWS : 2 * ROWS]
        partial_ref[blocks + block // ROWS, block % ROWS : block % ROWS + 1, :] = total_ref[
            block, 2 * ROWS : 2 * ROWS + 1
        ]


def apply_tiles(stored, value_ref, list_ref, held_refs, partial_ref, vector_ref, total_ref):
    blocks = value_ref.shape[0]

    def put_block(block, carry):
        store_pieces(vector_ref, block, value_ref[block], False)
        return carry

    lax.fori_loop(0, blocks, put_block, 0, unroll=4)
    total_ref[...] = jnp.zeros_like(total_ref)

    def run_group(group, carry):
        for place in range(GROUP):
            slot = group * GROUP + place
            row_block = list_ref[1 + 4 * slot]
            col_block = list_ref[2 + 4 * slot]
            if stored:
                head, tail = held_refs[0][slot, 0], held_refs[0][slot, 1]
            else:
                head, tail = form_tile(held_refs[0][row_block], held_refs[1][col_block])
            to_cols, to_rows = tile_products(vector_ref[row_block], vector_ref[col_block], head, tail)
            row_to = list_ref[3 + 4 * slot]
            col_to = list_ref[4 + 4 * slot]
            total_ref[col_to] += to_cols
            total_ref[row_to] += to_rows
        return carry

    lax.fori_loop(0, list_ref[0], run_group, 0)
    partial_ref[...] = total_ref[0:blocks, 0:ROWS] + total_ref[0:blocks, ROWS : 2 * ROWS]


def row_sum(value):
    return jnp.sum(jnp.sum(value, axis=0, keepdims=True), axis=2, keepdims=True)


def first_step_kernel(stored, list_ref, mine_ref, other_ref, base_ref, *rest):
    held, rest = rest[:-6], rest[-6:]
    residual_ref, direction_ref, partial_ref, scalars_ref, vector_ref, total_ref = rest
    blocks = base_ref.shape[0]
    largest = jnp.max(mine_ref[blocks:] + other_ref[blocks:])
    base = base_ref[...]
    applied = ridge_shift * base + (mine_ref[0:blocks] + other_ref[0:blocks]) / largest
    norm_now = row_sum(base * base)
    step_size = norm_now / row_sum(base * applied)
    residual = base - step_size * applied
    norm_next = row_sum(residual * residual)
    direction = residual + (norm_next / norm_now) * base
    residual_ref[...] = residual
    direction_ref[...] = direction
    scalars_ref[0] = jnp.broadcast_to(step_size[0], (ROWS, LANES))
    scalars_ref[1] = jnp.broadcast_to(norm_next[0], (ROWS, LANES))
    scalars_ref[2] = jnp.full((ROWS, LANES), largest, f32)
    apply_tiles(stored, direction_ref, list_ref, held, partial_ref, vector_ref, total_ref)


def next_step_kernel(
    stored, list_ref, mine_ref, other_ref, base_ref, residual_ref, direction_ref, scalars_ref, *rest
):
    held, rest = rest[:-7], rest[-7:]
    weights_out, residual_out, direction_out, partial_ref, scalars_out, vector_ref, total_ref = rest
    step_before = scalars_ref[0:1, :, 0:1]
    norm_now = scalars_ref[1:2, :, 0:1]
    largest = scalars_ref[2:3, :, 0:1]
    direction = direction_ref[...]
    applied = ridge_shift * direction + (mine_ref[...] + other_ref[...]) / largest
    step_size = norm_now / row_sum(direction * applied)
    weights_out[...] = step_before * base_ref[...] + step_size * direction
    residual = residual_ref[...] - step_size * applied
    norm_next = row_sum(residual * residual)
    residual_out[...] = residual
    direction_out[...] = residual + (norm_next / norm_now) * direction
    scalars_out[0] = scalars_ref[0]
    scalars_out[1] = jnp.broadcast_to(norm_next[0], (ROWS, LANES))
    scalars_out[2] = scalars_ref[2]
    apply_tiles(stored, direction_out, list_ref, held, partial_ref, vector_ref, total_ref)


def last_step_kernel(mine_ref, other_ref, weights_ref, residual_ref, direction_ref, scalars_ref, out_ref):
    norm_now = scalars_ref[1:2, :, 0:1]
    largest = scalars_ref[2:3, :, 0:1]
    direction = direction_ref[...]
    applied = ridge_shift * direction + (mine_ref[...] + other_ref[...]) / largest
    step_size = norm_now / row_sum(direction * applied)
    core = lax.rem(lax.axis_index("row"), 2)

    @pl.when(core == 0)
    def _():
        out_ref[...] = weights_ref[...] + step_size * direction

    @pl.when(core == 1)
    def _():
        out_ref[...] = residual_ref[...] - step_size * applied


def unpack_kernel(n_row, n_col, group_rows, received_ref, weights_ref, residual_ref):
    for row in range(n_row):
        target = residual_ref if row % 2 else weights_ref
        for col in range(n_col):
            start = (row // 2 * n_col + col) * group_rows
            for half in range(BLOCK_DEV):
                target[start : start + group_rows, half * BLOCK : (half + 1) * BLOCK] = received_ref[
                    (row * n_col + col) * BLOCK_DEV + half, 0:group_rows
                ]


def call(kernel, out_shape, *args, scratch=(), in_spaces=None, out_spaces=None, vmem=16):
    spaces = in_spaces or [pltpu.VMEM] * len(args)
    outs = out_spaces or jax.tree.map(lambda _: pltpu.VMEM, out_shape)
    return pl.pallas_call(
        kernel,
        out_shape=out_shape,
        in_specs=[pl.BlockSpec(memory_space=space) for space in spaces],
        out_specs=jax.tree.map(lambda space: pl.BlockSpec(memory_space=space), outs),
        scratch_shapes=list(scratch),
        compiler_params=pltpu.CompilerParams(vmem_limit_bytes=vmem * 2**20),
    )(*args)


def local(positions, targets, pairs, counts):
    n_row = lax.axis_size("row")
    n_col = lax.axis_size("col")
    n_dev = n_row * n_col
    blocks = n_dev * BLOCK_DEV
    entries = pairs.shape[1]
    target_rows = targets.shape[0]
    group_rows = target_rows // (n_dev // 2)
    room = -(-(n_dev * entries // 2) // GROUP) * GROUP
    stored = room <= STORED_MAX
    both = ("row", "col")
    siblings = [(index, index ^ 1) for index in range(n_row)]
    shape = jax.ShapeDtypeStruct
    kept = pltpu.VMEM if stored else shape
    vmem = 12 if stored else 58
    field = shape((blocks, ROWS, BLOCK), f32)
    scalars = shape((3, ROWS, LANES), f32)

    def resident(array):
        return pltpu.with_memory_space_constraint(array, pltpu.VMEM) if stored else array

    def from_sibling(array):
        return lax.ppermute(array, "row", siblings)

    packed = call(
        functools.partial(pack_kernel, n_row, n_col),
        kept((n_dev, ROWS, BLOCK + LANES), f32),
        targets,
        positions,
        pairs,
        counts,
        in_spaces=[pltpu.VMEM] * 3 + [pltpu.SMEM],
        scratch=[pltpu.VMEM((BLOCK_DEV, ROWS, LANES), f32)],
    )
    mine = resident(lax.all_to_all(packed, both, 0, 0, tiled=True))
    other = from_sibling(mine)

    factor_shapes = [
        ((blocks, BLOCK, PIECE_DEPTH), bf16),
        ((blocks, PIECE_DEPTH, BLOCK), bf16),
    ]
    if stored:
        held = [kept((room, 2, BLOCK, BLOCK), bf16)]
    else:
        held = [shape(*factor) for factor in factor_shapes]
    listed, base, partial, *held = call(
        functools.partial(form_kernel, n_row, n_col, stored),
        [
            shape((1 + 4 * room,), jnp.int32),
            field,
            shape((blocks + -(-blocks // ROWS), ROWS, BLOCK), f32),
            *held,
        ],
        mine,
        other,
        out_spaces=[pltpu.SMEM] + [pltpu.VMEM] * (2 + len(held)),
        scratch=[
            pltpu.SMEM((n_dev, ROWS, LANES), f32),
            pltpu.SemaphoreType.DMA,
            pltpu.VMEM((blocks, 4 * ROWS, BLOCK), bf16),
            pltpu.VMEM((blocks + 1, 4 * ROWS, BLOCK), f32),
        ]
        + [pltpu.VMEM(*factor) for factor in factor_shapes if stored],
        vmem=vmem,
    )
    held = [resident(array) for array in held]
    apply_scratch = [
        pltpu.VMEM((blocks, 2 * ROWS, BLOCK), bf16),
        pltpu.VMEM((blocks + 1, 2 * ROWS, BLOCK), f32),
    ]

    def step(kernel, out_shape, *args):
        outs = call(
            functools.partial(kernel, stored),
            out_shape,
            listed,
            *args,
            *held,
            in_spaces=[pltpu.SMEM] + [pltpu.VMEM] * (len(args) + len(held)),
            scratch=apply_scratch,
            vmem=vmem,
        )
        return outs

    residual, direction, partial, numbers = step(
        first_step_kernel, (field, field, field, scalars), partial, from_sibling(partial), base
    )
    weights, residual, direction, partial, numbers = step(
        next_step_kernel,
        (field, field, field, field, scalars),
        partial,
        from_sibling(partial),
        base,
        residual,
        direction,
        numbers,
    )
    result = call(
        last_step_kernel, field, partial, from_sibling(partial), weights, residual, direction, numbers
    )
    home = resident(lax.all_to_all(resident(result), both, 0, 0, tiled=True))
    out = shape(targets.shape, f32)
    return call(functools.partial(unpack_kernel, n_row, n_col, group_rows), (out, out), home)


def solution(mesh):
    placed = (
        P(None, ("groups", "row", "col")),
        P(None, ("groups", "row", "col")),
        P(None, ("groups", "row", "col")),
        P(("groups", "row", "col")),
    )
    return jax.shard_map(
        local,
        mesh=mesh,
        in_specs=placed,
        out_specs=(P(None, ("groups", "row", "col")), P(None, ("groups", "row", "col"))),
        check_vma=False,
    )
```

```python
import functools

import jax
import jax.numpy as jnp
from jax import lax
from jax.experimental import pallas as pl
from jax.experimental.pallas import tpu as pltpu
from jax.sharding import PartitionSpec as P

BLOCK = 256
BLOCK_DEV = 2
LANES = 128
ROWS = 8
PIECE_DEPTH = 64
GROUP = 16
QUARTER = 4
STORED_MAX = 192
LISTED = 256
READ_SLOTS = 3
WRITE_SLOTS = 2

support_radius = 0.5
ridge_shift = 1.5
f32 = jnp.float32
bf16 = jnp.bfloat16


def pack_kernel(
    n_row, n_col, targets_in, positions_in, pairs_in, counts_in, out_ref, targets_ref, positions_ref, pairs_ref, counts_ref, extra_ref, sems
):
    copies = [
        pltpu.make_async_copy(source, kept, sems.at[index])
        for index, (source, kept) in enumerate(
            (
                (positions_in, positions_ref),
                (pairs_in, pairs_ref),
                (counts_in, counts_ref),
                (targets_in, targets_ref),
            )
        )
    ]
    for copy in copies:
        copy.start()
    for copy in copies[:3]:
        copy.wait()
    entries = pairs_ref.shape[1]
    group_rows = targets_ref.shape[0] // (n_row // 2 * n_col)
    lane = lax.broadcasted_iota(jnp.int32, (1, LANES), 1)
    for half in range(BLOCK_DEV):
        extra_ref[half] = jnp.zeros((ROWS, LANES), f32)
        for part in range(2):
            start = half * BLOCK + part * LANES
            extra_ref[half, 4 * part : 4 * part + 3, :] = positions_ref[:, start : start + LANES]
        extra_ref[half, 3:4, :] = jnp.where(lane == LANES - 1, counts_ref[0], 0).astype(f32)
        extra_ref[half, 3:4, 0:entries] = pairs_ref[0:1, :].astype(f32)
        extra_ref[half, 7:8, 0:entries] = pairs_ref[1:2, :].astype(f32)
    copies[3].wait()
    for row in range(n_row):
        for col in range(n_col):
            device = row * n_col + col
            group = row // 2 * n_col + col
            half = row % 2
            if group_rows < ROWS:
                out_ref[device, :, 0:BLOCK] = jnp.zeros((ROWS, BLOCK), f32)
            out_ref[device, 0:group_rows, 0:BLOCK] = targets_ref[
                group * group_rows : (group + 1) * group_rows, half * BLOCK : (half + 1) * BLOCK
            ]
            out_ref[device, :, BLOCK : BLOCK + LANES] = extra_ref[half]


def split(value, pieces):
    found = []
    for _ in range(pieces):
        piece = value.astype(bf16).astype(f32)
        found.append(piece)
        value = value - piece
    return found


def point_factors(extra):
    row = lax.broadcasted_iota(jnp.int32, (ROWS, BLOCK), 0)
    coords = jnp.concatenate([extra, pltpu.roll(extra, 4, 0)], axis=1)
    coords = jnp.where(row < 3, (coords - 0.5) * (1.0 / support_radius), 0.0)
    first, second, third = split(coords, 3)
    norm = jnp.sum(coords * coords, axis=0, keepdims=True)
    norm_pieces = split(jnp.broadcast_to(norm, (ROWS, BLOCK)), 3)
    zero = jnp.zeros((ROWS, BLOCK), f32)
    norms = jnp.where(
        row == 0, norm_pieces[0], jnp.where(row == 1, norm_pieces[1], jnp.where(row == 2, norm_pieces[2], zero))
    )
    ones = jnp.where(row < 3, 1.0, 0.0).astype(f32)
    left = jnp.concatenate([first, first, second, second, first, third, norms, ones], axis=0)
    right = jnp.concatenate(
        [-2.0 * piece for piece in (first, second, first, second, third, first)] + [ones, norms], axis=0
    )
    return left, right


def form_tile(left, right, times):
    square = jnp.maximum(jnp.dot(left, right, preferred_element_type=f32), 1e-30)
    remain = jnp.maximum(1.0 - square * lax.rsqrt(square), 0.0)
    remain_two = remain * remain
    tile = remain_two * remain_two * (1.25 * times - times * remain)
    head = tile.astype(bf16)
    return head, (tile - head.astype(f32)).astype(bf16)


def add_products(vector_ref, total_ref, row_block, col_block, row_to, head, tail):
    over_rows = (((1,), (0,)), ((), ()))
    over_cols = (((1,), (1,)), ((), ()))
    row_vector, col_vector = vector_ref[row_block], vector_ref[col_block]
    to_cols = lax.dot_general(row_vector, head, over_rows, preferred_element_type=f32) + lax.dot_general(
        row_vector, tail, over_rows, preferred_element_type=f32
    )
    to_rows = lax.dot_general(col_vector, head, over_cols, preferred_element_type=f32) + lax.dot_general(
        col_vector, tail, over_cols, preferred_element_type=f32
    )
    total_ref[col_block] += to_cols
    total_ref[row_to] += to_rows


def store_pieces(vector_ref, block, value, with_ones):
    parts = split(value, 2)
    if with_ones:
        row = lax.broadcasted_iota(jnp.int32, (2 * ROWS, BLOCK), 0)
        parts.append(jnp.where(row == 0, 1.0, 0.0).astype(f32))
    vector_ref[block] = jnp.concatenate(parts, axis=0).astype(bf16)


def global_blocks(n_col, meta_ref, device):
    row_ids = meta_ref[device, 3:4, BLOCK : BLOCK + LANES].astype(jnp.int32)
    col_ids = meta_ref[device, 7:8, BLOCK : BLOCK + LANES].astype(jnp.int32)
    count = row_ids[:, LANES - 1 :]
    in_use = lax.broadcasted_iota(jnp.int32, (1, LANES), 1) < count
    row_block = (device // n_col) * (n_col * BLOCK_DEV) + row_ids
    col_block = ((col_ids >> 1) * n_col + lax.rem(device, n_col)) * BLOCK_DEV + (col_ids & 1)
    return jnp.minimum(row_block, col_block), jnp.maximum(row_block, col_block), in_use


def merged_list(n_dev, n_col, core, meta_ref, keys_ref, times_ref):
    blocks = n_dev * BLOCK_DEV
    block_id = lax.broadcasted_iota(jnp.int32, (blocks, LANES), 0)
    smaller, larger = [], []
    for device in range(n_dev):
        low, high, in_use = global_blocks(n_col, meta_ref, device)
        smaller.append(jnp.where((block_id == low) & in_use, 1.0, 0.0))
        larger.append(jnp.where((block_id == high) & in_use, 1.0, 0.0))
    over_lanes = (((1,), (1,)), ((), ()))
    times = lax.dot_general(
        jnp.concatenate(larger, axis=1).astype(bf16),
        jnp.concatenate(smaller, axis=1).astype(bf16),
        over_lanes,
        preferred_element_type=f32,
    )
    present = jnp.where(times > 0.0, 1.0, 0.0)
    high_id = lax.broadcasted_iota(jnp.int32, (blocks, blocks), 0)
    low_id = lax.broadcasted_iota(jnp.int32, (blocks, blocks), 1)
    before = jnp.where(high_id > low_id, 1.0, 0.0).astype(bf16)
    present_low = present.astype(bf16)
    in_column = jnp.dot(before, present_low, preferred_element_type=f32)
    column_sums = jnp.sum(present, axis=0, keepdims=True)
    column_starts = lax.dot_general(
        jnp.broadcast_to(column_sums, (ROWS, blocks)).astype(bf16), before, over_lanes, preferred_element_type=f32
    )[0:1]
    place = (in_column + column_starts).astype(jnp.int32)
    mine = (present > 0.0) & ((place & 1) == core)
    slot = jnp.where(mine, place >> 1, -1)
    key = low_id * blocks + high_id
    lane = lax.broadcasted_iota(jnp.int32, (blocks, LISTED), 1)
    keys = jnp.zeros((blocks, LISTED), jnp.int32)
    counted = jnp.zeros((blocks, LISTED), f32)
    for low in range(blocks):
        here = lane == slot[:, low : low + 1]
        keys = keys + jnp.where(here, key[:, low : low + 1], 0)
        counted = counted + jnp.where(here, times[:, low : low + 1], 0.0)
    held = jnp.sum(jnp.where(mine, 1.0, 0.0), axis=1, keepdims=True)
    held = jnp.sum(held, axis=0, keepdims=True).astype(jnp.int32)
    first_lane = lax.broadcasted_iota(jnp.int32, (1, LISTED), 1)
    keys_ref[...] = jnp.where(
        first_lane == LISTED - 1, held, jnp.sum(keys.astype(f32), axis=0, keepdims=True).astype(jnp.int32)
    )
    times_ref[...] = jnp.sum(counted, axis=0, keepdims=True)


def read_key(list_ref, slot, blocks):
    key = list_ref[0, slot]
    row_block, col_block = lax.div(key, blocks), lax.rem(key, blocks)
    return row_block, col_block, jnp.where(row_block == col_block, blocks, row_block)


def turn_copies(held, turn, slots, sems, hbm_ref, buffer_ref, to_hbm):
    slot = lax.rem(turn, slots)
    for quarter in range(GROUP // QUARTER):
        start = turn * GROUP + quarter * QUARTER
        far = hbm_ref.at[pl.ds(start, QUARTER)]
        near = buffer_ref.at[slot, pl.ds(quarter * QUARTER, QUARTER)]
        source, target = (near, far) if to_hbm else (far, near)
        yield start < held, pltpu.make_async_copy(source, target, sems.at[slot, quarter])


def start_turn(*args):
    for used, copy in turn_copies(*args):
        pl.when(used)(copy.start)


def wait_turn(*args):
    for used, copy in turn_copies(*args):
        pl.when(used)(copy.wait)


def assemble_block(source, device, block, base_ref, vector_ref, left_ref, right_ref):
    values = source[device, :, 0:BLOCK]
    base_ref[block] = values
    store_pieces(vector_ref, block, values, True)
    left, right = point_factors(source[device, :, BLOCK : BLOCK + LANES])
    left_ref[block] = left.T.astype(bf16)
    right_ref[block] = right.astype(bf16)


def finish_first(total_ref, partial_ref, blocks):
    for block in range(blocks):
        partial_ref[block] = total_ref[block, 0:ROWS] + total_ref[block, ROWS : 2 * ROWS]
        partial_ref[blocks + block // ROWS, block % ROWS : block % ROWS + 1, :] = total_ref[
            block, 2 * ROWS : 2 * ROWS + 1
        ]


def form_stored_kernel(
    n_row,
    n_col,
    mine_ref,
    other_ref,
    list_ref,
    base_ref,
    partial_ref,
    tiles_ref,
    times_ref,
    keys_vector,
    times_vector,
    list_sems,
    vector_ref,
    total_ref,
    left_ref,
    right_ref,
    buffer_ref,
    sems,
):
    n_dev = n_row * n_col
    blocks = n_dev * BLOCK_DEV
    core = lax.rem(lax.axis_index("row"), 2)
    merged_list(n_dev, n_col, core, mine_ref, keys_vector, times_vector)
    keys_copy = pltpu.make_async_copy(keys_vector, list_ref, list_sems.at[0])
    times_copy = pltpu.make_async_copy(times_vector, times_ref, list_sems.at[1])
    keys_copy.start()
    times_copy.start()

    def assemble(device, carry):
        for source, half in ((mine_ref, core), (other_ref, 1 - core)):
            assemble_block(source, device, BLOCK_DEV * device + half, base_ref, vector_ref, left_ref, right_ref)
        return carry

    lax.fori_loop(0, n_dev, assemble, 0, unroll=2)
    total_ref[...] = jnp.zeros_like(total_ref)
    keys_copy.wait()
    times_copy.wait()
    held = list_ref[0, LISTED - 1]

    def copies(turn):
        return held, turn, WRITE_SLOTS, sems, tiles_ref, buffer_ref, True

    def run_turn(turn, first, size):
        slot = lax.rem(turn, WRITE_SLOTS)
        if size == GROUP:
            pl.when(turn >= WRITE_SLOTS)(lambda: wait_turn(*copies(turn - WRITE_SLOTS)))
        for place in range(size):
            entry = turn * GROUP + first + place
            row_block, col_block, row_to = read_key(list_ref, entry, blocks)
            head, tail = form_tile(left_ref[row_block], right_ref[col_block], times_ref[0, entry])
            buffer_ref[slot, first + place, 0] = head
            buffer_ref[slot, first + place, 1] = tail
            add_products(vector_ref, total_ref, row_block, col_block, row_to, head, tail)
        if size == GROUP:
            start_turn(*copies(turn))

    full = held // GROUP
    turns = (held + GROUP - 1) // GROUP

    def run_full(turn, carry):
        run_turn(turn, 0, GROUP)
        return carry

    lax.fori_loop(0, full, run_full, 0)

    @pl.when(turns > full)
    def _():
        pl.when(full >= WRITE_SLOTS)(lambda: wait_turn(*copies(full - WRITE_SLOTS)))

        def run_rest(quarter, carry):
            run_turn(full, quarter * QUARTER, QUARTER)
            return carry

        lax.fori_loop(0, (held - full * GROUP + QUARTER - 1) // QUARTER, run_rest, 0)
        start_turn(*copies(full))

    finish_first(total_ref, partial_ref, blocks)
    for back in range(WRITE_SLOTS, 0, -1):
        pl.when(turns >= back)(lambda back=back: wait_turn(*copies(turns - back)))


def form_kernel(
    n_row, n_col, mine_ref, other_ref, list_ref, base_ref, partial_ref, left_ref, right_ref, meta_ref, meta_sem, vector_ref, total_ref
):
    n_dev = n_row * n_col
    blocks = n_dev * BLOCK_DEV
    core = lax.rem(lax.axis_index("row"), 2)
    meta_copy = pltpu.make_async_copy(mine_ref.at[:, :, BLOCK : BLOCK + LANES], meta_ref, meta_sem)
    meta_copy.start()

    def assemble(device, carry):
        for source, half in ((mine_ref, core), (other_ref, 1 - core)):
            assemble_block(source, device, BLOCK_DEV * device + half, base_ref, vector_ref, left_ref, right_ref)
        return carry

    lax.fori_loop(0, n_dev, assemble, 0)
    total_ref[...] = jnp.zeros_like(total_ref)
    meta_copy.wait()

    def read_device(device, carry):
        seen, held = carry
        row = device // n_col
        col = lax.rem(device, n_col)
        count = meta_ref[device, 3, LANES - 1].astype(jnp.int32)
        first = lax.rem(seen + core, 2)
        taken = (count - first + 1) // 2

        def read_entry(index, carry):
            slot = first + 2 * index
            row_id = meta_ref[device, 3, slot].astype(jnp.int32)
            col_id = meta_ref[device, 7, slot].astype(jnp.int32)
            row_block = row * (n_col * BLOCK_DEV) + row_id
            col_block = ((col_id // BLOCK_DEV) * n_col + col) * BLOCK_DEV + lax.rem(col_id, BLOCK_DEV)
            list_ref[0, held + index] = row_block * blocks + col_block
            return carry

        lax.fori_loop(0, taken, read_entry, 0)
        return seen + count, held + taken

    _, held = lax.fori_loop(0, n_dev, read_device, (0, 0))
    list_ref[0, list_ref.shape[1] - 1] = held
    apply_formed(list_ref, (left_ref, right_ref), vector_ref, total_ref, blocks)
    finish_first(total_ref, partial_ref, blocks)


def apply_formed(list_ref, factor_refs, vector_ref, total_ref, blocks):
    def run_entry(entry, carry):
        row_block, col_block, row_to = read_key(list_ref, entry, blocks)
        head, tail = form_tile(factor_refs[0][row_block], factor_refs[1][col_block], 1.0)
        add_products(vector_ref, total_ref, row_block, col_block, row_to, head, tail)
        return carry

    lax.fori_loop(0, list_ref[0, list_ref.shape[1] - 1], run_entry, 0)


def apply_stored(list_ref, tiles_ref, buffer_ref, sems, vector_ref, total_ref, blocks):
    held = list_ref[0, LISTED - 1]
    full = held // GROUP

    def copies(turn):
        return held, turn, READ_SLOTS, sems, tiles_ref, buffer_ref, False

    def run_turn(turn, first, size):
        slot = lax.rem(turn, READ_SLOTS)
        for place in range(size):
            row_block, col_block, row_to = read_key(list_ref, turn * GROUP + first + place, blocks)
            head, tail = buffer_ref[slot, first + place, 0], buffer_ref[slot, first + place, 1]
            add_products(vector_ref, total_ref, row_block, col_block, row_to, head, tail)

    def run_full(turn, carry):
        wait_turn(*copies(turn))
        run_turn(turn, 0, GROUP)
        start_turn(*copies(turn + READ_SLOTS))
        return carry

    def run_rest(quarter, carry):
        run_turn(full, quarter * QUARTER, QUARTER)
        return carry

    lax.fori_loop(0, full, run_full, 0)
    wait_turn(*copies(full))
    lax.fori_loop(0, (held - full * GROUP + QUARTER - 1) // QUARTER, run_rest, 0)


def start_reads(stored, list_ref, held_refs, scratch):
    if stored:
        for turn in range(READ_SLOTS):
            start_turn(list_ref[0, LISTED - 1], turn, READ_SLOTS, scratch[3], held_refs[0], scratch[2], False)


def apply_tiles(stored, value_ref, list_ref, held_refs, partial_ref, scratch):
    blocks = value_ref.shape[0]
    vector_ref, total_ref = scratch[:2]

    def put_block(block, carry):
        store_pieces(vector_ref, block, value_ref[block], False)
        return carry

    lax.fori_loop(0, blocks, put_block, 0, unroll=8)
    total_ref[...] = jnp.zeros_like(total_ref)
    if stored:
        apply_stored(list_ref, held_refs[0], scratch[2], scratch[3], vector_ref, total_ref, blocks)
    else:
        apply_formed(list_ref, held_refs, vector_ref, total_ref, blocks)
    partial_ref[...] = total_ref[0:blocks, 0:ROWS] + total_ref[0:blocks, ROWS : 2 * ROWS]


def row_sum(value):
    return jnp.sum(jnp.sum(value, axis=0, keepdims=True), axis=2, keepdims=True)


def first_step_kernel(stored, list_ref, mine_ref, other_ref, base_ref, *rest):
    count = 1 if stored else 2
    held, rest = rest[:count], rest[count:]
    residual_ref, direction_ref, partial_ref, scalars_ref, *scratch = rest
    start_reads(stored, list_ref, held, scratch)
    blocks = base_ref.shape[0]
    largest = jnp.max(mine_ref[blocks:] + other_ref[blocks:])
    base = base_ref[...]
    applied = ridge_shift * base + (mine_ref[0:blocks] + other_ref[0:blocks]) / largest
    norm_now = row_sum(base * base)
    step_size = norm_now / row_sum(base * applied)
    residual = base - step_size * applied
    norm_next = row_sum(residual * residual)
    direction = residual + (norm_next / norm_now) * base
    residual_ref[...] = residual
    direction_ref[...] = direction
    scalars_ref[0] = jnp.broadcast_to(step_size[0], (ROWS, LANES))
    scalars_ref[1] = jnp.broadcast_to(norm_next[0], (ROWS, LANES))
    scalars_ref[2] = jnp.full((ROWS, LANES), largest, f32)
    apply_tiles(stored, direction_ref, list_ref, held, partial_ref, scratch)


def next_step_kernel(
    stored, list_ref, mine_ref, other_ref, base_ref, residual_ref, direction_ref, scalars_ref, *rest
):
    count = 1 if stored else 2
    held, rest = rest[:count], rest[count:]
    weights_out, residual_out, direction_out, partial_ref, scalars_out, *scratch = rest
    start_reads(stored, list_ref, held, scratch)
    step_before = scalars_ref[0:1, :, 0:1]
    norm_now = scalars_ref[1:2, :, 0:1]
    largest = scalars_ref[2:3, :, 0:1]
    direction = direction_ref[...]
    applied = ridge_shift * direction + (mine_ref[...] + other_ref[...]) / largest
    step_size = norm_now / row_sum(direction * applied)
    weights_out[...] = step_before * base_ref[...] + step_size * direction
    residual = residual_ref[...] - step_size * applied
    norm_next = row_sum(residual * residual)
    residual_out[...] = residual
    direction_out[...] = residual + (norm_next / norm_now) * direction
    scalars_out[0] = scalars_ref[0]
    scalars_out[1] = jnp.broadcast_to(norm_next[0], (ROWS, LANES))
    scalars_out[2] = scalars_ref[2]
    apply_tiles(stored, direction_out, list_ref, held, partial_ref, scratch)


def last_step_kernel(mine_ref, other_ref, weights_ref, residual_ref, direction_ref, scalars_ref, out_ref):
    norm_now = scalars_ref[1:2, :, 0:1]
    largest = scalars_ref[2:3, :, 0:1]
    direction = direction_ref[...]
    applied = ridge_shift * direction + (mine_ref[...] + other_ref[...]) / largest
    step_size = norm_now / row_sum(direction * applied)
    core = lax.rem(lax.axis_index("row"), 2)

    @pl.when(core == 0)
    def _():
        out_ref[...] = weights_ref[...] + step_size * direction

    @pl.when(core == 1)
    def _():
        out_ref[...] = residual_ref[...] - step_size * applied


def unpack_kernel(n_row, n_col, group_rows, received_ref, weights_ref, residual_ref):
    for row in range(n_row):
        target = residual_ref if row % 2 else weights_ref
        for col in range(n_col):
            start = (row // 2 * n_col + col) * group_rows
            for half in range(BLOCK_DEV):
                target[start : start + group_rows, half * BLOCK : (half + 1) * BLOCK] = received_ref[
                    (row * n_col + col) * BLOCK_DEV + half, 0:group_rows
                ]


def call(kernel, out_shape, *args, scratch=(), in_spaces=None, out_spaces=None, vmem=16):
    spaces = in_spaces or [pltpu.VMEM] * len(args)
    outs = out_spaces or jax.tree.map(lambda _: pltpu.VMEM, out_shape)
    return pl.pallas_call(
        kernel,
        out_shape=out_shape,
        in_specs=[pl.BlockSpec(memory_space=space) for space in spaces],
        out_specs=jax.tree.map(lambda space: pl.BlockSpec(memory_space=space), outs),
        scratch_shapes=list(scratch),
        compiler_params=pltpu.CompilerParams(vmem_limit_bytes=vmem * 2**20),
    )(*args)


def local(positions, targets, pairs, counts):
    n_row = lax.axis_size("row")
    n_col = lax.axis_size("col")
    n_dev = n_row * n_col
    blocks = n_dev * BLOCK_DEV
    entries = pairs.shape[1]
    group_rows = targets.shape[0] // (n_dev // 2)
    room = -(-(n_dev * entries // 2) // GROUP) * GROUP
    stored = room <= STORED_MAX
    both = ("row", "col")
    siblings = [(index, index ^ 1) for index in range(n_row)]
    shape = jax.ShapeDtypeStruct
    kept = pltpu.VMEM if stored else shape
    vmem = 24 if stored else 58
    field = kept((blocks, ROWS, BLOCK), f32)
    scalars = kept((3, ROWS, LANES), f32)

    def resident(array):
        return pltpu.with_memory_space_constraint(array, pltpu.VMEM) if stored else array

    def from_sibling(array):
        return resident(lax.ppermute(array, "row", siblings))

    packed = call(
        functools.partial(pack_kernel, n_row, n_col),
        kept((n_dev, ROWS, BLOCK + LANES), f32),
        targets,
        positions,
        pairs,
        counts,
        in_spaces=[pl.ANY] * 4,
        scratch=[
            pltpu.VMEM(targets.shape, f32),
            pltpu.VMEM(positions.shape, f32),
            pltpu.VMEM(pairs.shape, jnp.int32),
            pltpu.SMEM(counts.shape, jnp.int32),
            pltpu.VMEM((BLOCK_DEV, ROWS, LANES), f32),
            pltpu.SemaphoreType.DMA((4,)),
        ],
        vmem=60,
    )
    mine = resident(lax.all_to_all(resident(packed), both, 0, 0, tiled=True))
    other = from_sibling(mine)

    factors = [((blocks, BLOCK, PIECE_DEPTH), bf16), ((blocks, PIECE_DEPTH, BLOCK), bf16)]
    factor_scratch = [pltpu.VMEM(*factor) for factor in factors]
    first_partial = kept((blocks + -(-blocks // ROWS), ROWS, BLOCK), f32)
    first_scratch = [
        pltpu.VMEM((blocks, 4 * ROWS, BLOCK), bf16),
        pltpu.VMEM((blocks + 1, 4 * ROWS, BLOCK), f32),
    ]
    step_scratch = [
        pltpu.VMEM((blocks, 2 * ROWS, BLOCK), bf16),
        pltpu.VMEM((blocks + 1, 2 * ROWS, BLOCK), f32),
    ]
    if stored:
        listed, base, partial, *held = call(
            functools.partial(form_stored_kernel, n_row, n_col),
            [shape((1, LISTED), jnp.int32), field, first_partial, shape((room, 2, BLOCK, BLOCK), bf16)],
            mine,
            other,
            out_spaces=[pltpu.SMEM, pltpu.VMEM, pltpu.VMEM, pl.ANY],
            scratch=[
                pltpu.SMEM((1, LISTED), f32),
                pltpu.VMEM((1, LISTED), jnp.int32),
                pltpu.VMEM((1, LISTED), f32),
                pltpu.SemaphoreType.DMA((2,)),
                *first_scratch,
                *factor_scratch,
                pltpu.VMEM((WRITE_SLOTS, GROUP, 2, BLOCK, BLOCK), bf16),
                pltpu.SemaphoreType.DMA((WRITE_SLOTS, GROUP // QUARTER)),
            ],
            vmem=vmem,
        )
        held_spaces = [pl.ANY]
        step_scratch += [
            pltpu.VMEM((READ_SLOTS, GROUP, 2, BLOCK, BLOCK), bf16),
            pltpu.SemaphoreType.DMA((READ_SLOTS, GROUP // QUARTER)),
        ]
    else:
        listed, base, partial, *held = call(
            functools.partial(form_kernel, n_row, n_col),
            [shape((1, room + 1), jnp.int32), field, first_partial, *(shape(*factor) for factor in factors)],
            mine,
            other,
            out_spaces=[pltpu.SMEM] + [pltpu.VMEM] * 4,
            scratch=[pltpu.SMEM((n_dev, ROWS, LANES), f32), pltpu.SemaphoreType.DMA, *first_scratch],
            vmem=vmem,
        )
        held_spaces = [pltpu.VMEM] * 2
    base, partial = resident(base), resident(partial)

    def step(kernel, out_shape, *args):
        outs = call(
            functools.partial(kernel, stored),
            out_shape,
            listed,
            *args,
            *held,
            in_spaces=[pltpu.SMEM] + [pltpu.VMEM] * len(args) + held_spaces,
            scratch=step_scratch,
            vmem=vmem,
        )
        return [resident(out) for out in outs]

    residual, direction, partial, numbers = step(
        first_step_kernel, (field, field, field, scalars), partial, from_sibling(partial), base
    )
    weights, residual, direction, partial, numbers = step(
        next_step_kernel,
        (field, field, field, field, scalars),
        partial,
        from_sibling(partial),
        base,
        residual,
        direction,
        numbers,
    )
    result = call(
        last_step_kernel, field, partial, from_sibling(partial), weights, residual, direction, numbers
    )
    home = resident(lax.all_to_all(resident(result), both, 0, 0, tiled=True))
    out = shape(targets.shape, f32)
    return call(functools.partial(unpack_kernel, n_row, n_col, group_rows), (out, out), home)


def solution(mesh):
    placed = (
        P(None, ("groups", "row", "col")),
        P(None, ("groups", "row", "col")),
        P(None, ("groups", "row", "col")),
        P(("groups", "row", "col")),
    )
    return jax.shard_map(
        local,
        mesh=mesh,
        in_specs=placed,
        out_specs=(P(None, ("groups", "row", "col")), P(None, ("groups", "row", "col"))),
        check_vma=False,
    )
```

```python
import functools

import jax
import jax.numpy as jnp
from jax import lax
from jax.experimental import pallas as pl
from jax.experimental.pallas import tpu as pltpu
from jax.sharding import PartitionSpec as P

BLOCK = 256
BLOCK_DEV = 2
LANES = 128
ROWS = 8
PIECE_DEPTH = 64
TURN = 8
STORED_MAX = 192
LISTED = 256
WRITE_SLOTS = 2

support_radius = 0.5
ridge_shift = 1.5
f32 = jnp.float32
bf16 = jnp.bfloat16


def pack_kernel(
    n_row, n_col, targets_in, positions_in, pairs_in, counts_in, out_ref, targets_ref, positions_ref, pairs_ref, counts_ref, extra_ref, sems
):
    copies = [
        pltpu.make_async_copy(source, kept, sems.at[index])
        for index, (source, kept) in enumerate(
            (
                (positions_in, positions_ref),
                (pairs_in, pairs_ref),
                (counts_in, counts_ref),
                (targets_in, targets_ref),
            )
        )
    ]
    for copy in copies:
        copy.start()
    for copy in copies[:3]:
        copy.wait()
    entries = pairs_ref.shape[1]
    group_rows = targets_ref.shape[0] // (n_row // 2 * n_col)
    lane = lax.broadcasted_iota(jnp.int32, (1, LANES), 1)
    for half in range(BLOCK_DEV):
        extra_ref[half] = jnp.zeros((ROWS, LANES), f32)
        for part in range(2):
            start = half * BLOCK + part * LANES
            extra_ref[half, 4 * part : 4 * part + 3, :] = positions_ref[:, start : start + LANES]
        extra_ref[half, 3:4, :] = jnp.where(lane == LANES - 1, counts_ref[0], 0).astype(f32)
        extra_ref[half, 3:4, 0:entries] = pairs_ref[0:1, :].astype(f32)
        extra_ref[half, 7:8, 0:entries] = pairs_ref[1:2, :].astype(f32)
    copies[3].wait()
    for row in range(n_row):
        for col in range(n_col):
            device = row * n_col + col
            group = row // 2 * n_col + col
            half = row % 2
            if group_rows < ROWS:
                out_ref[device, :, 0:BLOCK] = jnp.zeros((ROWS, BLOCK), f32)
            out_ref[device, 0:group_rows, 0:BLOCK] = targets_ref[
                group * group_rows : (group + 1) * group_rows, half * BLOCK : (half + 1) * BLOCK
            ]
            out_ref[device, :, BLOCK : BLOCK + LANES] = extra_ref[half]


def split(value, pieces):
    found = []
    for _ in range(pieces):
        piece = value.astype(bf16).astype(f32)
        found.append(piece)
        value = value - piece
    return found


def point_factors(extra):
    row = lax.broadcasted_iota(jnp.int32, (ROWS, BLOCK), 0)
    coords = jnp.concatenate([extra, pltpu.roll(extra, 4, 0)], axis=1)
    coords = jnp.where(row < 3, (coords - 0.5) * (1.0 / support_radius), 0.0)
    first, second, third = split(coords, 3)
    norm = jnp.sum(coords * coords, axis=0, keepdims=True)
    norm_pieces = split(jnp.broadcast_to(norm, (ROWS, BLOCK)), 3)
    zero = jnp.zeros((ROWS, BLOCK), f32)
    norms = jnp.where(
        row == 0, norm_pieces[0], jnp.where(row == 1, norm_pieces[1], jnp.where(row == 2, norm_pieces[2], zero))
    )
    ones = jnp.where(row < 3, 1.0, 0.0).astype(f32)
    left = jnp.concatenate([first, first, second, second, first, third, norms, ones], axis=0)
    right = jnp.concatenate(
        [-2.0 * piece for piece in (first, second, first, second, third, first)] + [ones, norms], axis=0
    )
    return left, right


def form_tile(left, right, times):
    square = jnp.maximum(jnp.dot(left, right, preferred_element_type=f32), 1e-30)
    remain = jnp.maximum(1.0 - square * lax.rsqrt(square), 0.0)
    remain_two = remain * remain
    tile = remain_two * remain_two * (1.25 * times - times * remain)
    head = tile.astype(bf16)
    return head, (tile - head.astype(f32)).astype(bf16)


def add_products(vector_ref, total_ref, row_block, col_block, row_to, head, tail):
    over_rows = (((1,), (0,)), ((), ()))
    over_cols = (((1,), (1,)), ((), ()))
    row_vector, col_vector = vector_ref[row_block], vector_ref[col_block]
    to_cols = lax.dot_general(row_vector, head, over_rows, preferred_element_type=f32) + lax.dot_general(
        row_vector, tail, over_rows, preferred_element_type=f32
    )
    to_rows = lax.dot_general(col_vector, head, over_cols, preferred_element_type=f32) + lax.dot_general(
        col_vector, tail, over_cols, preferred_element_type=f32
    )
    total_ref[col_block] += to_cols
    total_ref[row_to] += to_rows


def store_pieces(vector_ref, block, value, with_ones):
    parts = split(value, 2)
    if with_ones:
        row = lax.broadcasted_iota(jnp.int32, (2 * ROWS, BLOCK), 0)
        parts.append(jnp.where(row == 0, 1.0, 0.0).astype(f32))
    vector_ref[block] = jnp.concatenate(parts, axis=0).astype(bf16)


def global_blocks(n_col, meta_ref, device):
    row_ids = meta_ref[device, 3:4, BLOCK : BLOCK + LANES].astype(jnp.int32)
    col_ids = meta_ref[device, 7:8, BLOCK : BLOCK + LANES].astype(jnp.int32)
    count = row_ids[:, LANES - 1 :]
    in_use = lax.broadcasted_iota(jnp.int32, (1, LANES), 1) < count
    row_block = (device // n_col) * (n_col * BLOCK_DEV) + row_ids
    col_block = ((col_ids >> 1) * n_col + lax.rem(device, n_col)) * BLOCK_DEV + (col_ids & 1)
    return jnp.minimum(row_block, col_block), jnp.maximum(row_block, col_block), in_use


def merged_list(n_dev, n_col, core, meta_ref, keys_ref, times_ref):
    blocks = n_dev * BLOCK_DEV
    block_id = lax.broadcasted_iota(jnp.int32, (blocks, LANES), 0)
    smaller, larger = [], []
    for device in range(n_dev):
        low, high, in_use = global_blocks(n_col, meta_ref, device)
        smaller.append(jnp.where((block_id == low) & in_use, 1.0, 0.0))
        larger.append(jnp.where((block_id == high) & in_use, 1.0, 0.0))
    over_lanes = (((1,), (1,)), ((), ()))
    times = lax.dot_general(
        jnp.concatenate(larger, axis=1).astype(bf16),
        jnp.concatenate(smaller, axis=1).astype(bf16),
        over_lanes,
        preferred_element_type=f32,
    )
    present = jnp.where(times > 0.0, 1.0, 0.0)
    high_id = lax.broadcasted_iota(jnp.int32, (blocks, blocks), 0)
    low_id = lax.broadcasted_iota(jnp.int32, (blocks, blocks), 1)
    before = jnp.where(high_id > low_id, 1.0, 0.0).astype(bf16)
    present_low = present.astype(bf16)
    in_column = jnp.dot(before, present_low, preferred_element_type=f32)
    column_sums = jnp.sum(present, axis=0, keepdims=True)
    column_starts = lax.dot_general(
        jnp.broadcast_to(column_sums, (ROWS, blocks)).astype(bf16), before, over_lanes, preferred_element_type=f32
    )[0:1]
    place = (in_column + column_starts).astype(jnp.int32)
    mine = (present > 0.0) & ((place & 1) == core)
    slot = jnp.where(mine, place >> 1, -1)
    key = low_id * blocks + high_id
    lane = lax.broadcasted_iota(jnp.int32, (blocks, LISTED), 1)
    keys = jnp.zeros((blocks, LISTED), jnp.int32)
    counted = jnp.zeros((blocks, LISTED), f32)
    for low in range(blocks):
        here = lane == slot[:, low : low + 1]
        keys = keys + jnp.where(here, key[:, low : low + 1], 0)
        counted = counted + jnp.where(here, times[:, low : low + 1], 0.0)
    held = jnp.sum(jnp.where(mine, 1.0, 0.0), axis=1, keepdims=True)
    held = jnp.sum(held, axis=0, keepdims=True).astype(jnp.int32)
    first_lane = lax.broadcasted_iota(jnp.int32, (1, LISTED), 1)
    keys_ref[...] = jnp.where(
        first_lane == LISTED - 1, held, jnp.sum(keys.astype(f32), axis=0, keepdims=True).astype(jnp.int32)
    )
    times_ref[...] = jnp.sum(counted, axis=0, keepdims=True)


def read_key(list_ref, slot, blocks):
    key = list_ref[0, slot]
    row_block, col_block = lax.div(key, blocks), lax.rem(key, blocks)
    return row_block, col_block, jnp.where(row_block == col_block, blocks, row_block)


def assemble_block(source, device, block, base_ref, vector_ref, left_ref, right_ref):
    values = source[device, :, 0:BLOCK]
    base_ref[block] = values
    store_pieces(vector_ref, block, values, True)
    left, right = point_factors(source[device, :, BLOCK : BLOCK + LANES])
    left_ref[block] = left.T.astype(bf16)
    right_ref[block] = right.astype(bf16)


def finish_first(total_ref, partial_ref, blocks):
    for block in range(blocks):
        partial_ref[block] = total_ref[block, 0:ROWS] + total_ref[block, ROWS : 2 * ROWS]
        partial_ref[blocks + block // ROWS, block % ROWS : block % ROWS + 1, :] = total_ref[
            block, 2 * ROWS : 2 * ROWS + 1
        ]


def form_stored_kernel(
    n_row,
    n_col,
    mine_ref,
    other_ref,
    list_ref,
    base_ref,
    partial_ref,
    tiles_ref,
    times_ref,
    keys_vector,
    times_vector,
    list_sems,
    vector_ref,
    total_ref,
    left_ref,
    right_ref,
    sems,
    *place_refs,
):
    n_dev = n_row * n_col
    blocks = n_dev * BLOCK_DEV
    core = lax.rem(lax.axis_index("row"), 2)
    merged_list(n_dev, n_col, core, mine_ref, keys_vector, times_vector)
    keys_copy = pltpu.make_async_copy(keys_vector, list_ref, list_sems.at[0])
    times_copy = pltpu.make_async_copy(times_vector, times_ref, list_sems.at[1])
    keys_copy.start()
    times_copy.start()

    def assemble(device, carry):
        for source, half in ((mine_ref, core), (other_ref, 1 - core)):
            assemble_block(source, device, BLOCK_DEV * device + half, base_ref, vector_ref, left_ref, right_ref)
        return carry

    lax.fori_loop(0, n_dev, assemble, 0, unroll=2)
    total_ref[...] = jnp.zeros_like(total_ref)
    last_place = place_refs[TURN - 1]
    last_place[WRITE_SLOTS - 1] = jnp.zeros(last_place.shape[1:], bf16)
    keys_copy.wait()
    times_copy.wait()
    held = list_ref[0, LISTED - 1]

    def copies(turn):
        slot = lax.rem(turn, WRITE_SLOTS)
        return [
            pltpu.make_async_copy(place_refs[place].at[slot], tiles_ref.at[turn * TURN + place], sems.at[slot, place])
            for place in range(TURN)
        ]

    def wait_turn(turn):
        for copy in copies(turn):
            copy.wait()

    def multiply(entry, place, slot):
        row_block, col_block, row_to = read_key(list_ref, entry, blocks)
        head, tail = place_refs[place][slot, 0], place_refs[place][slot, 1]
        add_products(vector_ref, total_ref, row_block, col_block, row_to, head, tail)

    def run_turn(turn, carry):
        slot = lax.rem(turn, WRITE_SLOTS)
        pl.when(turn >= WRITE_SLOTS)(lambda: wait_turn(turn - WRITE_SLOTS))
        for place in range(TURN):
            entry = turn * TURN + place
            row_block, col_block, _ = read_key(list_ref, entry, blocks)
            head, tail = form_tile(left_ref[row_block], right_ref[col_block], times_ref[0, entry])
            place_refs[place][slot, 0] = head
            place_refs[place][slot, 1] = tail
            if place:
                multiply(entry - 1, place - 1, slot)
            else:
                multiply(jnp.maximum(entry - 1, 0), TURN - 1, WRITE_SLOTS - 1 - slot)
        for copy in copies(turn):
            copy.start()
        return carry

    turns = (held + TURN - 1) // TURN
    lax.fori_loop(0, turns, run_turn, 0)
    multiply(turns * TURN - 1, TURN - 1, lax.rem(turns - 1, WRITE_SLOTS))
    finish_first(total_ref, partial_ref, blocks)
    pl.when(turns >= 2)(lambda: wait_turn(turns - 2))
    wait_turn(turns - 1)


def form_kernel(
    n_row, n_col, mine_ref, other_ref, list_ref, base_ref, partial_ref, left_ref, right_ref, meta_ref, meta_sem, vector_ref, total_ref
):
    n_dev = n_row * n_col
    blocks = n_dev * BLOCK_DEV
    core = lax.rem(lax.axis_index("row"), 2)
    meta_copy = pltpu.make_async_copy(mine_ref.at[:, :, BLOCK : BLOCK + LANES], meta_ref, meta_sem)
    meta_copy.start()

    def assemble(device, carry):
        for source, half in ((mine_ref, core), (other_ref, 1 - core)):
            assemble_block(source, device, BLOCK_DEV * device + half, base_ref, vector_ref, left_ref, right_ref)
        return carry

    lax.fori_loop(0, n_dev, assemble, 0)
    total_ref[...] = jnp.zeros_like(total_ref)
    meta_copy.wait()

    def read_device(device, carry):
        seen, held = carry
        row = device // n_col
        col = lax.rem(device, n_col)
        count = meta_ref[device, 3, LANES - 1].astype(jnp.int32)
        first = lax.rem(seen + core, 2)
        taken = (count - first + 1) // 2

        def read_entry(index, carry):
            slot = first + 2 * index
            row_id = meta_ref[device, 3, slot].astype(jnp.int32)
            col_id = meta_ref[device, 7, slot].astype(jnp.int32)
            row_block = row * (n_col * BLOCK_DEV) + row_id
            col_block = ((col_id // BLOCK_DEV) * n_col + col) * BLOCK_DEV + lax.rem(col_id, BLOCK_DEV)
            list_ref[0, held + index] = row_block * blocks + col_block
            return carry

        lax.fori_loop(0, taken, read_entry, 0)
        return seen + count, held + taken

    _, held = lax.fori_loop(0, n_dev, read_device, (0, 0))
    list_ref[0, list_ref.shape[1] - 1] = held
    apply_formed(list_ref, (left_ref, right_ref), vector_ref, total_ref, blocks)
    finish_first(total_ref, partial_ref, blocks)


def apply_formed(list_ref, factor_refs, vector_ref, total_ref, blocks):
    def run_entry(entry, carry):
        row_block, col_block, row_to = read_key(list_ref, entry, blocks)
        head, tail = form_tile(factor_refs[0][row_block], factor_refs[1][col_block], 1.0)
        add_products(vector_ref, total_ref, row_block, col_block, row_to, head, tail)
        return carry

    lax.fori_loop(0, list_ref[0, list_ref.shape[1] - 1], run_entry, 0)


def read_copy(turn, tiles_ref, buffer_ref, sems):
    span = pl.ds(turn * TURN, TURN)
    return pltpu.make_async_copy(tiles_ref.at[span], buffer_ref.at[span], sems.at[turn])


def start_reads(list_ref, tiles_ref, buffer_ref, sems):
    def start(turn, carry):
        read_copy(turn, tiles_ref, buffer_ref, sems).start()
        return carry

    lax.fori_loop(0, (list_ref[0, LISTED - 1] + TURN - 1) // TURN, start, 0)


def apply_stored(list_ref, tiles_ref, buffer_ref, sems, vector_ref, total_ref, blocks):
    turns = (list_ref[0, LISTED - 1] + TURN - 1) // TURN

    def run_turns(first, count):
        for turn in range(count):
            read_copy(first + turn, tiles_ref, buffer_ref, sems).wait()
        for place in range(count * TURN):
            entry = first * TURN + place
            row_block, col_block, row_to = read_key(list_ref, entry, blocks)
            head, tail = buffer_ref[entry, 0], buffer_ref[entry, 1]
            add_products(vector_ref, total_ref, row_block, col_block, row_to, head, tail)

    def run_pair(pair, carry):
        run_turns(2 * pair, 2)
        return carry

    lax.fori_loop(0, turns // 2, run_pair, 0)
    pl.when(lax.rem(turns, 2) == 1)(lambda: run_turns(turns - 1, 1))


def apply_tiles(stored, value_ref, list_ref, held_refs, partial_ref, scratch):
    blocks = value_ref.shape[0]
    vector_ref, total_ref = scratch[:2]

    def put_block(block, carry):
        store_pieces(vector_ref, block, value_ref[block], False)
        return carry

    lax.fori_loop(0, blocks, put_block, 0, unroll=8)
    total_ref[...] = jnp.zeros_like(total_ref)
    if stored:
        apply_stored(list_ref, held_refs[0], scratch[2], scratch[3], vector_ref, total_ref, blocks)
    else:
        apply_formed(list_ref, held_refs, vector_ref, total_ref, blocks)
    partial_ref[...] = total_ref[0:blocks, 0:ROWS] + total_ref[0:blocks, ROWS : 2 * ROWS]


def row_sum(value):
    return jnp.sum(jnp.sum(value, axis=0, keepdims=True), axis=2, keepdims=True)


def first_step_kernel(stored, list_ref, mine_ref, other_ref, base_ref, *rest):
    count = 1 if stored else 2
    held, rest = rest[:count], rest[count:]
    residual_ref, direction_ref, partial_ref, scalars_ref, *scratch = rest
    if stored:
        start_reads(list_ref, held[0], scratch[2], scratch[3])
    blocks = base_ref.shape[0]
    largest = jnp.max(mine_ref[blocks:] + other_ref[blocks:])
    base = base_ref[...]
    applied = ridge_shift * base + (mine_ref[0:blocks] + other_ref[0:blocks]) / largest
    norm_now = row_sum(base * base)
    step_size = norm_now / row_sum(base * applied)
    residual = base - step_size * applied
    norm_next = row_sum(residual * residual)
    direction = residual + (norm_next / norm_now) * base
    residual_ref[...] = residual
    direction_ref[...] = direction
    scalars_ref[0] = jnp.broadcast_to(step_size[0], (ROWS, LANES))
    scalars_ref[1] = jnp.broadcast_to(norm_next[0], (ROWS, LANES))
    scalars_ref[2] = jnp.full((ROWS, LANES), largest, f32)
    apply_tiles(stored, direction_ref, list_ref, held, partial_ref, scratch)


def next_step_kernel(
    stored, list_ref, mine_ref, other_ref, base_ref, residual_ref, direction_ref, scalars_ref, *rest
):
    count = 1 if stored else 2
    held, rest = rest[:count], rest[count:]
    weights_out, residual_out, direction_out, partial_ref, scalars_out, *scratch = rest
    if stored:
        start_reads(list_ref, held[0], scratch[2], scratch[3])
    step_before = scalars_ref[0:1, :, 0:1]
    norm_now = scalars_ref[1:2, :, 0:1]
    largest = scalars_ref[2:3, :, 0:1]
    direction = direction_ref[...]
    applied = ridge_shift * direction + (mine_ref[...] + other_ref[...]) / largest
    step_size = norm_now / row_sum(direction * applied)
    weights_out[...] = step_before * base_ref[...] + step_size * direction
    residual = residual_ref[...] - step_size * applied
    norm_next = row_sum(residual * residual)
    residual_out[...] = residual
    direction_out[...] = residual + (norm_next / norm_now) * direction
    scalars_out[0] = scalars_ref[0]
    scalars_out[1] = jnp.broadcast_to(norm_next[0], (ROWS, LANES))
    scalars_out[2] = scalars_ref[2]
    apply_tiles(stored, direction_out, list_ref, held, partial_ref, scratch)


def last_step_kernel(mine_ref, other_ref, weights_ref, residual_ref, direction_ref, scalars_ref, out_ref):
    norm_now = scalars_ref[1:2, :, 0:1]
    largest = scalars_ref[2:3, :, 0:1]
    direction = direction_ref[...]
    applied = ridge_shift * direction + (mine_ref[...] + other_ref[...]) / largest
    step_size = norm_now / row_sum(direction * applied)
    core = lax.rem(lax.axis_index("row"), 2)

    @pl.when(core == 0)
    def _():
        out_ref[...] = weights_ref[...] + step_size * direction

    @pl.when(core == 1)
    def _():
        out_ref[...] = residual_ref[...] - step_size * applied


def unpack_kernel(n_row, n_col, group_rows, received_ref, weights_ref, residual_ref):
    for row in range(n_row):
        target = residual_ref if row % 2 else weights_ref
        for col in range(n_col):
            start = (row // 2 * n_col + col) * group_rows
            for half in range(BLOCK_DEV):
                target[start : start + group_rows, half * BLOCK : (half + 1) * BLOCK] = received_ref[
                    (row * n_col + col) * BLOCK_DEV + half, 0:group_rows
                ]


def call(kernel, out_shape, *args, scratch=(), in_spaces=None, out_spaces=None, vmem=16):
    spaces = in_spaces or [pltpu.VMEM] * len(args)
    outs = out_spaces or jax.tree.map(lambda _: pltpu.VMEM, out_shape)
    return pl.pallas_call(
        kernel,
        out_shape=out_shape,
        in_specs=[pl.BlockSpec(memory_space=space) for space in spaces],
        out_specs=jax.tree.map(lambda space: pl.BlockSpec(memory_space=space), outs),
        scratch_shapes=list(scratch),
        compiler_params=pltpu.CompilerParams(vmem_limit_bytes=vmem * 2**20),
    )(*args)


def local(positions, targets, pairs, counts):
    n_row = lax.axis_size("row")
    n_col = lax.axis_size("col")
    n_dev = n_row * n_col
    blocks = n_dev * BLOCK_DEV
    entries = pairs.shape[1]
    group_rows = targets.shape[0] // (n_dev // 2)
    room = -(-(n_dev * entries // 2) // TURN) * TURN
    stored = room <= STORED_MAX
    both = ("row", "col")
    siblings = [(index, index ^ 1) for index in range(n_row)]
    shape = jax.ShapeDtypeStruct
    kept = pltpu.VMEM if stored else shape
    vmem = 52 if stored else 58
    field = kept((blocks, ROWS, BLOCK), f32)
    scalars = kept((3, ROWS, LANES), f32)

    def resident(array):
        return pltpu.with_memory_space_constraint(array, pltpu.VMEM) if stored else array

    def from_sibling(array):
        return resident(lax.ppermute(array, "row", siblings))

    packed = call(
        functools.partial(pack_kernel, n_row, n_col),
        kept((n_dev, ROWS, BLOCK + LANES), f32),
        targets,
        positions,
        pairs,
        counts,
        in_spaces=[pl.ANY] * 4,
        scratch=[
            pltpu.VMEM(targets.shape, f32),
            pltpu.VMEM(positions.shape, f32),
            pltpu.VMEM(pairs.shape, jnp.int32),
            pltpu.SMEM(counts.shape, jnp.int32),
            pltpu.VMEM((BLOCK_DEV, ROWS, LANES), f32),
            pltpu.SemaphoreType.DMA((4,)),
        ],
        vmem=60,
    )
    mine = resident(lax.all_to_all(resident(packed), both, 0, 0, tiled=True))
    other = from_sibling(mine)

    factors = [((blocks, BLOCK, PIECE_DEPTH), bf16), ((blocks, PIECE_DEPTH, BLOCK), bf16)]
    factor_scratch = [pltpu.VMEM(*factor) for factor in factors]
    first_partial = kept((blocks + -(-blocks // ROWS), ROWS, BLOCK), f32)
    first_scratch = [
        pltpu.VMEM((blocks, 4 * ROWS, BLOCK), bf16),
        pltpu.VMEM((blocks + 1, 4 * ROWS, BLOCK), f32),
    ]
    step_scratch = [
        pltpu.VMEM((blocks, 2 * ROWS, BLOCK), bf16),
        pltpu.VMEM((blocks + 1, 2 * ROWS, BLOCK), f32),
    ]
    if stored:
        listed, base, partial, *held = call(
            functools.partial(form_stored_kernel, n_row, n_col),
            [shape((1, LISTED), jnp.int32), field, first_partial, shape((room, 2, BLOCK, BLOCK), bf16)],
            mine,
            other,
            out_spaces=[pltpu.SMEM, pltpu.VMEM, pltpu.VMEM, pl.ANY],
            scratch=[
                pltpu.SMEM((1, LISTED), f32),
                pltpu.VMEM((1, LISTED), jnp.int32),
                pltpu.VMEM((1, LISTED), f32),
                pltpu.SemaphoreType.DMA((2,)),
                *first_scratch,
                *factor_scratch,
                pltpu.SemaphoreType.DMA((WRITE_SLOTS, TURN)),
                *[pltpu.VMEM((WRITE_SLOTS, 2, BLOCK, BLOCK), bf16)] * TURN,
            ],
            vmem=vmem,
        )
        held_spaces = [pl.ANY]
        step_scratch += [
            pltpu.VMEM((room, 2, BLOCK, BLOCK), bf16),
            pltpu.SemaphoreType.DMA((room // TURN,)),
        ]
    else:
        listed, base, partial, *held = call(
            functools.partial(form_kernel, n_row, n_col),
            [shape((1, room + 1), jnp.int32), field, first_partial, *(shape(*factor) for factor in factors)],
            mine,
            other,
            out_spaces=[pltpu.SMEM] + [pltpu.VMEM] * 4,
            scratch=[pltpu.SMEM((n_dev, ROWS, LANES), f32), pltpu.SemaphoreType.DMA, *first_scratch],
            vmem=vmem,
        )
        held_spaces = [pltpu.VMEM] * 2
    base, partial = resident(base), resident(partial)

    def step(kernel, out_shape, *args):
        outs = call(
            functools.partial(kernel, stored),
            out_shape,
            listed,
            *args,
            *held,
            in_spaces=[pltpu.SMEM] + [pltpu.VMEM] * len(args) + held_spaces,
            scratch=step_scratch,
            vmem=vmem,
        )
        return [resident(out) for out in outs]

    residual, direction, partial, numbers = step(
        first_step_kernel, (field, field, field, scalars), partial, from_sibling(partial), base
    )
    weights, residual, direction, partial, numbers = step(
        next_step_kernel,
        (field, field, field, field, scalars),
        partial,
        from_sibling(partial),
        base,
        residual,
        direction,
        numbers,
    )
    result = call(
        last_step_kernel, field, partial, from_sibling(partial), weights, residual, direction, numbers
    )
    home = resident(lax.all_to_all(resident(result), both, 0, 0, tiled=True))
    out = shape(targets.shape, f32)
    return call(functools.partial(unpack_kernel, n_row, n_col, group_rows), (out, out), home)


def solution(mesh):
    placed = (
        P(None, ("groups", "row", "col")),
        P(None, ("groups", "row", "col")),
        P(None, ("groups", "row", "col")),
        P(("groups", "row", "col")),
    )
    return jax.shard_map(
        local,
        mesh=mesh,
        in_specs=placed,
        out_specs=(P(None, ("groups", "row", "col")), P(None, ("groups", "row", "col"))),
        check_vma=False,
    )
```

```python
import functools

import jax
import jax.numpy as jnp
from jax import lax
from jax.experimental import pallas as pl
from jax.experimental.pallas import tpu as pltpu
from jax.sharding import PartitionSpec as P

BLOCK = 256
BLOCK_DEV = 2
LANES = 128
POINTS_DEV = BLOCK * BLOCK_DEV
ROWS = 8
PIECE_DEPTH = 64
TURN = 8
STORED_MAX = 192
LISTED = 256
WRITE_SLOTS = 2

support_radius = 0.5
ridge_shift = 1.5
f32 = jnp.float32
bf16 = jnp.bfloat16


def pack_kernel(
    n_row, n_col, targets_in, positions_in, pairs_in, counts_in, out_ref, targets_ref, positions_ref, pairs_ref, counts_ref, extra_ref, sems
):
    copies = [
        pltpu.make_async_copy(source, kept, sems.at[index])
        for index, (source, kept) in enumerate(
            (
                (positions_in, positions_ref),
                (pairs_in, pairs_ref),
                (counts_in, counts_ref),
                (targets_in, targets_ref),
            )
        )
    ]
    for copy in copies:
        copy.start()
    for copy in copies[:3]:
        copy.wait()
    entries = pairs_ref.shape[1]
    groups = n_row // 2 * n_col
    group_rows = targets_ref.shape[0] // groups
    lane = lax.broadcasted_iota(jnp.int32, (1, BLOCK), 1)
    for half in range(BLOCK_DEV):
        extra_ref[4 * half : 4 * half + 3, :] = positions_ref[:, half * BLOCK : (half + 1) * BLOCK]
    extra_ref[3:4, :] = jnp.where(lane == LANES - 1, counts_ref[0], 0).astype(f32)
    extra_ref[7:8, :] = jnp.zeros((1, BLOCK), f32)
    extra_ref[3:4, 0:entries] = pairs_ref[0:1, :].astype(f32)
    extra_ref[7:8, 0:entries] = pairs_ref[1:2, :].astype(f32)
    copies[3].wait()
    for group in range(groups):
        if group_rows < ROWS:
            out_ref[group, :, 0:POINTS_DEV] = jnp.zeros((ROWS, POINTS_DEV), f32)
        out_ref[group, 0:group_rows, 0:POINTS_DEV] = targets_ref[group * group_rows : (group + 1) * group_rows, :]
        out_ref[group, :, POINTS_DEV : POINTS_DEV + BLOCK] = extra_ref[...]


def split(value, pieces):
    found = []
    for _ in range(pieces):
        piece = value.astype(bf16).astype(f32)
        found.append(piece)
        value = value - piece
    return found


def point_factors(extra, half):
    row = lax.broadcasted_iota(jnp.int32, (ROWS, BLOCK), 0)
    coords = pltpu.roll(extra, 4, 0) if half else extra
    coords = jnp.where(row < 3, (coords - 0.5) * (1.0 / support_radius), 0.0)
    first, second, third = split(coords, 3)
    norm = jnp.sum(coords * coords, axis=0, keepdims=True)
    norm_pieces = split(jnp.broadcast_to(norm, (ROWS, BLOCK)), 3)
    zero = jnp.zeros((ROWS, BLOCK), f32)
    norms = jnp.where(
        row == 0, norm_pieces[0], jnp.where(row == 1, norm_pieces[1], jnp.where(row == 2, norm_pieces[2], zero))
    )
    ones = jnp.where(row < 3, 1.0, 0.0).astype(f32)
    left = jnp.concatenate([first, first, second, second, first, third, norms, ones], axis=0)
    right = jnp.concatenate(
        [-2.0 * piece for piece in (first, second, first, second, third, first)] + [ones, norms], axis=0
    )
    return left, right


def form_tile(left, right, times):
    square = jnp.maximum(jnp.dot(left, right, preferred_element_type=f32), 1e-30)
    remain = jnp.maximum(1.0 - square * lax.rsqrt(square), 0.0)
    remain_two = remain * remain
    tile = remain_two * remain_two * (1.25 * times - times * remain)
    head = tile.astype(bf16)
    return head, (tile - head.astype(f32)).astype(bf16)


def add_products(vector_ref, total_ref, row_block, col_block, row_to, head, tail):
    over_rows = (((1,), (0,)), ((), ()))
    over_cols = (((1,), (1,)), ((), ()))
    row_vector, col_vector = vector_ref[row_block], vector_ref[col_block]
    to_cols = lax.dot_general(row_vector, head, over_rows, preferred_element_type=f32) + lax.dot_general(
        row_vector, tail, over_rows, preferred_element_type=f32
    )
    to_rows = lax.dot_general(col_vector, head, over_cols, preferred_element_type=f32) + lax.dot_general(
        col_vector, tail, over_cols, preferred_element_type=f32
    )
    total_ref[col_block] += to_cols
    total_ref[row_to] += to_rows


def store_pieces(vector_ref, block, value, with_ones):
    parts = split(value, 2)
    if with_ones:
        row = lax.broadcasted_iota(jnp.int32, (2 * ROWS, BLOCK), 0)
        parts.append(jnp.where(row == 0, 1.0, 0.0).astype(f32))
    vector_ref[block] = jnp.concatenate(parts, axis=0).astype(bf16)


def global_blocks(n_col, source, group, core):
    row_ids = source[group, 3:4, POINTS_DEV : POINTS_DEV + LANES].astype(jnp.int32)
    col_ids = source[group, 7:8, POINTS_DEV : POINTS_DEV + LANES].astype(jnp.int32)
    count = row_ids[:, LANES - 1 :]
    row, col = 2 * (group // n_col) + core, group % n_col
    in_use = lax.broadcasted_iota(jnp.int32, (1, LANES), 1) < count
    row_block = row * (n_col * BLOCK_DEV) + row_ids
    col_block = ((col_ids >> 1) * n_col + col) * BLOCK_DEV + (col_ids & 1)
    return jnp.minimum(row_block, col_block), jnp.maximum(row_block, col_block), in_use


def merged_list(n_dev, n_col, core, sources, keys_ref, times_ref):
    blocks = n_dev * BLOCK_DEV
    block_id = lax.broadcasted_iota(jnp.int32, (blocks, LANES), 0)
    smaller, larger = [], []
    for source, source_core in sources:
        for group in range(n_dev // 2):
            low, high, in_use = global_blocks(n_col, source, group, source_core)
            smaller.append(jnp.where((block_id == low) & in_use, 1.0, 0.0))
            larger.append(jnp.where((block_id == high) & in_use, 1.0, 0.0))
    over_lanes = (((1,), (1,)), ((), ()))
    times = lax.dot_general(
        jnp.concatenate(larger, axis=1).astype(bf16),
        jnp.concatenate(smaller, axis=1).astype(bf16),
        over_lanes,
        preferred_element_type=f32,
    )
    present = jnp.where(times > 0.0, 1.0, 0.0)
    high_id = lax.broadcasted_iota(jnp.int32, (blocks, blocks), 0)
    low_id = lax.broadcasted_iota(jnp.int32, (blocks, blocks), 1)
    before = jnp.where(high_id > low_id, 1.0, 0.0).astype(bf16)
    present_low = present.astype(bf16)
    in_column = jnp.dot(before, present_low, preferred_element_type=f32)
    column_sums = jnp.sum(present, axis=0, keepdims=True)
    column_starts = lax.dot_general(
        jnp.broadcast_to(column_sums, (ROWS, blocks)).astype(bf16), before, over_lanes, preferred_element_type=f32
    )[0:1]
    place = (in_column + column_starts).astype(jnp.int32)
    mine = (present > 0.0) & ((place & 1) == core)
    slot = jnp.where(mine, place >> 1, -1)
    key = low_id * blocks + high_id
    lane = lax.broadcasted_iota(jnp.int32, (blocks, LISTED), 1)
    keys = jnp.zeros((blocks, LISTED), jnp.int32)
    counted = jnp.zeros((blocks, LISTED), f32)
    for low in range(blocks):
        here = lane == slot[:, low : low + 1]
        keys = keys + jnp.where(here, key[:, low : low + 1], 0)
        counted = counted + jnp.where(here, times[:, low : low + 1], 0.0)
    held = jnp.sum(jnp.where(mine, 1.0, 0.0), axis=1, keepdims=True)
    held = jnp.sum(held, axis=0, keepdims=True).astype(jnp.int32)
    first_lane = lax.broadcasted_iota(jnp.int32, (1, LISTED), 1)
    keys_ref[...] = jnp.where(
        first_lane == LISTED - 1, held, jnp.sum(keys.astype(f32), axis=0, keepdims=True).astype(jnp.int32)
    )
    times_ref[...] = jnp.sum(counted, axis=0, keepdims=True)


def read_key(list_ref, slot, blocks):
    key = list_ref[0, slot]
    row_block, col_block = lax.div(key, blocks), lax.rem(key, blocks)
    return row_block, col_block, jnp.where(row_block == col_block, blocks, row_block)


def assemble_group(n_col, group, sources, base_ref, vector_ref, left_ref, right_ref):
    for source, source_core in sources:
        device = (2 * (group // n_col) + source_core) * n_col + lax.rem(group, n_col)
        extra = source[group, :, POINTS_DEV : POINTS_DEV + BLOCK]
        for half in range(BLOCK_DEV):
            block = BLOCK_DEV * device + half
            values = source[group, :, half * BLOCK : (half + 1) * BLOCK]
            base_ref[block] = values
            store_pieces(vector_ref, block, values, True)
            left, right = point_factors(extra, half)
            left_ref[block] = left.T.astype(bf16)
            right_ref[block] = right.astype(bf16)


def finish_first(total_ref, partial_ref, blocks):
    for block in range(blocks):
        partial_ref[block] = total_ref[block, 0:ROWS] + total_ref[block, ROWS : 2 * ROWS]
        partial_ref[blocks + block // ROWS, block % ROWS : block % ROWS + 1, :] = total_ref[
            block, 2 * ROWS : 2 * ROWS + 1
        ]


def form_stored_kernel(
    n_row,
    n_col,
    mine_ref,
    other_ref,
    list_ref,
    base_ref,
    partial_ref,
    tiles_ref,
    times_ref,
    keys_vector,
    times_vector,
    list_sems,
    vector_ref,
    total_ref,
    left_ref,
    right_ref,
    sems,
    *place_refs,
):
    n_dev = n_row * n_col
    blocks = n_dev * BLOCK_DEV
    core = lax.rem(lax.axis_index("row"), 2)
    sources = ((mine_ref, core), (other_ref, 1 - core))
    merged_list(n_dev, n_col, core, sources, keys_vector, times_vector)
    keys_copy = pltpu.make_async_copy(keys_vector, list_ref, list_sems.at[0])
    times_copy = pltpu.make_async_copy(times_vector, times_ref, list_sems.at[1])
    keys_copy.start()
    times_copy.start()

    def assemble(group, carry):
        assemble_group(n_col, group, sources, base_ref, vector_ref, left_ref, right_ref)
        return carry

    lax.fori_loop(0, n_dev // 2, assemble, 0)
    total_ref[...] = jnp.zeros_like(total_ref)
    last_place = place_refs[TURN - 1]
    last_place[WRITE_SLOTS - 1] = jnp.zeros(last_place.shape[1:], bf16)
    keys_copy.wait()
    times_copy.wait()
    held = list_ref[0, LISTED - 1]

    def copies(turn):
        slot = lax.rem(turn, WRITE_SLOTS)
        return [
            pltpu.make_async_copy(place_refs[place].at[slot], tiles_ref.at[turn * TURN + place], sems.at[slot, place])
            for place in range(TURN)
        ]

    def wait_turn(turn):
        for copy in copies(turn):
            copy.wait()

    def multiply(entry, place, slot):
        row_block, col_block, row_to = read_key(list_ref, entry, blocks)
        head, tail = place_refs[place][slot, 0], place_refs[place][slot, 1]
        add_products(vector_ref, total_ref, row_block, col_block, row_to, head, tail)

    def run_turn(turn, carry):
        slot = lax.rem(turn, WRITE_SLOTS)
        pl.when(turn >= WRITE_SLOTS)(lambda: wait_turn(turn - WRITE_SLOTS))
        for place in range(TURN):
            entry = turn * TURN + place
            row_block, col_block, _ = read_key(list_ref, entry, blocks)
            head, tail = form_tile(left_ref[row_block], right_ref[col_block], times_ref[0, entry])
            place_refs[place][slot, 0] = head
            place_refs[place][slot, 1] = tail
            if place:
                multiply(entry - 1, place - 1, slot)
            else:
                multiply(jnp.maximum(entry - 1, 0), TURN - 1, WRITE_SLOTS - 1 - slot)
        for copy in copies(turn):
            copy.start()
        return carry

    turns = (held + TURN - 1) // TURN
    lax.fori_loop(0, turns, run_turn, 0)
    multiply(turns * TURN - 1, TURN - 1, lax.rem(turns - 1, WRITE_SLOTS))
    finish_first(total_ref, partial_ref, blocks)
    pl.when(turns >= 2)(lambda: wait_turn(turns - 2))
    wait_turn(turns - 1)


def form_kernel(
    n_row, n_col, mine_ref, other_ref, list_ref, base_ref, partial_ref, left_ref, right_ref, meta_ref, meta_sems, vector_ref, total_ref
):
    n_dev = n_row * n_col
    blocks = n_dev * BLOCK_DEV
    core = lax.rem(lax.axis_index("row"), 2)
    sources = ((mine_ref, core), (other_ref, 1 - core))
    meta_copies = [
        pltpu.make_async_copy(
            source.at[:, :, POINTS_DEV : POINTS_DEV + LANES], meta_ref.at[source_core], meta_sems.at[index]
        )
        for index, (source, source_core) in enumerate(sources)
    ]
    for copy in meta_copies:
        copy.start()

    def assemble(group, carry):
        assemble_group(n_col, group, sources, base_ref, vector_ref, left_ref, right_ref)
        return carry

    lax.fori_loop(0, n_dev // 2, assemble, 0)
    total_ref[...] = jnp.zeros_like(total_ref)
    for copy in meta_copies:
        copy.wait()

    def read_device(device, carry):
        seen, held = carry
        row = device // n_col
        col = lax.rem(device, n_col)
        source_core, group = lax.rem(row, 2), (row // 2) * n_col + col
        count = meta_ref[source_core, group, 3, LANES - 1].astype(jnp.int32)
        first = lax.rem(seen + core, 2)
        taken = (count - first + 1) // 2

        def read_entry(index, carry):
            slot = first + 2 * index
            row_id = meta_ref[source_core, group, 3, slot].astype(jnp.int32)
            col_id = meta_ref[source_core, group, 7, slot].astype(jnp.int32)
            row_block = row * (n_col * BLOCK_DEV) + row_id
            col_block = ((col_id // BLOCK_DEV) * n_col + col) * BLOCK_DEV + lax.rem(col_id, BLOCK_DEV)
            list_ref[0, held + index] = row_block * blocks + col_block
            return carry

        lax.fori_loop(0, taken, read_entry, 0)
        return seen + count, held + taken

    _, held = lax.fori_loop(0, n_dev, read_device, (0, 0))
    list_ref[0, list_ref.shape[1] - 1] = held
    apply_formed(list_ref, (left_ref, right_ref), vector_ref, total_ref, blocks)
    finish_first(total_ref, partial_ref, blocks)


def apply_formed(list_ref, factor_refs, vector_ref, total_ref, blocks):
    def run_entry(entry, carry):
        row_block, col_block, row_to = read_key(list_ref, entry, blocks)
        head, tail = form_tile(factor_refs[0][row_block], factor_refs[1][col_block], 1.0)
        add_products(vector_ref, total_ref, row_block, col_block, row_to, head, tail)
        return carry

    lax.fori_loop(0, list_ref[0, list_ref.shape[1] - 1], run_entry, 0)


def read_copy(turn, tiles_ref, buffer_ref, sems):
    span = pl.ds(turn * TURN, TURN)
    return pltpu.make_async_copy(tiles_ref.at[span], buffer_ref.at[span], sems.at[turn])


def start_reads(list_ref, tiles_ref, buffer_ref, sems):
    def start(turn, carry):
        read_copy(turn, tiles_ref, buffer_ref, sems).start()
        return carry

    lax.fori_loop(0, (list_ref[0, LISTED - 1] + TURN - 1) // TURN, start, 0)


def apply_stored(list_ref, tiles_ref, buffer_ref, sems, vector_ref, total_ref, blocks):
    turns = (list_ref[0, LISTED - 1] + TURN - 1) // TURN

    def run_turns(first, count):
        for turn in range(count):
            read_copy(first + turn, tiles_ref, buffer_ref, sems).wait()
        for place in range(count * TURN):
            entry = first * TURN + place
            row_block, col_block, row_to = read_key(list_ref, entry, blocks)
            head, tail = buffer_ref[entry, 0], buffer_ref[entry, 1]
            add_products(vector_ref, total_ref, row_block, col_block, row_to, head, tail)

    def run_pair(pair, carry):
        run_turns(2 * pair, 2)
        return carry

    lax.fori_loop(0, turns // 2, run_pair, 0)
    pl.when(lax.rem(turns, 2) == 1)(lambda: run_turns(turns - 1, 1))


def apply_tiles(stored, value_ref, list_ref, held_refs, partial_ref, scratch):
    blocks = value_ref.shape[0]
    vector_ref, total_ref = scratch[:2]

    def put_block(block, carry):
        store_pieces(vector_ref, block, value_ref[block], False)
        return carry

    lax.fori_loop(0, blocks, put_block, 0, unroll=8)
    total_ref[...] = jnp.zeros_like(total_ref)
    if stored:
        apply_stored(list_ref, held_refs[0], scratch[2], scratch[3], vector_ref, total_ref, blocks)
    else:
        apply_formed(list_ref, held_refs, vector_ref, total_ref, blocks)
    partial_ref[...] = total_ref[0:blocks, 0:ROWS] + total_ref[0:blocks, ROWS : 2 * ROWS]


def row_sum(value):
    return jnp.sum(jnp.sum(value, axis=0, keepdims=True), axis=2, keepdims=True)


def first_step_kernel(stored, list_ref, mine_ref, other_ref, base_ref, *rest):
    count = 1 if stored else 2
    held, rest = rest[:count], rest[count:]
    residual_ref, direction_ref, partial_ref, scalars_ref, *scratch = rest
    if stored:
        start_reads(list_ref, held[0], scratch[2], scratch[3])
    blocks = base_ref.shape[0]
    largest = jnp.max(mine_ref[blocks:] + other_ref[blocks:])
    base = base_ref[...]
    applied = ridge_shift * base + (mine_ref[0:blocks] + other_ref[0:blocks]) / largest
    norm_now = row_sum(base * base)
    step_size = norm_now / row_sum(base * applied)
    residual = base - step_size * applied
    norm_next = row_sum(residual * residual)
    direction = residual + (norm_next / norm_now) * base
    residual_ref[...] = residual
    direction_ref[...] = direction
    scalars_ref[0] = jnp.broadcast_to(step_size[0], (ROWS, LANES))
    scalars_ref[1] = jnp.broadcast_to(norm_next[0], (ROWS, LANES))
    scalars_ref[2] = jnp.full((ROWS, LANES), largest, f32)
    apply_tiles(stored, direction_ref, list_ref, held, partial_ref, scratch)


def next_step_kernel(
    stored, list_ref, mine_ref, other_ref, base_ref, residual_ref, direction_ref, scalars_ref, *rest
):
    count = 1 if stored else 2
    held, rest = rest[:count], rest[count:]
    weights_out, residual_out, direction_out, partial_ref, scalars_out, *scratch = rest
    if stored:
        start_reads(list_ref, held[0], scratch[2], scratch[3])
    step_before = scalars_ref[0:1, :, 0:1]
    norm_now = scalars_ref[1:2, :, 0:1]
    largest = scalars_ref[2:3, :, 0:1]
    direction = direction_ref[...]
    applied = ridge_shift * direction + (mine_ref[...] + other_ref[...]) / largest
    step_size = norm_now / row_sum(direction * applied)
    weights_out[...] = step_before * base_ref[...] + step_size * direction
    residual = residual_ref[...] - step_size * applied
    norm_next = row_sum(residual * residual)
    residual_out[...] = residual
    direction_out[...] = residual + (norm_next / norm_now) * direction
    scalars_out[0] = scalars_ref[0]
    scalars_out[1] = jnp.broadcast_to(norm_next[0], (ROWS, LANES))
    scalars_out[2] = scalars_ref[2]
    apply_tiles(stored, direction_out, list_ref, held, partial_ref, scratch)


def last_step_kernel(
    n_row, n_col, mine_ref, other_ref, weights_ref, residual_ref, direction_ref, scalars_ref, out_ref
):
    norm_now = scalars_ref[1:2, :, 0:1]
    largest = scalars_ref[2:3, :, 0:1]
    direction = direction_ref[...]
    applied = ridge_shift * direction + (mine_ref[...] + other_ref[...]) / largest
    step_size = norm_now / row_sum(direction * applied)
    core = lax.rem(lax.axis_index("row"), 2)
    row_blocks = n_col * BLOCK_DEV
    for pair in range(n_row // 2):
        span = pl.ds((2 * pair + core) * row_blocks, row_blocks)
        direction = direction_ref[span]
        applied = ridge_shift * direction + (mine_ref[span] + other_ref[span]) / largest
        weights = weights_ref[span] + step_size * direction
        residual = residual_ref[span] - step_size * applied
        for col in range(n_col):
            start = (pair * n_col + col) * 2 * BLOCK_DEV
            taken = slice(col * BLOCK_DEV, (col + 1) * BLOCK_DEV)
            out_ref[start : start + BLOCK_DEV] = weights[taken]
            out_ref[start + BLOCK_DEV : start + 2 * BLOCK_DEV] = residual[taken]


def unpack_kernel(groups, group_rows, received_ref, weights_ref, residual_ref):
    for group in range(groups):
        rows = slice(group * group_rows, (group + 1) * group_rows)
        for index, target in enumerate((weights_ref, residual_ref)):
            for half in range(BLOCK_DEV):
                target[rows, half * BLOCK : (half + 1) * BLOCK] = received_ref[
                    (2 * group + index) * BLOCK_DEV + half, 0:group_rows
                ]


def call(kernel, out_shape, *args, scratch=(), in_spaces=None, out_spaces=None, vmem=16):
    spaces = in_spaces or [pltpu.VMEM] * len(args)
    outs = out_spaces or jax.tree.map(lambda _: pltpu.VMEM, out_shape)
    return pl.pallas_call(
        kernel,
        out_shape=out_shape,
        in_specs=[pl.BlockSpec(memory_space=space) for space in spaces],
        out_specs=jax.tree.map(lambda space: pl.BlockSpec(memory_space=space), outs),
        scratch_shapes=list(scratch),
        compiler_params=pltpu.CompilerParams(vmem_limit_bytes=vmem * 2**20),
    )(*args)


def local(positions, targets, pairs, counts):
    n_row = lax.axis_size("row")
    n_col = lax.axis_size("col")
    n_dev = n_row * n_col
    blocks = n_dev * BLOCK_DEV
    entries = pairs.shape[1]
    groups = n_dev // 2
    group_rows = targets.shape[0] // groups
    room = -(-(n_dev * entries // 2) // TURN) * TURN
    stored = room <= STORED_MAX
    same_core = [
        [row * n_col + col for row in range(core, n_row, 2) for col in range(n_col)] for core in range(2)
    ]
    siblings = [(index, index ^ 1) for index in range(n_row)]
    shape = jax.ShapeDtypeStruct
    kept = pltpu.VMEM if stored else shape
    vmem = 52 if stored else 58
    field = kept((blocks, ROWS, BLOCK), f32)
    scalars = kept((3, ROWS, LANES), f32)

    def resident(array):
        return pltpu.with_memory_space_constraint(array, pltpu.VMEM) if stored else array

    def from_sibling(array):
        return resident(lax.ppermute(array, "row", siblings))

    def among_cores(array):
        return resident(
            lax.all_to_all(array, ("row", "col"), 0, 0, axis_index_groups=same_core, tiled=True)
        )

    packed = call(
        functools.partial(pack_kernel, n_row, n_col),
        kept((groups, ROWS, POINTS_DEV + BLOCK), f32),
        targets,
        positions,
        pairs,
        counts,
        in_spaces=[pl.ANY] * 4,
        scratch=[
            pltpu.VMEM(targets.shape, f32),
            pltpu.VMEM(positions.shape, f32),
            pltpu.VMEM(pairs.shape, jnp.int32),
            pltpu.SMEM(counts.shape, jnp.int32),
            pltpu.VMEM((ROWS, BLOCK), f32),
            pltpu.SemaphoreType.DMA((4,)),
        ],
        vmem=60,
    )
    mine = among_cores(resident(packed))
    other = from_sibling(mine)

    factors = [((blocks, BLOCK, PIECE_DEPTH), bf16), ((blocks, PIECE_DEPTH, BLOCK), bf16)]
    factor_scratch = [pltpu.VMEM(*factor) for factor in factors]
    first_partial = kept((blocks + -(-blocks // ROWS), ROWS, BLOCK), f32)
    first_scratch = [
        pltpu.VMEM((blocks, 4 * ROWS, BLOCK), bf16),
        pltpu.VMEM((blocks + 1, 4 * ROWS, BLOCK), f32),
    ]
    step_scratch = [
        pltpu.VMEM((blocks, 2 * ROWS, BLOCK), bf16),
        pltpu.VMEM((blocks + 1, 2 * ROWS, BLOCK), f32),
    ]
    if stored:
        listed, base, partial, *held = call(
            functools.partial(form_stored_kernel, n_row, n_col),
            [shape((1, LISTED), jnp.int32), field, first_partial, shape((room, 2, BLOCK, BLOCK), bf16)],
            mine,
            other,
            out_spaces=[pltpu.SMEM, pltpu.VMEM, pltpu.VMEM, pl.ANY],
            scratch=[
                pltpu.SMEM((1, LISTED), f32),
                pltpu.VMEM((1, LISTED), jnp.int32),
                pltpu.VMEM((1, LISTED), f32),
                pltpu.SemaphoreType.DMA((2,)),
                *first_scratch,
                *factor_scratch,
                pltpu.SemaphoreType.DMA((WRITE_SLOTS, TURN)),
                *[pltpu.VMEM((WRITE_SLOTS, 2, BLOCK, BLOCK), bf16)] * TURN,
            ],
            vmem=vmem,
        )
        held_spaces = [pl.ANY]
        step_scratch += [
            pltpu.VMEM((room, 2, BLOCK, BLOCK), bf16),
            pltpu.SemaphoreType.DMA((room // TURN,)),
        ]
    else:
        listed, base, partial, *held = call(
            functools.partial(form_kernel, n_row, n_col),
            [shape((1, room + 1), jnp.int32), field, first_partial, *(shape(*factor) for factor in factors)],
            mine,
            other,
            out_spaces=[pltpu.SMEM] + [pltpu.VMEM] * 4,
            scratch=[
                pltpu.SMEM((2, n_dev // 2, ROWS, LANES), f32),
                pltpu.SemaphoreType.DMA((2,)),
                *first_scratch,
            ],
            vmem=vmem,
        )
        held_spaces = [pltpu.VMEM] * 2
    base, partial = resident(base), resident(partial)

    def step(kernel, out_shape, *args):
        outs = call(
            functools.partial(kernel, stored),
            out_shape,
            listed,
            *args,
            *held,
            in_spaces=[pltpu.SMEM] + [pltpu.VMEM] * len(args) + held_spaces,
            scratch=step_scratch,
            vmem=vmem,
        )
        return [resident(out) for out in outs]

    residual, direction, partial, numbers = step(
        first_step_kernel, (field, field, field, scalars), partial, from_sibling(partial), base
    )
    weights, residual, direction, partial, numbers = step(
        next_step_kernel,
        (field, field, field, field, scalars),
        partial,
        from_sibling(partial),
        base,
        residual,
        direction,
        numbers,
    )
    result = call(
        functools.partial(last_step_kernel, n_row, n_col),
        field,
        partial,
        from_sibling(partial),
        weights,
        residual,
        direction,
        numbers,
    )
    home = among_cores(resident(result))
    out = shape(targets.shape, f32)
    return call(functools.partial(unpack_kernel, groups, group_rows), (out, out), home)


def solution(mesh):
    placed = (
        P(None, ("groups", "row", "col")),
        P(None, ("groups", "row", "col")),
        P(None, ("groups", "row", "col")),
        P(("groups", "row", "col")),
    )
    return jax.shard_map(
        local,
        mesh=mesh,
        in_specs=placed,
        out_specs=(P(None, ("groups", "row", "col")), P(None, ("groups", "row", "col"))),
        check_vma=False,
    )
```

```python
import functools

import jax
import jax.numpy as jnp
from jax import lax
from jax.experimental import pallas as pl
from jax.experimental.pallas import tpu as pltpu
from jax.sharding import PartitionSpec as P

BLOCK = 256
BLOCK_DEV = 2
LANES = 128
POINTS_DEV = BLOCK * BLOCK_DEV
ROWS = 8
PIECE_DEPTH = 64
TURN = 8
HALF = TURN // 2
STORED_MAX = 192
LISTED = 256
WRITE_SLOTS = 2

support_radius = 0.5
ridge_shift = 1.5
f32 = jnp.float32
bf16 = jnp.bfloat16


def pack_kernel(
    n_row, n_col, targets_in, positions_in, pairs_in, counts_in, out_ref, targets_ref, positions_ref, pairs_ref, counts_ref, extra_ref, sems
):
    copies = [
        pltpu.make_async_copy(source, kept, sems.at[index])
        for index, (source, kept) in enumerate(
            (
                (positions_in, positions_ref),
                (pairs_in, pairs_ref),
                (counts_in, counts_ref),
                (targets_in, targets_ref),
            )
        )
    ]
    for copy in copies:
        copy.start()
    for copy in copies[:3]:
        copy.wait()
    entries = pairs_ref.shape[1]
    groups = n_row // 2 * n_col
    group_rows = targets_ref.shape[0] // groups
    lane = lax.broadcasted_iota(jnp.int32, (1, BLOCK), 1)
    for half in range(BLOCK_DEV):
        extra_ref[4 * half : 4 * half + 3, :] = positions_ref[:, half * BLOCK : (half + 1) * BLOCK]
    extra_ref[3:4, :] = jnp.where(lane == LANES - 1, counts_ref[0], 0).astype(f32)
    extra_ref[7:8, :] = jnp.zeros((1, BLOCK), f32)
    extra_ref[3:4, 0:entries] = pairs_ref[0:1, :].astype(f32)
    extra_ref[7:8, 0:entries] = pairs_ref[1:2, :].astype(f32)
    copies[3].wait()
    for group in range(groups):
        if group_rows < ROWS:
            out_ref[group, :, 0:POINTS_DEV] = jnp.zeros((ROWS, POINTS_DEV), f32)
        out_ref[group, 0:group_rows, 0:POINTS_DEV] = targets_ref[group * group_rows : (group + 1) * group_rows, :]
        out_ref[group, :, POINTS_DEV : POINTS_DEV + BLOCK] = extra_ref[...]


def split(value, pieces):
    found = []
    for _ in range(pieces):
        piece = value.astype(bf16).astype(f32)
        found.append(piece)
        value = value - piece
    return found


def point_factors(extra, half):
    row = lax.broadcasted_iota(jnp.int32, (ROWS, BLOCK), 0)
    coords = pltpu.roll(extra, 4, 0) if half else extra
    coords = jnp.where(row < 3, (coords - 0.5) * (1.0 / support_radius), 0.0)
    first, second, third = split(coords, 3)
    norm = jnp.sum(coords * coords, axis=0, keepdims=True)
    norm_pieces = split(jnp.broadcast_to(norm, (ROWS, BLOCK)), 3)
    zero = jnp.zeros((ROWS, BLOCK), f32)
    norms = jnp.where(
        row == 0, norm_pieces[0], jnp.where(row == 1, norm_pieces[1], jnp.where(row == 2, norm_pieces[2], zero))
    )
    ones = jnp.where(row < 3, 1.0, 0.0).astype(f32)
    left = jnp.concatenate([first, first, second, second, first, third, norms, ones], axis=0)
    right = jnp.concatenate(
        [-2.0 * piece for piece in (first, second, first, second, third, first)] + [ones, norms], axis=0
    )
    return left, right


def form_tile(left, right, times):
    square = jnp.maximum(jnp.dot(left, right, preferred_element_type=f32), 1e-30)
    remain = jnp.maximum(1.0 - square * lax.rsqrt(square), 0.0)
    remain_two = remain * remain
    tile = remain_two * remain_two * (1.25 * times - times * remain)
    head = tile.astype(bf16)
    return head, (tile - head.astype(f32)).astype(bf16)


def add_diagonal(vector_ref, total_ref, block, head, tail):
    vector = vector_ref[block]
    total_ref[block] += jnp.dot(vector, head, preferred_element_type=f32) + jnp.dot(
        vector, tail, preferred_element_type=f32
    )


def add_products(vector_ref, total_ref, row_block, col_block, row_to, head, tail):
    over_cols = (((1,), (1,)), ((), ()))
    row_vector, col_vector = vector_ref[row_block], vector_ref[col_block]
    to_cols = jnp.dot(row_vector, head, preferred_element_type=f32) + jnp.dot(
        row_vector, tail, preferred_element_type=f32
    )
    to_rows = lax.dot_general(col_vector, head, over_cols, preferred_element_type=f32) + lax.dot_general(
        col_vector, tail, over_cols, preferred_element_type=f32
    )
    total_ref[col_block] += to_cols
    total_ref[row_to] += to_rows


def store_pieces(vector_ref, block, value, with_ones):
    parts = split(value, 2)
    if with_ones:
        row = lax.broadcasted_iota(jnp.int32, (2 * ROWS, BLOCK), 0)
        parts.append(jnp.where(row == 0, 1.0, 0.0).astype(f32))
    vector_ref[block] = jnp.concatenate(parts, axis=0).astype(bf16)


def global_blocks(n_col, source, group, core):
    row_ids = source[group, 3:4, POINTS_DEV : POINTS_DEV + LANES].astype(jnp.int32)
    col_ids = source[group, 7:8, POINTS_DEV : POINTS_DEV + LANES].astype(jnp.int32)
    count = row_ids[:, LANES - 1 :]
    row, col = 2 * (group // n_col) + core, group % n_col
    in_use = lax.broadcasted_iota(jnp.int32, (1, LANES), 1) < count
    row_block = row * (n_col * BLOCK_DEV) + row_ids
    col_block = ((col_ids >> 1) * n_col + col) * BLOCK_DEV + (col_ids & 1)
    return jnp.minimum(row_block, col_block), jnp.maximum(row_block, col_block), in_use


def merged_list(n_dev, n_col, core, sources, keys_ref, times_ref):
    blocks = n_dev * BLOCK_DEV
    block_id = lax.broadcasted_iota(jnp.int32, (blocks, LANES), 0)
    smaller, larger = [], []
    for source, source_core in sources:
        for group in range(n_dev // 2):
            low, high, in_use = global_blocks(n_col, source, group, source_core)
            smaller.append(jnp.where((block_id == low) & in_use, 1.0, 0.0))
            larger.append(jnp.where((block_id == high) & in_use, 1.0, 0.0))
    over_lanes = (((1,), (1,)), ((), ()))
    times = lax.dot_general(
        jnp.concatenate(larger, axis=1).astype(bf16),
        jnp.concatenate(smaller, axis=1).astype(bf16),
        over_lanes,
        preferred_element_type=f32,
    )
    high_id = lax.broadcasted_iota(jnp.int32, (blocks, blocks), 0)
    low_id = lax.broadcasted_iota(jnp.int32, (blocks, blocks), 1)
    present = jnp.where((times > 0.0) & (high_id > low_id), 1.0, 0.0)
    before = jnp.where(high_id > low_id, 1.0, 0.0).astype(bf16)
    present_low = present.astype(bf16)
    in_column = jnp.dot(before, present_low, preferred_element_type=f32)
    column_sums = jnp.sum(present, axis=0, keepdims=True)
    column_starts = lax.dot_general(
        jnp.broadcast_to(column_sums, (ROWS, blocks)).astype(bf16), before, over_lanes, preferred_element_type=f32
    )[0:1]
    place = (in_column + column_starts).astype(jnp.int32)
    mine = (present > 0.0) & ((place & 1) == core)
    slot = jnp.where(mine, place >> 1, -1)
    key = low_id * blocks + high_id
    lane = lax.broadcasted_iota(jnp.int32, (blocks, LISTED), 1)
    keys = jnp.zeros((blocks, LISTED), jnp.int32)
    counted = jnp.zeros((blocks, LISTED), f32)
    for low in range(blocks):
        here = lane == slot[:, low : low + 1]
        keys = keys + jnp.where(here, key[:, low : low + 1], 0)
        counted = counted + jnp.where(here, times[:, low : low + 1], 0.0)
    held = jnp.sum(jnp.where(mine, 1.0, 0.0), axis=1, keepdims=True)
    held = jnp.sum(held, axis=0, keepdims=True).astype(jnp.int32)
    first_lane = lax.broadcasted_iota(jnp.int32, (1, LISTED), 1)
    keys_ref[...] = jnp.where(
        first_lane == LISTED - 1, held, jnp.sum(keys.astype(f32), axis=0, keepdims=True).astype(jnp.int32)
    )
    times_ref[...] = jnp.sum(counted, axis=0, keepdims=True)


def read_key(list_ref, slot, blocks):
    key = list_ref[0, slot]
    row_block, col_block = lax.div(key, blocks), lax.rem(key, blocks)
    return row_block, col_block, jnp.where(row_block == col_block, blocks, row_block)


def assemble_group(n_col, group, sources, base_ref, vector_ref, left_ref, right_ref):
    for source, source_core in sources:
        device = (2 * (group // n_col) + source_core) * n_col + lax.rem(group, n_col)
        extra = source[group, :, POINTS_DEV : POINTS_DEV + BLOCK]
        for half in range(BLOCK_DEV):
            block = BLOCK_DEV * device + half
            values = source[group, :, half * BLOCK : (half + 1) * BLOCK]
            base_ref[block] = values
            store_pieces(vector_ref, block, values, True)
            left, right = point_factors(extra, half)
            left_ref[block] = left.T.astype(bf16)
            right_ref[block] = right.astype(bf16)


def finish_first(total_ref, partial_ref, blocks):
    for block in range(blocks):
        partial_ref[block] = total_ref[block, 0:ROWS] + total_ref[block, ROWS : 2 * ROWS]
        partial_ref[blocks + block // ROWS, block % ROWS : block % ROWS + 1, :] = total_ref[
            block, 2 * ROWS : 2 * ROWS + 1
        ]


def form_stored_kernel(
    n_row,
    n_col,
    mine_ref,
    other_ref,
    list_ref,
    base_ref,
    partial_ref,
    tiles_ref,
    times_ref,
    keys_vector,
    times_vector,
    list_sems,
    vector_ref,
    total_ref,
    left_ref,
    right_ref,
    sems,
    *place_refs,
):
    n_dev = n_row * n_col
    blocks = n_dev * BLOCK_DEV
    core = lax.rem(lax.axis_index("row"), 2)
    sources = ((mine_ref, core), (other_ref, 1 - core))
    merged_list(n_dev, n_col, core, sources, keys_vector, times_vector)
    keys_copy = pltpu.make_async_copy(keys_vector, list_ref, list_sems.at[0])
    times_copy = pltpu.make_async_copy(times_vector, times_ref, list_sems.at[1])
    keys_copy.start()
    times_copy.start()

    def assemble(group, carry):
        assemble_group(n_col, group, sources, base_ref, vector_ref, left_ref, right_ref)
        return carry

    lax.fori_loop(0, n_dev // 2, assemble, 0)
    total_ref[...] = jnp.zeros_like(total_ref)
    last_place = place_refs[TURN - 1]
    last_place[WRITE_SLOTS - 1] = jnp.zeros(last_place.shape[1:], bf16)
    keys_copy.wait()
    times_copy.wait()
    held = list_ref[0, LISTED - 1]
    diagonal = blocks // 2
    diagonal_turns = diagonal // TURN

    def diagonal_block(slot):
        return 2 * slot + core

    def copies(turn, size=TURN):
        place_slot = lax.rem(turn, WRITE_SLOTS)
        return [
            pltpu.make_async_copy(
                place_refs[place].at[place_slot], tiles_ref.at[turn * TURN + place], sems.at[place_slot, place]
            )
            for place in range(size)
        ]

    def wait_turn(turn, size=TURN):
        for copy in copies(turn, size):
            copy.wait()

    def form(turn, place, row_block, col_block, times):
        head, tail = form_tile(left_ref[row_block], right_ref[col_block], times)
        place_refs[place][lax.rem(turn, WRITE_SLOTS), 0] = head
        place_refs[place][lax.rem(turn, WRITE_SLOTS), 1] = tail

    def kept_tile(turn, place):
        place_slot = lax.rem(turn, WRITE_SLOTS)
        return place_refs[place][place_slot, 0], place_refs[place][place_slot, 1]

    def multiply(turn, place):
        slot = turn * TURN + place
        row_block, col_block, _ = read_key(list_ref, jnp.maximum(slot - diagonal, 0), blocks)
        on_diagonal = slot < diagonal
        row_block = jnp.where(on_diagonal, diagonal_block(slot), row_block)
        col_block = jnp.where(on_diagonal, diagonal_block(slot), col_block)
        row_to = jnp.where(on_diagonal, blocks, row_block)
        add_products(vector_ref, total_ref, row_block, col_block, row_to, *kept_tile(turn, place))

    def run_diagonal(turn, carry):
        pl.when(turn >= WRITE_SLOTS)(lambda: wait_turn(turn - WRITE_SLOTS))
        for place in range(TURN):
            slot = turn * TURN + place
            form(turn, place, diagonal_block(slot), diagonal_block(slot), 1.0)
            before = (turn, place - 1) if place else (turn + 1, TURN - 1)
            add_diagonal(vector_ref, total_ref, diagonal_block(jnp.maximum(slot - 1, 0)), *kept_tile(*before))
        for copy in copies(turn):
            copy.start()
        return carry

    def run_turn(turn, size):
        wait_turn(turn - WRITE_SLOTS)
        for place in range(size):
            entry = turn * TURN + place - diagonal
            row_block, col_block, _ = read_key(list_ref, entry, blocks)
            form(turn, place, row_block, col_block, times_ref[0, entry])
            multiply(*((turn, place - 1) if place else (turn - 1, TURN - 1)))
        for copy in copies(turn, size):
            copy.start()

    def run_full(turn, carry):
        run_turn(turn, TURN)
        return carry

    turns = diagonal_turns + (held + TURN - HALF - 1) // TURN
    with_half = held > (turns - diagonal_turns) * TURN
    lax.fori_loop(0, diagonal_turns, run_diagonal, 0)
    lax.fori_loop(diagonal_turns, turns, run_full, 0)

    @pl.when(with_half)
    def _():
        run_turn(turns, HALF)
        multiply(turns, HALF - 1)
        wait_turn(turns, HALF)

    @pl.when(jnp.logical_not(with_half))
    def _():
        multiply(turns - 1, TURN - 1)
        wait_turn(turns - 2)

    finish_first(total_ref, partial_ref, blocks)
    wait_turn(turns - 1)


def form_kernel(
    n_row, n_col, mine_ref, other_ref, list_ref, base_ref, partial_ref, left_ref, right_ref, meta_ref, meta_sems, vector_ref, total_ref
):
    n_dev = n_row * n_col
    blocks = n_dev * BLOCK_DEV
    core = lax.rem(lax.axis_index("row"), 2)
    sources = ((mine_ref, core), (other_ref, 1 - core))
    meta_copies = [
        pltpu.make_async_copy(
            source.at[:, :, POINTS_DEV : POINTS_DEV + LANES], meta_ref.at[source_core], meta_sems.at[index]
        )
        for index, (source, source_core) in enumerate(sources)
    ]
    for copy in meta_copies:
        copy.start()

    def assemble(group, carry):
        assemble_group(n_col, group, sources, base_ref, vector_ref, left_ref, right_ref)
        return carry

    lax.fori_loop(0, n_dev // 2, assemble, 0)
    total_ref[...] = jnp.zeros_like(total_ref)
    for copy in meta_copies:
        copy.wait()

    def read_device(device, carry):
        seen, held = carry
        row = device // n_col
        col = lax.rem(device, n_col)
        source_core, group = lax.rem(row, 2), (row // 2) * n_col + col
        count = meta_ref[source_core, group, 3, LANES - 1].astype(jnp.int32)
        first = lax.rem(seen + core, 2)
        taken = (count - first + 1) // 2

        def read_entry(index, carry):
            slot = first + 2 * index
            row_id = meta_ref[source_core, group, 3, slot].astype(jnp.int32)
            col_id = meta_ref[source_core, group, 7, slot].astype(jnp.int32)
            row_block = row * (n_col * BLOCK_DEV) + row_id
            col_block = ((col_id // BLOCK_DEV) * n_col + col) * BLOCK_DEV + lax.rem(col_id, BLOCK_DEV)
            list_ref[0, held + index] = row_block * blocks + col_block
            return carry

        lax.fori_loop(0, taken, read_entry, 0)
        return seen + count, held + taken

    _, held = lax.fori_loop(0, n_dev, read_device, (0, 0))
    list_ref[0, list_ref.shape[1] - 1] = held
    apply_formed(list_ref, (left_ref, right_ref), vector_ref, total_ref, blocks)
    finish_first(total_ref, partial_ref, blocks)


def apply_formed(list_ref, factor_refs, vector_ref, total_ref, blocks):
    def run_entry(entry, carry):
        row_block, col_block, row_to = read_key(list_ref, entry, blocks)
        head, tail = form_tile(factor_refs[0][row_block], factor_refs[1][col_block], 1.0)
        add_products(vector_ref, total_ref, row_block, col_block, row_to, head, tail)
        return carry

    lax.fori_loop(0, list_ref[0, list_ref.shape[1] - 1], run_entry, 0)


def read_copy(part, tiles_ref, buffer_ref, sems):
    span = pl.ds(part * HALF, HALF)
    return pltpu.make_async_copy(tiles_ref.at[span], buffer_ref.at[span], sems.at[part])


def start_reads(list_ref, tiles_ref, buffer_ref, sems, blocks):
    def start(part, carry):
        read_copy(part, tiles_ref, buffer_ref, sems).start()
        return carry

    diagonal = blocks // 2
    lax.fori_loop(diagonal // HALF, (diagonal + list_ref[0, LISTED - 1] + HALF - 1) // HALF, start, 0)
    lax.fori_loop(0, diagonal // HALF, start, 0)


def apply_stored(list_ref, tiles_ref, buffer_ref, sems, vector_ref, total_ref, blocks):
    held = list_ref[0, LISTED - 1]
    core = lax.rem(lax.axis_index("row"), 2)
    diagonal = blocks // 2

    def wait_tiles(slot, count):
        for part in range(count // HALF):
            read_copy(slot // HALF + part, tiles_ref, buffer_ref, sems).wait()

    def run_entries(first, count):
        wait_tiles(diagonal + first, count)
        for place in range(count):
            row_block, col_block, _ = read_key(list_ref, first + place, blocks)
            slot = diagonal + first + place
            head, tail = buffer_ref[slot, 0], buffer_ref[slot, 1]
            add_products(vector_ref, total_ref, row_block, col_block, row_block, head, tail)

    def run_pair(pair, carry):
        run_entries(pair * 2 * TURN, 2 * TURN)
        return carry

    def run_diagonal(turn, carry):
        wait_tiles(turn * TURN, TURN)
        for place in range(TURN):
            slot = turn * TURN + place
            add_diagonal(vector_ref, total_ref, 2 * slot + core, buffer_ref[slot, 0], buffer_ref[slot, 1])
        return carry

    pairs = (held + HALF - 1) // (2 * TURN)
    lax.fori_loop(0, pairs, run_pair, 0)
    first = pairs * 2 * TURN
    parts = (jnp.maximum(held - first, 0) + HALF - 1) // HALF
    pl.when(parts >= 2)(lambda: run_entries(first, TURN))
    pl.when(lax.rem(parts, 2) == 1)(lambda: run_entries(first + (parts - 1) * HALF, HALF))
    lax.fori_loop(0, diagonal // TURN, run_diagonal, 0)


def apply_tiles(stored, value_ref, list_ref, held_refs, partial_ref, scratch):
    blocks = value_ref.shape[0]
    vector_ref, total_ref = scratch[:2]

    def put_block(block, carry):
        store_pieces(vector_ref, block, value_ref[block], False)
        return carry

    lax.fori_loop(0, blocks, put_block, 0, unroll=8)
    total_ref[...] = jnp.zeros_like(total_ref)
    if stored:
        apply_stored(list_ref, held_refs[0], scratch[2], scratch[3], vector_ref, total_ref, blocks)
    else:
        apply_formed(list_ref, held_refs, vector_ref, total_ref, blocks)
    partial_ref[...] = total_ref[0:blocks, 0:ROWS] + total_ref[0:blocks, ROWS : 2 * ROWS]


def row_sum(value):
    return jnp.sum(jnp.sum(value, axis=0, keepdims=True), axis=2, keepdims=True)


def first_step_kernel(stored, list_ref, mine_ref, other_ref, base_ref, *rest):
    count = 1 if stored else 2
    held, rest = rest[:count], rest[count:]
    residual_ref, direction_ref, partial_ref, scalars_ref, *scratch = rest
    if stored:
        start_reads(list_ref, held[0], scratch[2], scratch[3], base_ref.shape[0])
    blocks = base_ref.shape[0]
    largest = jnp.max(mine_ref[blocks:] + other_ref[blocks:])
    base = base_ref[...]
    applied = ridge_shift * base + (mine_ref[0:blocks] + other_ref[0:blocks]) / largest
    norm_now = row_sum(base * base)
    step_size = norm_now / row_sum(base * applied)
    residual = base - step_size * applied
    norm_next = row_sum(residual * residual)
    direction = residual + (norm_next / norm_now) * base
    residual_ref[...] = residual
    direction_ref[...] = direction
    scalars_ref[0] = jnp.broadcast_to(step_size[0], (ROWS, LANES))
    scalars_ref[1] = jnp.broadcast_to(norm_next[0], (ROWS, LANES))
    scalars_ref[2] = jnp.full((ROWS, LANES), largest, f32)
    apply_tiles(stored, direction_ref, list_ref, held, partial_ref, scratch)


def next_step_kernel(
    stored, list_ref, mine_ref, other_ref, base_ref, residual_ref, direction_ref, scalars_ref, *rest
):
    count = 1 if stored else 2
    held, rest = rest[:count], rest[count:]
    weights_out, residual_out, direction_out, partial_ref, scalars_out, *scratch = rest
    if stored:
        start_reads(list_ref, held[0], scratch[2], scratch[3], base_ref.shape[0])
    step_before = scalars_ref[0:1, :, 0:1]
    norm_now = scalars_ref[1:2, :, 0:1]
    largest = scalars_ref[2:3, :, 0:1]
    direction = direction_ref[...]
    applied = ridge_shift * direction + (mine_ref[...] + other_ref[...]) / largest
    step_size = norm_now / row_sum(direction * applied)
    weights_out[...] = step_before * base_ref[...] + step_size * direction
    residual = residual_ref[...] - step_size * applied
    norm_next = row_sum(residual * residual)
    residual_out[...] = residual
    direction_out[...] = residual + (norm_next / norm_now) * direction
    scalars_out[0] = scalars_ref[0]
    scalars_out[1] = jnp.broadcast_to(norm_next[0], (ROWS, LANES))
    scalars_out[2] = scalars_ref[2]
    apply_tiles(stored, direction_out, list_ref, held, partial_ref, scratch)


def last_step_kernel(
    n_row, n_col, mine_ref, other_ref, weights_ref, residual_ref, direction_ref, scalars_ref, out_ref
):
    norm_now = scalars_ref[1:2, :, 0:1]
    largest = scalars_ref[2:3, :, 0:1]
    direction = direction_ref[...]
    applied = ridge_shift * direction + (mine_ref[...] + other_ref[...]) / largest
    step_size = norm_now / row_sum(direction * applied)
    core = lax.rem(lax.axis_index("row"), 2)
    row_blocks = n_col * BLOCK_DEV
    for pair in range(n_row // 2):
        span = pl.ds((2 * pair + core) * row_blocks, row_blocks)
        direction = direction_ref[span]
        applied = ridge_shift * direction + (mine_ref[span] + other_ref[span]) / largest
        weights = weights_ref[span] + step_size * direction
        residual = residual_ref[span] - step_size * applied
        for col in range(n_col):
            start = (pair * n_col + col) * 2 * BLOCK_DEV
            taken = slice(col * BLOCK_DEV, (col + 1) * BLOCK_DEV)
            out_ref[start : start + BLOCK_DEV] = weights[taken]
            out_ref[start + BLOCK_DEV : start + 2 * BLOCK_DEV] = residual[taken]


def unpack_kernel(groups, group_rows, received_ref, weights_ref, residual_ref):
    for group in range(groups):
        rows = slice(group * group_rows, (group + 1) * group_rows)
        for index, target in enumerate((weights_ref, residual_ref)):
            for half in range(BLOCK_DEV):
                target[rows, half * BLOCK : (half + 1) * BLOCK] = received_ref[
                    (2 * group + index) * BLOCK_DEV + half, 0:group_rows
                ]


def call(kernel, out_shape, *args, scratch=(), in_spaces=None, out_spaces=None, vmem=16):
    spaces = in_spaces or [pltpu.VMEM] * len(args)
    outs = out_spaces or jax.tree.map(lambda _: pltpu.VMEM, out_shape)
    return pl.pallas_call(
        kernel,
        out_shape=out_shape,
        in_specs=[pl.BlockSpec(memory_space=space) for space in spaces],
        out_specs=jax.tree.map(lambda space: pl.BlockSpec(memory_space=space), outs),
        scratch_shapes=list(scratch),
        compiler_params=pltpu.CompilerParams(vmem_limit_bytes=vmem * 2**20),
    )(*args)


def local(positions, targets, pairs, counts):
    n_row = lax.axis_size("row")
    n_col = lax.axis_size("col")
    n_dev = n_row * n_col
    blocks = n_dev * BLOCK_DEV
    entries = pairs.shape[1]
    groups = n_dev // 2
    group_rows = targets.shape[0] // groups
    room = -(-(n_dev * entries // 2) // TURN) * TURN
    stored = room <= STORED_MAX and blocks % (2 * TURN) == 0
    same_core = [
        [row * n_col + col for row in range(core, n_row, 2) for col in range(n_col)] for core in range(2)
    ]
    siblings = [(index, index ^ 1) for index in range(n_row)]
    shape = jax.ShapeDtypeStruct
    kept = pltpu.VMEM if stored else shape
    vmem = 52 if stored else 58
    field = kept((blocks, ROWS, BLOCK), f32)
    scalars = kept((3, ROWS, LANES), f32)

    def resident(array):
        return pltpu.with_memory_space_constraint(array, pltpu.VMEM) if stored else array

    def from_sibling(array):
        return resident(lax.ppermute(array, "row", siblings))

    def among_cores(array):
        return resident(
            lax.all_to_all(array, ("row", "col"), 0, 0, axis_index_groups=same_core, tiled=True)
        )

    packed = call(
        functools.partial(pack_kernel, n_row, n_col),
        kept((groups, ROWS, POINTS_DEV + BLOCK), f32),
        targets,
        positions,
        pairs,
        counts,
        in_spaces=[pl.ANY] * 4,
        scratch=[
            pltpu.VMEM(targets.shape, f32),
            pltpu.VMEM(positions.shape, f32),
            pltpu.VMEM(pairs.shape, jnp.int32),
            pltpu.SMEM(counts.shape, jnp.int32),
            pltpu.VMEM((ROWS, BLOCK), f32),
            pltpu.SemaphoreType.DMA((4,)),
        ],
        vmem=60,
    )
    mine = among_cores(resident(packed))
    other = from_sibling(mine)

    factors = [((blocks, BLOCK, PIECE_DEPTH), bf16), ((blocks, PIECE_DEPTH, BLOCK), bf16)]
    factor_scratch = [pltpu.VMEM(*factor) for factor in factors]
    first_partial = kept((blocks + -(-blocks // ROWS), ROWS, BLOCK), f32)
    first_scratch = [
        pltpu.VMEM((blocks, 4 * ROWS, BLOCK), bf16),
        pltpu.VMEM((blocks + 1, 4 * ROWS, BLOCK), f32),
    ]
    step_scratch = [
        pltpu.VMEM((blocks, 2 * ROWS, BLOCK), bf16),
        pltpu.VMEM((blocks + 1, 2 * ROWS, BLOCK), f32),
    ]
    if stored:
        listed, base, partial, *held = call(
            functools.partial(form_stored_kernel, n_row, n_col),
            [shape((1, LISTED), jnp.int32), field, first_partial, shape((room, 2, BLOCK, BLOCK), bf16)],
            mine,
            other,
            out_spaces=[pltpu.SMEM, pltpu.VMEM, pltpu.VMEM, pl.ANY],
            scratch=[
                pltpu.SMEM((1, LISTED), f32),
                pltpu.VMEM((1, LISTED), jnp.int32),
                pltpu.VMEM((1, LISTED), f32),
                pltpu.SemaphoreType.DMA((2,)),
                *first_scratch,
                *factor_scratch,
                pltpu.SemaphoreType.DMA((WRITE_SLOTS, TURN)),
                *[pltpu.VMEM((WRITE_SLOTS, 2, BLOCK, BLOCK), bf16)] * TURN,
            ],
            vmem=vmem,
        )
        held_spaces = [pl.ANY]
        step_scratch += [
            pltpu.VMEM((room, 2, BLOCK, BLOCK), bf16),
            pltpu.SemaphoreType.DMA((room // HALF,)),
        ]
    else:
        listed, base, partial, *held = call(
            functools.partial(form_kernel, n_row, n_col),
            [shape((1, room + 1), jnp.int32), field, first_partial, *(shape(*factor) for factor in factors)],
            mine,
            other,
            out_spaces=[pltpu.SMEM] + [pltpu.VMEM] * 4,
            scratch=[
                pltpu.SMEM((2, n_dev // 2, ROWS, LANES), f32),
                pltpu.SemaphoreType.DMA((2,)),
                *first_scratch,
            ],
            vmem=vmem,
        )
        held_spaces = [pltpu.VMEM] * 2
    base, partial = resident(base), resident(partial)

    def step(kernel, out_shape, *args):
        outs = call(
            functools.partial(kernel, stored),
            out_shape,
            listed,
            *args,
            *held,
            in_spaces=[pltpu.SMEM] + [pltpu.VMEM] * len(args) + held_spaces,
            scratch=step_scratch,
            vmem=vmem,
        )
        return [resident(out) for out in outs]

    residual, direction, partial, numbers = step(
        first_step_kernel, (field, field, field, scalars), partial, from_sibling(partial), base
    )
    weights, residual, direction, partial, numbers = step(
        next_step_kernel,
        (field, field, field, field, scalars),
        partial,
        from_sibling(partial),
        base,
        residual,
        direction,
        numbers,
    )
    result = call(
        functools.partial(last_step_kernel, n_row, n_col),
        field,
        partial,
        from_sibling(partial),
        weights,
        residual,
        direction,
        numbers,
    )
    home = among_cores(resident(result))
    out = shape(targets.shape, f32)
    return call(functools.partial(unpack_kernel, groups, group_rows), (out, out), home)


def solution(mesh):
    placed = (
        P(None, ("groups", "row", "col")),
        P(None, ("groups", "row", "col")),
        P(None, ("groups", "row", "col")),
        P(("groups", "row", "col")),
    )
    return jax.shard_map(
        local,
        mesh=mesh,
        in_specs=placed,
        out_specs=(P(None, ("groups", "row", "col")), P(None, ("groups", "row", "col"))),
        check_vma=False,
    )
```

```python
import functools

import jax
import jax.numpy as jnp
from jax import lax
from jax.experimental import pallas as pl
from jax.experimental.pallas import tpu as pltpu
from jax.sharding import PartitionSpec as P

BLOCK = 256
BLOCK_DEV = 2
LANES = 128
POINTS_DEV = BLOCK * BLOCK_DEV
ROWS = 8
PIECE_DEPTH = 64
TURN = 8
HALF = TURN // 2
STORED_MAX = 192
LISTED = 256
WRITE_SLOTS = 2

support_radius = 0.5
ridge_shift = 1.5
f32 = jnp.float32
bf16 = jnp.bfloat16


def pack_kernel(
    n_row, n_col, targets_in, positions_in, pairs_in, counts_in, out_ref, targets_ref, positions_ref, pairs_ref, counts_ref, extra_ref, sems
):
    copies = [
        pltpu.make_async_copy(source, kept, sems.at[index])
        for index, (source, kept) in enumerate(
            (
                (positions_in, positions_ref),
                (pairs_in, pairs_ref),
                (counts_in, counts_ref),
                (targets_in, targets_ref),
            )
        )
    ]
    for copy in copies:
        copy.start()
    for copy in copies[:3]:
        copy.wait()
    entries = pairs_ref.shape[1]
    groups = n_row // 2 * n_col
    group_rows = targets_ref.shape[0] // groups
    lane = lax.broadcasted_iota(jnp.int32, (1, BLOCK), 1)
    for half in range(BLOCK_DEV):
        extra_ref[4 * half : 4 * half + 3, :] = positions_ref[:, half * BLOCK : (half + 1) * BLOCK]
    extra_ref[3:4, :] = jnp.where(lane == LANES - 1, counts_ref[0], 0).astype(f32)
    extra_ref[7:8, :] = jnp.zeros((1, BLOCK), f32)
    extra_ref[3:4, 0:entries] = pairs_ref[0:1, :].astype(f32)
    extra_ref[7:8, 0:entries] = pairs_ref[1:2, :].astype(f32)
    copies[3].wait()
    for group in range(groups):
        if group_rows < ROWS:
            out_ref[group, :, 0:POINTS_DEV] = jnp.zeros((ROWS, POINTS_DEV), f32)
        out_ref[group, 0:group_rows, 0:POINTS_DEV] = targets_ref[group * group_rows : (group + 1) * group_rows, :]
        out_ref[group, :, POINTS_DEV : POINTS_DEV + BLOCK] = extra_ref[...]


def split(value, pieces):
    found = []
    for _ in range(pieces):
        piece = value.astype(bf16).astype(f32)
        found.append(piece)
        value = value - piece
    return found


def point_factors(extra, half):
    row = lax.broadcasted_iota(jnp.int32, (ROWS, BLOCK), 0)
    coords = pltpu.roll(extra, 4, 0) if half else extra
    coords = jnp.where(row < 3, (coords - 0.5) * (1.0 / support_radius), 0.0)
    first, second, third = split(coords, 3)
    norm = jnp.sum(coords * coords, axis=0, keepdims=True)
    norm_pieces = split(jnp.broadcast_to(norm, (ROWS, BLOCK)), 3)
    zero = jnp.zeros((ROWS, BLOCK), f32)
    norms = jnp.where(
        row == 0, norm_pieces[0], jnp.where(row == 1, norm_pieces[1], jnp.where(row == 2, norm_pieces[2], zero))
    )
    ones = jnp.where(row < 3, 1.0, 0.0).astype(f32)
    left = jnp.concatenate([first, first, second, second, first, third, norms, ones], axis=0)
    right = jnp.concatenate(
        [-2.0 * piece for piece in (first, second, first, second, third, first)] + [ones, norms], axis=0
    )
    return left, right


def form_tile(left, right, times):
    square = jnp.maximum(jnp.dot(left, right, preferred_element_type=f32), 1e-30)
    remain = jnp.maximum(1.0 - square * lax.rsqrt(square), 0.0)
    remain_two = remain * remain
    tile = remain_two * remain_two * (1.25 * times - times * remain)
    head = tile.astype(bf16)
    return head, (tile - head.astype(f32)).astype(bf16)


def add_diagonal(vector_ref, total_ref, block, head, tail):
    vector = vector_ref[block]
    total_ref[block] += jnp.dot(vector, head, preferred_element_type=f32) + jnp.dot(
        vector, tail, preferred_element_type=f32
    )


def add_products(vector_ref, total_ref, row_block, col_block, row_to, head, tail):
    over_cols = (((1,), (1,)), ((), ()))
    row_vector, col_vector = vector_ref[row_block], vector_ref[col_block]
    to_cols = jnp.dot(row_vector, head, preferred_element_type=f32) + jnp.dot(
        row_vector, tail, preferred_element_type=f32
    )
    to_rows = lax.dot_general(col_vector, head, over_cols, preferred_element_type=f32) + lax.dot_general(
        col_vector, tail, over_cols, preferred_element_type=f32
    )
    total_ref[col_block] += to_cols
    total_ref[row_to] += to_rows


def add_mixed_products(vector_ref, total_ref, side_ref, row_block, col_block, head, tail):
    over_cols = (((1,), (1,)), ((), ()))
    row_vector, col_vector = vector_ref[row_block], vector_ref[col_block]
    total_ref[col_block] += jnp.dot(row_vector, head, preferred_element_type=f32) + jnp.dot(
        row_vector, tail, preferred_element_type=f32
    )
    total_ref[row_block] += lax.dot_general(col_vector, head, over_cols, preferred_element_type=f32)
    side_ref[row_block] += lax.dot_general(tail, col_vector, over_cols, preferred_element_type=f32)


def store_pieces(vector_ref, block, value, with_ones):
    parts = split(value, 2)
    if with_ones:
        row = lax.broadcasted_iota(jnp.int32, (2 * ROWS, BLOCK), 0)
        parts.append(jnp.where(row == 0, 1.0, 0.0).astype(f32))
    vector_ref[block] = jnp.concatenate(parts, axis=0).astype(bf16)


def global_blocks(n_col, source, group, core):
    row_ids = source[group, 3:4, POINTS_DEV : POINTS_DEV + LANES].astype(jnp.int32)
    col_ids = source[group, 7:8, POINTS_DEV : POINTS_DEV + LANES].astype(jnp.int32)
    count = row_ids[:, LANES - 1 :]
    row, col = 2 * (group // n_col) + core, group % n_col
    in_use = lax.broadcasted_iota(jnp.int32, (1, LANES), 1) < count
    row_block = row * (n_col * BLOCK_DEV) + row_ids
    col_block = ((col_ids >> 1) * n_col + col) * BLOCK_DEV + (col_ids & 1)
    return jnp.minimum(row_block, col_block), jnp.maximum(row_block, col_block), in_use


def merged_list(n_dev, n_col, core, sources, keys_ref, times_ref):
    blocks = n_dev * BLOCK_DEV
    block_id = lax.broadcasted_iota(jnp.int32, (blocks, LANES), 0)
    smaller, larger = [], []
    for source, source_core in sources:
        for group in range(n_dev // 2):
            low, high, in_use = global_blocks(n_col, source, group, source_core)
            smaller.append(jnp.where((block_id == low) & in_use, 1.0, 0.0))
            larger.append(jnp.where((block_id == high) & in_use, 1.0, 0.0))
    over_lanes = (((1,), (1,)), ((), ()))
    times = lax.dot_general(
        jnp.concatenate(larger, axis=1).astype(bf16),
        jnp.concatenate(smaller, axis=1).astype(bf16),
        over_lanes,
        preferred_element_type=f32,
    )
    high_id = lax.broadcasted_iota(jnp.int32, (blocks, blocks), 0)
    low_id = lax.broadcasted_iota(jnp.int32, (blocks, blocks), 1)
    present = jnp.where((times > 0.0) & (high_id > low_id), 1.0, 0.0)
    before = jnp.where(high_id > low_id, 1.0, 0.0).astype(bf16)
    present_low = present.astype(bf16)
    in_column = jnp.dot(before, present_low, preferred_element_type=f32)
    column_sums = jnp.sum(present, axis=0, keepdims=True)
    column_starts = lax.dot_general(
        jnp.broadcast_to(column_sums, (ROWS, blocks)).astype(bf16), before, over_lanes, preferred_element_type=f32
    )[0:1]
    place = (in_column + column_starts).astype(jnp.int32)
    mine = (present > 0.0) & ((place & 1) == core)
    slot = jnp.where(mine, place >> 1, -1)
    key = low_id * blocks + high_id
    lane = lax.broadcasted_iota(jnp.int32, (blocks, LISTED), 1)
    keys = jnp.zeros((blocks, LISTED), jnp.int32)
    counted = jnp.zeros((blocks, LISTED), f32)
    for low in range(blocks):
        here = lane == slot[:, low : low + 1]
        keys = keys + jnp.where(here, key[:, low : low + 1], 0)
        counted = counted + jnp.where(here, times[:, low : low + 1], 0.0)
    held = jnp.sum(jnp.where(mine, 1.0, 0.0), axis=1, keepdims=True)
    held = jnp.sum(held, axis=0, keepdims=True).astype(jnp.int32)
    first_lane = lax.broadcasted_iota(jnp.int32, (1, LISTED), 1)
    keys_ref[...] = jnp.where(
        first_lane == LISTED - 1, held, jnp.sum(keys.astype(f32), axis=0, keepdims=True).astype(jnp.int32)
    )
    times_ref[...] = jnp.sum(counted, axis=0, keepdims=True)


def read_key(list_ref, slot, blocks):
    key = list_ref[0, slot]
    row_block, col_block = lax.div(key, blocks), lax.rem(key, blocks)
    return row_block, col_block, jnp.where(row_block == col_block, blocks, row_block)


def assemble_group(n_col, group, sources, base_ref, vector_ref, left_ref, right_ref):
    for source, source_core in sources:
        device = (2 * (group // n_col) + source_core) * n_col + lax.rem(group, n_col)
        extra = source[group, :, POINTS_DEV : POINTS_DEV + BLOCK]
        for half in range(BLOCK_DEV):
            block = BLOCK_DEV * device + half
            values = source[group, :, half * BLOCK : (half + 1) * BLOCK]
            base_ref[block] = values
            store_pieces(vector_ref, block, values, True)
            left, right = point_factors(extra, half)
            left_ref[block] = left.T.astype(bf16)
            right_ref[block] = right.astype(bf16)


def finish_first(total_ref, partial_ref, blocks):
    for block in range(blocks):
        partial_ref[block] = total_ref[block, 0:ROWS] + total_ref[block, ROWS : 2 * ROWS]
        partial_ref[blocks + block // ROWS, block % ROWS : block % ROWS + 1, :] = total_ref[
            block, 2 * ROWS : 2 * ROWS + 1
        ]


def form_stored_kernel(
    n_row,
    n_col,
    mine_ref,
    other_ref,
    list_ref,
    base_ref,
    partial_ref,
    tiles_ref,
    times_ref,
    keys_vector,
    times_vector,
    list_sems,
    vector_ref,
    total_ref,
    left_ref,
    right_ref,
    sems,
    *place_refs,
):
    n_dev = n_row * n_col
    blocks = n_dev * BLOCK_DEV
    core = lax.rem(lax.axis_index("row"), 2)
    sources = ((mine_ref, core), (other_ref, 1 - core))
    merged_list(n_dev, n_col, core, sources, keys_vector, times_vector)
    keys_copy = pltpu.make_async_copy(keys_vector, list_ref, list_sems.at[0])
    times_copy = pltpu.make_async_copy(times_vector, times_ref, list_sems.at[1])
    keys_copy.start()
    times_copy.start()

    def assemble(group, carry):
        assemble_group(n_col, group, sources, base_ref, vector_ref, left_ref, right_ref)
        return carry

    lax.fori_loop(0, n_dev // 2, assemble, 0)
    total_ref[...] = jnp.zeros_like(total_ref)
    last_place = place_refs[TURN - 1]
    last_place[WRITE_SLOTS - 1] = jnp.zeros(last_place.shape[1:], bf16)
    keys_copy.wait()
    times_copy.wait()
    held = list_ref[0, LISTED - 1]
    diagonal = blocks // 2
    diagonal_turns = diagonal // TURN

    def diagonal_block(slot):
        return 2 * slot + core

    def copies(turn, size=TURN):
        place_slot = lax.rem(turn, WRITE_SLOTS)
        return [
            pltpu.make_async_copy(
                place_refs[place].at[place_slot], tiles_ref.at[turn * TURN + place], sems.at[place_slot, place]
            )
            for place in range(size)
        ]

    def wait_turn(turn, size=TURN):
        for copy in copies(turn, size):
            copy.wait()

    def form(turn, place, row_block, col_block, times):
        head, tail = form_tile(left_ref[row_block], right_ref[col_block], times)
        place_refs[place][lax.rem(turn, WRITE_SLOTS), 0] = head
        place_refs[place][lax.rem(turn, WRITE_SLOTS), 1] = tail

    def kept_tile(turn, place):
        place_slot = lax.rem(turn, WRITE_SLOTS)
        return place_refs[place][place_slot, 0], place_refs[place][place_slot, 1]

    def multiply(turn, place):
        slot = turn * TURN + place
        row_block, col_block, _ = read_key(list_ref, jnp.maximum(slot - diagonal, 0), blocks)
        on_diagonal = slot < diagonal
        row_block = jnp.where(on_diagonal, diagonal_block(slot), row_block)
        col_block = jnp.where(on_diagonal, diagonal_block(slot), col_block)
        row_to = jnp.where(on_diagonal, blocks, row_block)
        add_products(vector_ref, total_ref, row_block, col_block, row_to, *kept_tile(turn, place))

    def run_diagonal(turn, carry):
        pl.when(turn >= WRITE_SLOTS)(lambda: wait_turn(turn - WRITE_SLOTS))
        for place in range(TURN):
            slot = turn * TURN + place
            form(turn, place, diagonal_block(slot), diagonal_block(slot), 1.0)
            before = (turn, place - 1) if place else (turn + 1, TURN - 1)
            add_diagonal(vector_ref, total_ref, diagonal_block(jnp.maximum(slot - 1, 0)), *kept_tile(*before))
        for copy in copies(turn):
            copy.start()
        return carry

    def run_turn(turn, size):
        wait_turn(turn - WRITE_SLOTS)
        for place in range(size):
            entry = turn * TURN + place - diagonal
            row_block, col_block, _ = read_key(list_ref, entry, blocks)
            form(turn, place, row_block, col_block, times_ref[0, entry])
            multiply(*((turn, place - 1) if place else (turn - 1, TURN - 1)))
        for copy in copies(turn, size):
            copy.start()

    def run_full(turn, carry):
        run_turn(turn, TURN)
        return carry

    turns = diagonal_turns + (held + TURN - HALF - 1) // TURN
    with_half = held > (turns - diagonal_turns) * TURN
    lax.fori_loop(0, diagonal_turns, run_diagonal, 0)
    lax.fori_loop(diagonal_turns, turns, run_full, 0)

    @pl.when(with_half)
    def _():
        run_turn(turns, HALF)
        multiply(turns, HALF - 1)
        wait_turn(turns, HALF)

    @pl.when(jnp.logical_not(with_half))
    def _():
        multiply(turns - 1, TURN - 1)
        wait_turn(turns - 2)

    finish_first(total_ref, partial_ref, blocks)
    wait_turn(turns - 1)


def form_kernel(
    n_row, n_col, mine_ref, other_ref, list_ref, base_ref, partial_ref, left_ref, right_ref, meta_ref, meta_sems, vector_ref, total_ref
):
    n_dev = n_row * n_col
    blocks = n_dev * BLOCK_DEV
    core = lax.rem(lax.axis_index("row"), 2)
    sources = ((mine_ref, core), (other_ref, 1 - core))
    meta_copies = [
        pltpu.make_async_copy(
            source.at[:, :, POINTS_DEV : POINTS_DEV + LANES], meta_ref.at[source_core], meta_sems.at[index]
        )
        for index, (source, source_core) in enumerate(sources)
    ]
    for copy in meta_copies:
        copy.start()

    def assemble(group, carry):
        assemble_group(n_col, group, sources, base_ref, vector_ref, left_ref, right_ref)
        return carry

    lax.fori_loop(0, n_dev // 2, assemble, 0)
    total_ref[...] = jnp.zeros_like(total_ref)
    for copy in meta_copies:
        copy.wait()

    def read_device(device, carry):
        seen, held = carry
        row = device // n_col
        col = lax.rem(device, n_col)
        source_core, group = lax.rem(row, 2), (row // 2) * n_col + col
        count = meta_ref[source_core, group, 3, LANES - 1].astype(jnp.int32)
        first = lax.rem(seen + core, 2)
        taken = (count - first + 1) // 2

        def read_entry(index, carry):
            slot = first + 2 * index
            row_id = meta_ref[source_core, group, 3, slot].astype(jnp.int32)
            col_id = meta_ref[source_core, group, 7, slot].astype(jnp.int32)
            row_block = row * (n_col * BLOCK_DEV) + row_id
            col_block = ((col_id // BLOCK_DEV) * n_col + col) * BLOCK_DEV + lax.rem(col_id, BLOCK_DEV)
            list_ref[0, held + index] = row_block * blocks + col_block
            return carry

        lax.fori_loop(0, taken, read_entry, 0)
        return seen + count, held + taken

    _, held = lax.fori_loop(0, n_dev, read_device, (0, 0))
    list_ref[0, list_ref.shape[1] - 1] = held
    apply_formed(list_ref, (left_ref, right_ref), vector_ref, total_ref, blocks)
    finish_first(total_ref, partial_ref, blocks)


def apply_formed(list_ref, factor_refs, vector_ref, total_ref, blocks):
    def run_entry(entry, carry):
        row_block, col_block, row_to = read_key(list_ref, entry, blocks)
        head, tail = form_tile(factor_refs[0][row_block], factor_refs[1][col_block], 1.0)
        add_products(vector_ref, total_ref, row_block, col_block, row_to, head, tail)
        return carry

    lax.fori_loop(0, list_ref[0, list_ref.shape[1] - 1], run_entry, 0)


def read_copy(part, tiles_ref, buffer_ref, sems):
    span = pl.ds(part * HALF, HALF)
    return pltpu.make_async_copy(tiles_ref.at[span], buffer_ref.at[span], sems.at[part])


def start_reads(list_ref, tiles_ref, buffer_ref, sems, blocks):
    def start(part, carry):
        read_copy(part, tiles_ref, buffer_ref, sems).start()
        return carry

    diagonal = blocks // 2
    lax.fori_loop(diagonal // HALF, (diagonal + list_ref[0, LISTED - 1] + HALF - 1) // HALF, start, 0)
    lax.fori_loop(0, diagonal // HALF, start, 0)


def apply_stored(list_ref, tiles_ref, buffer_ref, sems, side_ref, vector_ref, total_ref, blocks):
    held = list_ref[0, LISTED - 1]
    core = lax.rem(lax.axis_index("row"), 2)
    diagonal = blocks // 2

    def wait_tiles(slot, count):
        for part in range(count // HALF):
            read_copy(slot // HALF + part, tiles_ref, buffer_ref, sems).wait()

    def run_entries(first, count):
        wait_tiles(diagonal + first, count)
        for place in range(count):
            row_block, col_block, _ = read_key(list_ref, first + place, blocks)
            slot = diagonal + first + place
            head, tail = buffer_ref[slot, 0], buffer_ref[slot, 1]
            add_mixed_products(vector_ref, total_ref, side_ref, row_block, col_block, head, tail)

    def run_pair(pair, carry):
        run_entries(pair * 2 * TURN, 2 * TURN)
        return carry

    def run_diagonal(turn, carry):
        wait_tiles(turn * TURN, TURN)
        for place in range(TURN):
            slot = turn * TURN + place
            add_diagonal(vector_ref, total_ref, 2 * slot + core, buffer_ref[slot, 0], buffer_ref[slot, 1])
        return carry

    pairs = (held + HALF - 1) // (2 * TURN)
    lax.fori_loop(0, pairs, run_pair, 0)
    first = pairs * 2 * TURN
    parts = (jnp.maximum(held - first, 0) + HALF - 1) // HALF
    pl.when(parts >= 2)(lambda: run_entries(first, TURN))
    pl.when(lax.rem(parts, 2) == 1)(lambda: run_entries(first + (parts - 1) * HALF, HALF))
    lax.fori_loop(0, diagonal // TURN, run_diagonal, 0)


def apply_tiles(stored, value_ref, list_ref, held_refs, partial_ref, scratch):
    blocks = value_ref.shape[0]
    vector_ref, total_ref = scratch[:2]

    def put_block(block, carry):
        store_pieces(vector_ref, block, value_ref[block], False)
        return carry

    lax.fori_loop(0, blocks, put_block, 0, unroll=8)
    total_ref[...] = jnp.zeros_like(total_ref)
    if stored:
        side_ref = scratch[4]
        side_ref[...] = jnp.zeros_like(side_ref)
        apply_stored(list_ref, held_refs[0], *scratch[2:5], vector_ref, total_ref, blocks)
        place = lax.broadcasted_iota(jnp.int32, (ROWS, 2 * ROWS), 0)
        piece = lax.broadcasted_iota(jnp.int32, (ROWS, 2 * ROWS), 1)
        both_pieces = jnp.where((piece == place) | (piece == place + ROWS), 1.0, 0.0).astype(bf16)

        def finish_block(block, carry):
            turned = lax.dot_general(
                both_pieces, side_ref[block].astype(bf16), (((1,), (1,)), ((), ())), preferred_element_type=f32
            )
            partial_ref[block] = total_ref[block, 0:ROWS] + total_ref[block, ROWS : 2 * ROWS] + turned
            return carry

        lax.fori_loop(0, blocks, finish_block, 0, unroll=16)
    else:
        apply_formed(list_ref, held_refs, vector_ref, total_ref, blocks)
        partial_ref[...] = total_ref[0:blocks, 0:ROWS] + total_ref[0:blocks, ROWS : 2 * ROWS]


def row_sum(value):
    return jnp.sum(jnp.sum(value, axis=0, keepdims=True), axis=2, keepdims=True)


def first_step_kernel(stored, list_ref, mine_ref, other_ref, base_ref, *rest):
    count = 1 if stored else 2
    held, rest = rest[:count], rest[count:]
    residual_ref, direction_ref, partial_ref, scalars_ref, *scratch = rest
    if stored:
        start_reads(list_ref, held[0], scratch[2], scratch[3], base_ref.shape[0])
    blocks = base_ref.shape[0]
    largest = jnp.max(mine_ref[blocks:] + other_ref[blocks:])
    base = base_ref[...]
    applied = ridge_shift * base + (mine_ref[0:blocks] + other_ref[0:blocks]) / largest
    norm_now = row_sum(base * base)
    step_size = norm_now / row_sum(base * applied)
    residual = base - step_size * applied
    norm_next = row_sum(residual * residual)
    direction = residual + (norm_next / norm_now) * base
    residual_ref[...] = residual
    direction_ref[...] = direction
    scalars_ref[0] = jnp.broadcast_to(step_size[0], (ROWS, LANES))
    scalars_ref[1] = jnp.broadcast_to(norm_next[0], (ROWS, LANES))
    scalars_ref[2] = jnp.full((ROWS, LANES), largest, f32)
    apply_tiles(stored, direction_ref, list_ref, held, partial_ref, scratch)


def next_step_kernel(
    stored, list_ref, mine_ref, other_ref, base_ref, residual_ref, direction_ref, scalars_ref, *rest
):
    count = 1 if stored else 2
    held, rest = rest[:count], rest[count:]
    weights_out, residual_out, direction_out, partial_ref, scalars_out, *scratch = rest
    if stored:
        start_reads(list_ref, held[0], scratch[2], scratch[3], base_ref.shape[0])
    step_before = scalars_ref[0:1, :, 0:1]
    norm_now = scalars_ref[1:2, :, 0:1]
    largest = scalars_ref[2:3, :, 0:1]
    direction = direction_ref[...]
    applied = ridge_shift * direction + (mine_ref[...] + other_ref[...]) / largest
    step_size = norm_now / row_sum(direction * applied)
    weights_out[...] = step_before * base_ref[...] + step_size * direction
    residual = residual_ref[...] - step_size * applied
    norm_next = row_sum(residual * residual)
    residual_out[...] = residual
    direction_out[...] = residual + (norm_next / norm_now) * direction
    scalars_out[0] = scalars_ref[0]
    scalars_out[1] = jnp.broadcast_to(norm_next[0], (ROWS, LANES))
    scalars_out[2] = scalars_ref[2]
    apply_tiles(stored, direction_out, list_ref, held, partial_ref, scratch)


def last_step_kernel(
    n_row, n_col, mine_ref, other_ref, weights_ref, residual_ref, direction_ref, scalars_ref, out_ref
):
    norm_now = scalars_ref[1:2, :, 0:1]
    largest = scalars_ref[2:3, :, 0:1]
    direction = direction_ref[...]
    applied = ridge_shift * direction + (mine_ref[...] + other_ref[...]) / largest
    step_size = norm_now / row_sum(direction * applied)
    core = lax.rem(lax.axis_index("row"), 2)
    row_blocks = n_col * BLOCK_DEV
    for pair in range(n_row // 2):
        span = pl.ds((2 * pair + core) * row_blocks, row_blocks)
        direction = direction_ref[span]
        applied = ridge_shift * direction + (mine_ref[span] + other_ref[span]) / largest
        weights = weights_ref[span] + step_size * direction
        residual = residual_ref[span] - step_size * applied
        for col in range(n_col):
            start = (pair * n_col + col) * 2 * BLOCK_DEV
            taken = slice(col * BLOCK_DEV, (col + 1) * BLOCK_DEV)
            out_ref[start : start + BLOCK_DEV] = weights[taken]
            out_ref[start + BLOCK_DEV : start + 2 * BLOCK_DEV] = residual[taken]


def unpack_kernel(groups, group_rows, received_ref, weights_ref, residual_ref):
    for group in range(groups):
        rows = slice(group * group_rows, (group + 1) * group_rows)
        for index, target in enumerate((weights_ref, residual_ref)):
            for half in range(BLOCK_DEV):
                target[rows, half * BLOCK : (half + 1) * BLOCK] = received_ref[
                    (2 * group + index) * BLOCK_DEV + half, 0:group_rows
                ]


def call(kernel, out_shape, *args, scratch=(), in_spaces=None, out_spaces=None, vmem=16):
    spaces = in_spaces or [pltpu.VMEM] * len(args)
    outs = out_spaces or jax.tree.map(lambda _: pltpu.VMEM, out_shape)
    return pl.pallas_call(
        kernel,
        out_shape=out_shape,
        in_specs=[pl.BlockSpec(memory_space=space) for space in spaces],
        out_specs=jax.tree.map(lambda space: pl.BlockSpec(memory_space=space), outs),
        scratch_shapes=list(scratch),
        compiler_params=pltpu.CompilerParams(vmem_limit_bytes=vmem * 2**20),
    )(*args)


def local(positions, targets, pairs, counts):
    n_row = lax.axis_size("row")
    n_col = lax.axis_size("col")
    n_dev = n_row * n_col
    blocks = n_dev * BLOCK_DEV
    entries = pairs.shape[1]
    groups = n_dev // 2
    group_rows = targets.shape[0] // groups
    room = -(-(n_dev * entries // 2) // TURN) * TURN
    stored = room <= STORED_MAX and blocks % (2 * TURN) == 0
    same_core = [
        [row * n_col + col for row in range(core, n_row, 2) for col in range(n_col)] for core in range(2)
    ]
    siblings = [(index, index ^ 1) for index in range(n_row)]
    shape = jax.ShapeDtypeStruct
    kept = pltpu.VMEM if stored else shape
    vmem = 56 if stored else 58
    field = kept((blocks, ROWS, BLOCK), f32)
    scalars = kept((3, ROWS, LANES), f32)

    def resident(array):
        return pltpu.with_memory_space_constraint(array, pltpu.VMEM) if stored else array

    def from_sibling(array):
        return resident(lax.ppermute(array, "row", siblings))

    def among_cores(array):
        return resident(
            lax.all_to_all(array, ("row", "col"), 0, 0, axis_index_groups=same_core, tiled=True)
        )

    packed = call(
        functools.partial(pack_kernel, n_row, n_col),
        kept((groups, ROWS, POINTS_DEV + BLOCK), f32),
        targets,
        positions,
        pairs,
        counts,
        in_spaces=[pl.ANY] * 4,
        scratch=[
            pltpu.VMEM(targets.shape, f32),
            pltpu.VMEM(positions.shape, f32),
            pltpu.VMEM(pairs.shape, jnp.int32),
            pltpu.SMEM(counts.shape, jnp.int32),
            pltpu.VMEM((ROWS, BLOCK), f32),
            pltpu.SemaphoreType.DMA((4,)),
        ],
        vmem=60,
    )
    mine = among_cores(resident(packed))
    other = from_sibling(mine)

    factors = [((blocks, BLOCK, PIECE_DEPTH), bf16), ((blocks, PIECE_DEPTH, BLOCK), bf16)]
    factor_scratch = [pltpu.VMEM(*factor) for factor in factors]
    first_partial = kept((blocks + -(-blocks // ROWS), ROWS, BLOCK), f32)
    first_scratch = [
        pltpu.VMEM((blocks, 4 * ROWS, BLOCK), bf16),
        pltpu.VMEM((blocks + 1, 4 * ROWS, BLOCK), f32),
    ]
    step_scratch = [
        pltpu.VMEM((blocks, 2 * ROWS, BLOCK), bf16),
        pltpu.VMEM((blocks + 1, 2 * ROWS, BLOCK), f32),
    ]
    if stored:
        listed, base, partial, *held = call(
            functools.partial(form_stored_kernel, n_row, n_col),
            [shape((1, LISTED), jnp.int32), field, first_partial, shape((room, 2, BLOCK, BLOCK), bf16)],
            mine,
            other,
            out_spaces=[pltpu.SMEM, pltpu.VMEM, pltpu.VMEM, pl.ANY],
            scratch=[
                pltpu.SMEM((1, LISTED), f32),
                pltpu.VMEM((1, LISTED), jnp.int32),
                pltpu.VMEM((1, LISTED), f32),
                pltpu.SemaphoreType.DMA((2,)),
                *first_scratch,
                *factor_scratch,
                pltpu.SemaphoreType.DMA((WRITE_SLOTS, TURN)),
                *[pltpu.VMEM((WRITE_SLOTS, 2, BLOCK, BLOCK), bf16)] * TURN,
            ],
            vmem=vmem,
        )
        held_spaces = [pl.ANY]
        step_scratch += [
            pltpu.VMEM((room, 2, BLOCK, BLOCK), bf16),
            pltpu.SemaphoreType.DMA((room // HALF,)),
            pltpu.VMEM((blocks, BLOCK, 2 * ROWS), f32),
        ]
    else:
        listed, base, partial, *held = call(
            functools.partial(form_kernel, n_row, n_col),
            [shape((1, room + 1), jnp.int32), field, first_partial, *(shape(*factor) for factor in factors)],
            mine,
            other,
            out_spaces=[pltpu.SMEM] + [pltpu.VMEM] * 4,
            scratch=[
                pltpu.SMEM((2, n_dev // 2, ROWS, LANES), f32),
                pltpu.SemaphoreType.DMA((2,)),
                *first_scratch,
            ],
            vmem=vmem,
        )
        held_spaces = [pltpu.VMEM] * 2
    base, partial = resident(base), resident(partial)

    def step(kernel, out_shape, *args):
        outs = call(
            functools.partial(kernel, stored),
            out_shape,
            listed,
            *args,
            *held,
            in_spaces=[pltpu.SMEM] + [pltpu.VMEM] * len(args) + held_spaces,
            scratch=step_scratch,
            vmem=vmem,
        )
        return [resident(out) for out in outs]

    residual, direction, partial, numbers = step(
        first_step_kernel, (field, field, field, scalars), partial, from_sibling(partial), base
    )
    weights, residual, direction, partial, numbers = step(
        next_step_kernel,
        (field, field, field, field, scalars),
        partial,
        from_sibling(partial),
        base,
        residual,
        direction,
        numbers,
    )
    result = call(
        functools.partial(last_step_kernel, n_row, n_col),
        field,
        partial,
        from_sibling(partial),
        weights,
        residual,
        direction,
        numbers,
    )
    home = among_cores(resident(result))
    out = shape(targets.shape, f32)
    return call(functools.partial(unpack_kernel, groups, group_rows), (out, out), home)


def solution(mesh):
    placed = (
        P(None, ("groups", "row", "col")),
        P(None, ("groups", "row", "col")),
        P(None, ("groups", "row", "col")),
        P(("groups", "row", "col")),
    )
    return jax.shard_map(
        local,
        mesh=mesh,
        in_specs=placed,
        out_specs=(P(None, ("groups", "row", "col")), P(None, ("groups", "row", "col"))),
        check_vma=False,
    )
```

```python
import functools

import jax
import jax.numpy as jnp
from jax import lax
from jax.experimental import pallas as pl
from jax.experimental.pallas import tpu as pltpu
from jax.sharding import PartitionSpec as P

BLOCK = 256
BLOCK_DEV = 2
LANES = 128
POINTS_DEV = BLOCK * BLOCK_DEV
ROWS = 8
PIECE_DEPTH = 64
TURN = 8
HALF = TURN // 2
STORED_MAX = 192
LISTED = 256
WRITE_SLOTS = 2

support_radius = 0.5
ridge_shift = 1.5
f32 = jnp.float32
bf16 = jnp.bfloat16


def pack_kernel(
    n_row, n_col, targets_in, positions_in, pairs_in, counts_in, out_ref, targets_ref, positions_ref, pairs_ref, counts_ref, extra_ref, sems
):
    copies = [
        pltpu.make_async_copy(source, kept, sems.at[index])
        for index, (source, kept) in enumerate(
            (
                (positions_in, positions_ref),
                (pairs_in, pairs_ref),
                (counts_in, counts_ref),
                (targets_in, targets_ref),
            )
        )
    ]
    for copy in copies:
        copy.start()
    for copy in copies[:3]:
        copy.wait()
    entries = pairs_ref.shape[1]
    groups = n_row // 2 * n_col
    group_rows = targets_ref.shape[0] // groups
    lane = lax.broadcasted_iota(jnp.int32, (1, BLOCK), 1)
    for half in range(BLOCK_DEV):
        extra_ref[4 * half : 4 * half + 3, :] = positions_ref[:, half * BLOCK : (half + 1) * BLOCK]
    extra_ref[3:4, :] = jnp.where(lane == LANES - 1, counts_ref[0], 0).astype(f32)
    extra_ref[7:8, :] = jnp.zeros((1, BLOCK), f32)
    extra_ref[3:4, 0:entries] = pairs_ref[0:1, :].astype(f32)
    extra_ref[7:8, 0:entries] = pairs_ref[1:2, :].astype(f32)
    copies[3].wait()
    for group in range(groups):
        if group_rows < ROWS:
            out_ref[group, :, 0:POINTS_DEV] = jnp.zeros((ROWS, POINTS_DEV), f32)
        out_ref[group, 0:group_rows, 0:POINTS_DEV] = targets_ref[group * group_rows : (group + 1) * group_rows, :]
        out_ref[group, :, POINTS_DEV : POINTS_DEV + BLOCK] = extra_ref[...]


def split(value, pieces):
    found = []
    for _ in range(pieces):
        piece = value.astype(bf16).astype(f32)
        found.append(piece)
        value = value - piece
    return found


def point_factors(extra, half):
    row = lax.broadcasted_iota(jnp.int32, (ROWS, BLOCK), 0)
    coords = pltpu.roll(extra, 4, 0) if half else extra
    coords = jnp.where(row < 3, (coords - 0.5) * (1.0 / support_radius), 0.0)
    first, second, third = split(coords, 3)
    norm = jnp.sum(coords * coords, axis=0, keepdims=True)
    norm_pieces = split(jnp.broadcast_to(norm, (ROWS, BLOCK)), 3)
    zero = jnp.zeros((ROWS, BLOCK), f32)
    norms = jnp.where(
        row == 0, norm_pieces[0], jnp.where(row == 1, norm_pieces[1], jnp.where(row == 2, norm_pieces[2], zero))
    )
    ones = jnp.where(row < 3, 1.0, 0.0).astype(f32)
    left = jnp.concatenate([first, first, second, second, first, third, norms, ones], axis=0)
    right = jnp.concatenate(
        [-2.0 * piece for piece in (first, second, first, second, third, first)] + [ones, norms], axis=0
    )
    return left, right


def form_tile(left, right, times):
    square = jnp.maximum(jnp.dot(left, right, preferred_element_type=f32), 1e-30)
    remain = jnp.maximum(1.0 - square * lax.rsqrt(square), 0.0)
    remain_two = remain * remain
    tile = remain_two * remain_two * (1.25 * times - times * remain)
    head = tile.astype(bf16)
    return head, (tile - head.astype(f32)).astype(bf16)


def add_diagonal(vector_ref, total_ref, block, head, tail):
    vector = vector_ref[block]
    total_ref[block] += jnp.dot(vector, head, preferred_element_type=f32) + jnp.dot(
        vector, tail, preferred_element_type=f32
    )


def add_products(vector_ref, total_ref, row_block, col_block, row_to, head, tail):
    over_cols = (((1,), (1,)), ((), ()))
    row_vector, col_vector = vector_ref[row_block], vector_ref[col_block]
    to_cols = jnp.dot(row_vector, head, preferred_element_type=f32) + jnp.dot(
        row_vector, tail, preferred_element_type=f32
    )
    to_rows = lax.dot_general(col_vector, head, over_cols, preferred_element_type=f32) + lax.dot_general(
        col_vector, tail, over_cols, preferred_element_type=f32
    )
    total_ref[col_block] += to_cols
    total_ref[row_to] += to_rows


def add_mixed_products(vector_ref, total_ref, side_ref, row_block, col_block, head, tail):
    over_cols = (((1,), (1,)), ((), ()))
    row_vector, col_vector = vector_ref[row_block], vector_ref[col_block]
    total_ref[col_block] += jnp.dot(row_vector, head, preferred_element_type=f32) + jnp.dot(
        row_vector, tail, preferred_element_type=f32
    )
    total_ref[row_block] += lax.dot_general(col_vector, head, over_cols, preferred_element_type=f32)
    side_ref[row_block] += lax.dot_general(tail, col_vector, over_cols, preferred_element_type=f32)


def store_pieces(vector_ref, block, value, with_ones):
    parts = split(value, 2)
    if with_ones:
        row = lax.broadcasted_iota(jnp.int32, (2 * ROWS, BLOCK), 0)
        parts.append(jnp.where(row == 0, 1.0, 0.0).astype(f32))
    vector_ref[block] = jnp.concatenate(parts, axis=0).astype(bf16)


def global_blocks(n_col, source, group, core):
    row_ids = source[group, 3:4, POINTS_DEV : POINTS_DEV + LANES].astype(jnp.int32)
    col_ids = source[group, 7:8, POINTS_DEV : POINTS_DEV + LANES].astype(jnp.int32)
    count = row_ids[:, LANES - 1 :]
    row, col = 2 * (group // n_col) + core, group % n_col
    in_use = lax.broadcasted_iota(jnp.int32, (1, LANES), 1) < count
    row_block = row * (n_col * BLOCK_DEV) + row_ids
    col_block = ((col_ids >> 1) * n_col + col) * BLOCK_DEV + (col_ids & 1)
    return jnp.minimum(row_block, col_block), jnp.maximum(row_block, col_block), in_use


def merged_list(n_dev, n_col, core, sources, keys_ref, times_ref):
    blocks = n_dev * BLOCK_DEV
    block_id = lax.broadcasted_iota(jnp.int32, (blocks, LANES), 0)
    smaller, larger = [], []
    for source, source_core in sources:
        for group in range(n_dev // 2):
            low, high, in_use = global_blocks(n_col, source, group, source_core)
            smaller.append(jnp.where((block_id == low) & in_use, 1.0, 0.0))
            larger.append(jnp.where((block_id == high) & in_use, 1.0, 0.0))
    over_lanes = (((1,), (1,)), ((), ()))
    times = lax.dot_general(
        jnp.concatenate(larger, axis=1).astype(bf16),
        jnp.concatenate(smaller, axis=1).astype(bf16),
        over_lanes,
        preferred_element_type=f32,
    )
    high_id = lax.broadcasted_iota(jnp.int32, (blocks, blocks), 0)
    low_id = lax.broadcasted_iota(jnp.int32, (blocks, blocks), 1)
    present = jnp.where((times > 0.0) & (high_id > low_id), 1.0, 0.0)
    before = jnp.where(high_id > low_id, 1.0, 0.0).astype(bf16)
    present_low = present.astype(bf16)
    in_column = jnp.dot(before, present_low, preferred_element_type=f32)
    column_sums = jnp.sum(present, axis=0, keepdims=True)
    column_starts = lax.dot_general(
        jnp.broadcast_to(column_sums, (ROWS, blocks)).astype(bf16), before, over_lanes, preferred_element_type=f32
    )[0:1]
    place = (in_column + column_starts).astype(jnp.int32)
    mine = (present > 0.0) & ((place & 1) == core)
    slot = jnp.where(mine, place >> 1, -1)
    key = low_id * blocks + high_id
    lane = lax.broadcasted_iota(jnp.int32, (blocks, LISTED), 1)
    keys = jnp.zeros((blocks, LISTED), jnp.int32)
    counted = jnp.zeros((blocks, LISTED), f32)
    for low in range(blocks):
        here = lane == slot[:, low : low + 1]
        keys = keys + jnp.where(here, key[:, low : low + 1], 0)
        counted = counted + jnp.where(here, times[:, low : low + 1], 0.0)
    held = jnp.sum(jnp.where(mine, 1.0, 0.0), axis=1, keepdims=True)
    held = jnp.sum(held, axis=0, keepdims=True).astype(jnp.int32)
    first_lane = lax.broadcasted_iota(jnp.int32, (1, LISTED), 1)
    keys_ref[...] = jnp.where(
        first_lane == LISTED - 1, held, jnp.sum(keys.astype(f32), axis=0, keepdims=True).astype(jnp.int32)
    )
    times_ref[...] = jnp.sum(counted, axis=0, keepdims=True)


def read_key(list_ref, slot, blocks):
    key = list_ref[0, slot]
    row_block, col_block = lax.div(key, blocks), lax.rem(key, blocks)
    return row_block, col_block, jnp.where(row_block == col_block, blocks, row_block)


def assemble_group(n_col, group, sources, base_ref, vector_ref, left_ref, right_ref):
    for source, source_core in sources:
        device = (2 * (group // n_col) + source_core) * n_col + lax.rem(group, n_col)
        extra = source[group, :, POINTS_DEV : POINTS_DEV + BLOCK]
        for half in range(BLOCK_DEV):
            block = BLOCK_DEV * device + half
            values = source[group, :, half * BLOCK : (half + 1) * BLOCK]
            base_ref[block] = values
            store_pieces(vector_ref, block, values, True)
            left, right = point_factors(extra, half)
            left_ref[block] = left.T.astype(bf16)
            right_ref[block] = right.astype(bf16)


def finish_first(total_ref, partial_ref, blocks):
    for block in range(blocks):
        partial_ref[block] = total_ref[block, 0:ROWS] + total_ref[block, ROWS : 2 * ROWS]
        partial_ref[blocks + block // ROWS, block % ROWS : block % ROWS + 1, :] = total_ref[
            block, 2 * ROWS : 2 * ROWS + 1
        ]


def form_stored_kernel(
    n_row,
    n_col,
    mine_ref,
    other_ref,
    list_ref,
    base_ref,
    partial_ref,
    tiles_ref,
    times_ref,
    keys_vector,
    times_vector,
    list_sems,
    vector_ref,
    total_ref,
    left_ref,
    right_ref,
    sems,
    *place_refs,
):
    n_dev = n_row * n_col
    blocks = n_dev * BLOCK_DEV
    core = lax.rem(lax.axis_index("row"), 2)
    sources = ((mine_ref, core), (other_ref, 1 - core))
    merged_list(n_dev, n_col, core, sources, keys_vector, times_vector)
    keys_copy = pltpu.make_async_copy(keys_vector, list_ref, list_sems.at[0])
    times_copy = pltpu.make_async_copy(times_vector, times_ref, list_sems.at[1])
    keys_copy.start()
    times_copy.start()

    def assemble(group, carry):
        assemble_group(n_col, group, sources, base_ref, vector_ref, left_ref, right_ref)
        return carry

    lax.fori_loop(0, n_dev // 2, assemble, 0, unroll=4)
    total_ref[...] = jnp.zeros_like(total_ref)
    last_place = place_refs[TURN - 1]
    last_place[WRITE_SLOTS - 1] = jnp.zeros(last_place.shape[1:], bf16)
    keys_copy.wait()
    times_copy.wait()
    held = list_ref[0, LISTED - 1]
    diagonal = blocks // 2
    diagonal_turns = diagonal // TURN

    def diagonal_block(slot):
        return 2 * slot + core

    def copies(turn, size=TURN):
        place_slot = lax.rem(turn, WRITE_SLOTS)
        return [
            pltpu.make_async_copy(
                place_refs[place].at[place_slot], tiles_ref.at[turn * TURN + place], sems.at[place_slot, place]
            )
            for place in range(size)
        ]

    def wait_turn(turn, size=TURN):
        for copy in copies(turn, size):
            copy.wait()

    def form(turn, place, row_block, col_block, times):
        head, tail = form_tile(left_ref[row_block], right_ref[col_block], times)
        place_refs[place][lax.rem(turn, WRITE_SLOTS), 0] = head
        place_refs[place][lax.rem(turn, WRITE_SLOTS), 1] = tail

    def kept_tile(turn, place):
        place_slot = lax.rem(turn, WRITE_SLOTS)
        return place_refs[place][place_slot, 0], place_refs[place][place_slot, 1]

    def multiply(turn, place):
        slot = turn * TURN + place
        row_block, col_block, _ = read_key(list_ref, jnp.maximum(slot - diagonal, 0), blocks)
        on_diagonal = slot < diagonal
        row_block = jnp.where(on_diagonal, diagonal_block(slot), row_block)
        col_block = jnp.where(on_diagonal, diagonal_block(slot), col_block)
        row_to = jnp.where(on_diagonal, blocks, row_block)
        add_products(vector_ref, total_ref, row_block, col_block, row_to, *kept_tile(turn, place))

    def run_diagonal(turn, carry):
        pl.when(turn >= WRITE_SLOTS)(lambda: wait_turn(turn - WRITE_SLOTS))
        for place in range(TURN):
            slot = turn * TURN + place
            form(turn, place, diagonal_block(slot), diagonal_block(slot), 1.0)
            before = (turn, place - 1) if place else (turn + 1, TURN - 1)
            add_diagonal(vector_ref, total_ref, diagonal_block(jnp.maximum(slot - 1, 0)), *kept_tile(*before))
        for copy in copies(turn):
            copy.start()
        return carry

    def run_turn(turn, size):
        wait_turn(turn - WRITE_SLOTS)
        for place in range(size):
            entry = turn * TURN + place - diagonal
            row_block, col_block, _ = read_key(list_ref, entry, blocks)
            form(turn, place, row_block, col_block, times_ref[0, entry])
            multiply(*((turn, place - 1) if place else (turn - 1, TURN - 1)))
        for copy in copies(turn, size):
            copy.start()

    def run_full(turn, carry):
        run_turn(turn, TURN)
        return carry

    turns = diagonal_turns + (held + TURN - HALF - 1) // TURN
    with_half = held > (turns - diagonal_turns) * TURN
    lax.fori_loop(0, diagonal_turns, run_diagonal, 0)
    lax.fori_loop(diagonal_turns, turns, run_full, 0)

    @pl.when(with_half)
    def _():
        run_turn(turns, HALF)
        multiply(turns, HALF - 1)
        wait_turn(turns, HALF)

    @pl.when(jnp.logical_not(with_half))
    def _():
        multiply(turns - 1, TURN - 1)
        wait_turn(turns - 2)

    finish_first(total_ref, partial_ref, blocks)
    wait_turn(turns - 1)


def form_kernel(
    n_row, n_col, mine_ref, other_ref, list_ref, base_ref, partial_ref, left_ref, right_ref, meta_ref, meta_sems, vector_ref, total_ref
):
    n_dev = n_row * n_col
    blocks = n_dev * BLOCK_DEV
    core = lax.rem(lax.axis_index("row"), 2)
    sources = ((mine_ref, core), (other_ref, 1 - core))
    meta_copies = [
        pltpu.make_async_copy(
            source.at[:, :, POINTS_DEV : POINTS_DEV + LANES], meta_ref.at[source_core], meta_sems.at[index]
        )
        for index, (source, source_core) in enumerate(sources)
    ]
    for copy in meta_copies:
        copy.start()

    def assemble(group, carry):
        assemble_group(n_col, group, sources, base_ref, vector_ref, left_ref, right_ref)
        return carry

    lax.fori_loop(0, n_dev // 2, assemble, 0)
    total_ref[...] = jnp.zeros_like(total_ref)
    for copy in meta_copies:
        copy.wait()

    def read_device(device, carry):
        seen, held = carry
        row = device // n_col
        col = lax.rem(device, n_col)
        source_core, group = lax.rem(row, 2), (row // 2) * n_col + col
        count = meta_ref[source_core, group, 3, LANES - 1].astype(jnp.int32)
        first = lax.rem(seen + core, 2)
        taken = (count - first + 1) // 2

        def read_entry(index, carry):
            slot = first + 2 * index
            row_id = meta_ref[source_core, group, 3, slot].astype(jnp.int32)
            col_id = meta_ref[source_core, group, 7, slot].astype(jnp.int32)
            row_block = row * (n_col * BLOCK_DEV) + row_id
            col_block = ((col_id // BLOCK_DEV) * n_col + col) * BLOCK_DEV + lax.rem(col_id, BLOCK_DEV)
            list_ref[0, held + index] = row_block * blocks + col_block
            return carry

        lax.fori_loop(0, taken, read_entry, 0)
        return seen + count, held + taken

    _, held = lax.fori_loop(0, n_dev, read_device, (0, 0))
    list_ref[0, list_ref.shape[1] - 1] = held
    apply_formed(list_ref, (left_ref, right_ref), vector_ref, total_ref, blocks)
    finish_first(total_ref, partial_ref, blocks)


def apply_formed(list_ref, factor_refs, vector_ref, total_ref, blocks):
    def run_entry(entry, carry):
        row_block, col_block, row_to = read_key(list_ref, entry, blocks)
        head, tail = form_tile(factor_refs[0][row_block], factor_refs[1][col_block], 1.0)
        add_products(vector_ref, total_ref, row_block, col_block, row_to, head, tail)
        return carry

    lax.fori_loop(0, list_ref[0, list_ref.shape[1] - 1], run_entry, 0)


def read_copy(part, tiles_ref, buffer_ref, sems):
    span = pl.ds(part * HALF, HALF)
    return pltpu.make_async_copy(tiles_ref.at[span], buffer_ref.at[span], sems.at[part])


def start_reads(list_ref, tiles_ref, buffer_ref, sems, blocks):
    def start(part, carry):
        read_copy(part, tiles_ref, buffer_ref, sems).start()
        return carry

    diagonal = blocks // 2
    lax.fori_loop(diagonal // HALF, (diagonal + list_ref[0, LISTED - 1] + HALF - 1) // HALF, start, 0)
    lax.fori_loop(0, diagonal // HALF, start, 0)


def apply_stored(list_ref, tiles_ref, buffer_ref, sems, side_ref, vector_ref, total_ref, blocks):
    held = list_ref[0, LISTED - 1]
    core = lax.rem(lax.axis_index("row"), 2)
    diagonal = blocks // 2

    def wait_tiles(slot, count):
        for part in range(count // HALF):
            read_copy(slot // HALF + part, tiles_ref, buffer_ref, sems).wait()

    def run_entries(first, count):
        wait_tiles(diagonal + first, count)
        for place in range(count):
            row_block, col_block, _ = read_key(list_ref, first + place, blocks)
            slot = diagonal + first + place
            head, tail = buffer_ref[slot, 0], buffer_ref[slot, 1]
            add_mixed_products(vector_ref, total_ref, side_ref, row_block, col_block, head, tail)

    def run_full(turn, carry):
        run_entries(turn * TURN, TURN)
        return carry

    def run_diagonal(turn, carry):
        wait_tiles(turn * TURN, TURN)
        for place in range(TURN):
            slot = turn * TURN + place
            add_diagonal(vector_ref, total_ref, 2 * slot + core, buffer_ref[slot, 0], buffer_ref[slot, 1])
        return carry

    full = (held + HALF - 1) // TURN
    lax.fori_loop(0, full, run_full, 0)
    pl.when(held > full * TURN)(lambda: run_entries(full * TURN, HALF))
    lax.fori_loop(0, diagonal // TURN, run_diagonal, 0)


def apply_tiles(stored, value_ref, list_ref, held_refs, partial_ref, scratch):
    blocks = value_ref.shape[0]
    vector_ref, total_ref = scratch[:2]

    def put_block(block, carry):
        store_pieces(vector_ref, block, value_ref[block], False)
        return carry

    lax.fori_loop(0, blocks, put_block, 0, unroll=32)
    total_ref[...] = jnp.zeros_like(total_ref)
    if stored:
        side_ref = scratch[4]
        side_ref[...] = jnp.zeros_like(side_ref)
        apply_stored(list_ref, held_refs[0], *scratch[2:5], vector_ref, total_ref, blocks)
        place = lax.broadcasted_iota(jnp.int32, (ROWS, 2 * ROWS), 0)
        piece = lax.broadcasted_iota(jnp.int32, (ROWS, 2 * ROWS), 1)
        both_pieces = jnp.where((piece == place) | (piece == place + ROWS), 1.0, 0.0).astype(bf16)

        def finish_block(block, carry):
            turned = lax.dot_general(
                both_pieces, side_ref[block].astype(bf16), (((1,), (1,)), ((), ())), preferred_element_type=f32
            )
            partial_ref[block] = total_ref[block, 0:ROWS] + total_ref[block, ROWS : 2 * ROWS] + turned
            return carry

        lax.fori_loop(0, blocks, finish_block, 0, unroll=32)
    else:
        apply_formed(list_ref, held_refs, vector_ref, total_ref, blocks)
        partial_ref[...] = total_ref[0:blocks, 0:ROWS] + total_ref[0:blocks, ROWS : 2 * ROWS]


def row_sum(value):
    return jnp.sum(jnp.sum(value, axis=0, keepdims=True), axis=2, keepdims=True)


def first_step_kernel(stored, list_ref, mine_ref, other_ref, base_ref, *rest):
    count = 1 if stored else 2
    held, rest = rest[:count], rest[count:]
    residual_ref, direction_ref, partial_ref, scalars_ref, *scratch = rest
    if stored:
        start_reads(list_ref, held[0], scratch[2], scratch[3], base_ref.shape[0])
    blocks = base_ref.shape[0]
    largest = jnp.max(mine_ref[blocks:] + other_ref[blocks:])
    base = base_ref[...]
    applied = ridge_shift * base + (mine_ref[0:blocks] + other_ref[0:blocks]) / largest
    norm_now = row_sum(base * base)
    step_size = norm_now / row_sum(base * applied)
    residual = base - step_size * applied
    norm_next = row_sum(residual * residual)
    direction = residual + (norm_next / norm_now) * base
    residual_ref[...] = residual
    direction_ref[...] = direction
    scalars_ref[0] = jnp.broadcast_to(step_size[0], (ROWS, LANES))
    scalars_ref[1] = jnp.broadcast_to(norm_next[0], (ROWS, LANES))
    scalars_ref[2] = jnp.full((ROWS, LANES), largest, f32)
    apply_tiles(stored, direction_ref, list_ref, held, partial_ref, scratch)


def next_step_kernel(
    stored, list_ref, mine_ref, other_ref, base_ref, residual_ref, direction_ref, scalars_ref, *rest
):
    count = 1 if stored else 2
    held, rest = rest[:count], rest[count:]
    weights_out, residual_out, direction_out, partial_ref, scalars_out, *scratch = rest
    if stored:
        start_reads(list_ref, held[0], scratch[2], scratch[3], base_ref.shape[0])
    step_before = scalars_ref[0:1, :, 0:1]
    norm_now = scalars_ref[1:2, :, 0:1]
    largest = scalars_ref[2:3, :, 0:1]
    direction = direction_ref[...]
    applied = ridge_shift * direction + (mine_ref[...] + other_ref[...]) / largest
    step_size = norm_now / row_sum(direction * applied)
    weights_out[...] = step_before * base_ref[...] + step_size * direction
    residual = residual_ref[...] - step_size * applied
    norm_next = row_sum(residual * residual)
    residual_out[...] = residual
    direction_out[...] = residual + (norm_next / norm_now) * direction
    scalars_out[0] = scalars_ref[0]
    scalars_out[1] = jnp.broadcast_to(norm_next[0], (ROWS, LANES))
    scalars_out[2] = scalars_ref[2]
    apply_tiles(stored, direction_out, list_ref, held, partial_ref, scratch)


def last_step_kernel(
    n_row, n_col, mine_ref, other_ref, weights_ref, residual_ref, direction_ref, scalars_ref, out_ref
):
    norm_now = scalars_ref[1:2, :, 0:1]
    largest = scalars_ref[2:3, :, 0:1]
    direction = direction_ref[...]
    applied = ridge_shift * direction + (mine_ref[...] + other_ref[...]) / largest
    step_size = norm_now / row_sum(direction * applied)
    core = lax.rem(lax.axis_index("row"), 2)
    row_blocks = n_col * BLOCK_DEV
    for pair in range(n_row // 2):
        span = pl.ds((2 * pair + core) * row_blocks, row_blocks)
        direction = direction_ref[span]
        applied = ridge_shift * direction + (mine_ref[span] + other_ref[span]) / largest
        weights = weights_ref[span] + step_size * direction
        residual = residual_ref[span] - step_size * applied
        for col in range(n_col):
            start = (pair * n_col + col) * 2 * BLOCK_DEV
            taken = slice(col * BLOCK_DEV, (col + 1) * BLOCK_DEV)
            out_ref[start : start + BLOCK_DEV] = weights[taken]
            out_ref[start + BLOCK_DEV : start + 2 * BLOCK_DEV] = residual[taken]


def unpack_kernel(groups, group_rows, received_ref, weights_ref, residual_ref):
    for group in range(groups):
        rows = slice(group * group_rows, (group + 1) * group_rows)
        for index, target in enumerate((weights_ref, residual_ref)):
            for half in range(BLOCK_DEV):
                target[rows, half * BLOCK : (half + 1) * BLOCK] = received_ref[
                    (2 * group + index) * BLOCK_DEV + half, 0:group_rows
                ]


def call(kernel, out_shape, *args, scratch=(), in_spaces=None, out_spaces=None, vmem=16):
    spaces = in_spaces or [pltpu.VMEM] * len(args)
    outs = out_spaces or jax.tree.map(lambda _: pltpu.VMEM, out_shape)
    return pl.pallas_call(
        kernel,
        out_shape=out_shape,
        in_specs=[pl.BlockSpec(memory_space=space) for space in spaces],
        out_specs=jax.tree.map(lambda space: pl.BlockSpec(memory_space=space), outs),
        scratch_shapes=list(scratch),
        compiler_params=pltpu.CompilerParams(vmem_limit_bytes=vmem * 2**20),
    )(*args)


def local(positions, targets, pairs, counts):
    n_row = lax.axis_size("row")
    n_col = lax.axis_size("col")
    n_dev = n_row * n_col
    blocks = n_dev * BLOCK_DEV
    entries = pairs.shape[1]
    groups = n_dev // 2
    group_rows = targets.shape[0] // groups
    room = -(-(n_dev * entries // 2) // TURN) * TURN
    stored = room <= STORED_MAX and blocks % (2 * TURN) == 0
    same_core = [
        [row * n_col + col for row in range(core, n_row, 2) for col in range(n_col)] for core in range(2)
    ]
    siblings = [(index, index ^ 1) for index in range(n_row)]
    shape = jax.ShapeDtypeStruct
    kept = pltpu.VMEM if stored else shape
    vmem = 56 if stored else 58
    field = kept((blocks, ROWS, BLOCK), f32)
    scalars = kept((3, ROWS, LANES), f32)

    def resident(array):
        return pltpu.with_memory_space_constraint(array, pltpu.VMEM) if stored else array

    def from_sibling(array):
        return resident(lax.ppermute(array, "row", siblings))

    def among_cores(array):
        return resident(
            lax.all_to_all(array, ("row", "col"), 0, 0, axis_index_groups=same_core, tiled=True)
        )

    packed = call(
        functools.partial(pack_kernel, n_row, n_col),
        kept((groups, ROWS, POINTS_DEV + BLOCK), f32),
        targets,
        positions,
        pairs,
        counts,
        in_spaces=[pl.ANY] * 4,
        scratch=[
            pltpu.VMEM(targets.shape, f32),
            pltpu.VMEM(positions.shape, f32),
            pltpu.VMEM(pairs.shape, jnp.int32),
            pltpu.SMEM(counts.shape, jnp.int32),
            pltpu.VMEM((ROWS, BLOCK), f32),
            pltpu.SemaphoreType.DMA((4,)),
        ],
        vmem=60,
    )
    mine = among_cores(resident(packed))
    other = from_sibling(mine)

    factors = [((blocks, BLOCK, PIECE_DEPTH), bf16), ((blocks, PIECE_DEPTH, BLOCK), bf16)]
    factor_scratch = [pltpu.VMEM(*factor) for factor in factors]
    first_partial = kept((blocks + -(-blocks // ROWS), ROWS, BLOCK), f32)
    first_scratch = [
        pltpu.VMEM((blocks, 4 * ROWS, BLOCK), bf16),
        pltpu.VMEM((blocks + 1, 4 * ROWS, BLOCK), f32),
    ]
    step_scratch = [
        pltpu.VMEM((blocks, 2 * ROWS, BLOCK), bf16),
        pltpu.VMEM((blocks + 1, 2 * ROWS, BLOCK), f32),
    ]
    if stored:
        listed, base, partial, *held = call(
            functools.partial(form_stored_kernel, n_row, n_col),
            [shape((1, LISTED), jnp.int32), field, first_partial, shape((room, 2, BLOCK, BLOCK), bf16)],
            mine,
            other,
            out_spaces=[pltpu.SMEM, pltpu.VMEM, pltpu.VMEM, pl.ANY],
            scratch=[
                pltpu.SMEM((1, LISTED), f32),
                pltpu.VMEM((1, LISTED), jnp.int32),
                pltpu.VMEM((1, LISTED), f32),
                pltpu.SemaphoreType.DMA((2,)),
                *first_scratch,
                *factor_scratch,
                pltpu.SemaphoreType.DMA((WRITE_SLOTS, TURN)),
                *[pltpu.VMEM((WRITE_SLOTS, 2, BLOCK, BLOCK), bf16)] * TURN,
            ],
            vmem=vmem,
        )
        held_spaces = [pl.ANY]
        step_scratch += [
            pltpu.VMEM((room, 2, BLOCK, BLOCK), bf16),
            pltpu.SemaphoreType.DMA((room // HALF,)),
            pltpu.VMEM((blocks, BLOCK, 2 * ROWS), f32),
        ]
    else:
        listed, base, partial, *held = call(
            functools.partial(form_kernel, n_row, n_col),
            [shape((1, room + 1), jnp.int32), field, first_partial, *(shape(*factor) for factor in factors)],
            mine,
            other,
            out_spaces=[pltpu.SMEM] + [pltpu.VMEM] * 4,
            scratch=[
                pltpu.SMEM((2, n_dev // 2, ROWS, LANES), f32),
                pltpu.SemaphoreType.DMA((2,)),
                *first_scratch,
            ],
            vmem=vmem,
        )
        held_spaces = [pltpu.VMEM] * 2
    base, partial = resident(base), resident(partial)

    def step(kernel, out_shape, *args):
        outs = call(
            functools.partial(kernel, stored),
            out_shape,
            listed,
            *args,
            *held,
            in_spaces=[pltpu.SMEM] + [pltpu.VMEM] * len(args) + held_spaces,
            scratch=step_scratch,
            vmem=vmem,
        )
        return [resident(out) for out in outs]

    residual, direction, partial, numbers = step(
        first_step_kernel, (field, field, field, scalars), partial, from_sibling(partial), base
    )
    weights, residual, direction, partial, numbers = step(
        next_step_kernel,
        (field, field, field, field, scalars),
        partial,
        from_sibling(partial),
        base,
        residual,
        direction,
        numbers,
    )
    result = call(
        functools.partial(last_step_kernel, n_row, n_col),
        field,
        partial,
        from_sibling(partial),
        weights,
        residual,
        direction,
        numbers,
    )
    home = among_cores(resident(result))
    out = shape(targets.shape, f32)
    return call(functools.partial(unpack_kernel, groups, group_rows), (out, out), home)


def solution(mesh):
    placed = (
        P(None, ("groups", "row", "col")),
        P(None, ("groups", "row", "col")),
        P(None, ("groups", "row", "col")),
        P(("groups", "row", "col")),
    )
    return jax.shard_map(
        local,
        mesh=mesh,
        in_specs=placed,
        out_specs=(P(None, ("groups", "row", "col")), P(None, ("groups", "row", "col"))),
        check_vma=False,
    )
```

```python
import functools

import jax
import jax.numpy as jnp
from jax import lax
from jax.experimental import pallas as pl
from jax.experimental.pallas import tpu as pltpu
from jax.sharding import PartitionSpec as P

BLOCK = 256
BLOCK_DEV = 2
LANES = 128
POINTS_DEV = BLOCK * BLOCK_DEV
ROWS = 8
PIECE_DEPTH = 64
TURN = 8
HALF = TURN // 2
STORED_MAX = 192
LISTED = 256
WRITE_SLOTS = 2

support_radius = 0.5
ridge_shift = 1.5
f32 = jnp.float32
bf16 = jnp.bfloat16


def pack_kernel(
    n_row, n_col, targets_in, positions_in, pairs_in, counts_in, out_ref, targets_ref, positions_ref, pairs_ref, counts_ref, extra_ref, sems
):
    copies = [
        pltpu.make_async_copy(source, kept, sems.at[index])
        for index, (source, kept) in enumerate(
            (
                (positions_in, positions_ref),
                (pairs_in, pairs_ref),
                (counts_in, counts_ref),
                (targets_in, targets_ref),
            )
        )
    ]
    for copy in copies:
        copy.start()
    for copy in copies[:3]:
        copy.wait()
    entries = pairs_ref.shape[1]
    groups = n_row // 2 * n_col
    group_rows = targets_ref.shape[0] // groups
    lane = lax.broadcasted_iota(jnp.int32, (1, BLOCK), 1)
    for half in range(BLOCK_DEV):
        extra_ref[4 * half : 4 * half + 3, :] = positions_ref[:, half * BLOCK : (half + 1) * BLOCK]
    extra_ref[3:4, :] = jnp.where(lane == LANES - 1, counts_ref[0], 0).astype(f32)
    extra_ref[7:8, :] = jnp.zeros((1, BLOCK), f32)
    extra_ref[3:4, 0:entries] = pairs_ref[0:1, :].astype(f32)
    extra_ref[7:8, 0:entries] = pairs_ref[1:2, :].astype(f32)
    copies[3].wait()
    for group in range(groups):
        if group_rows < ROWS:
            out_ref[group, :, 0:POINTS_DEV] = jnp.zeros((ROWS, POINTS_DEV), f32)
        out_ref[group, 0:group_rows, 0:POINTS_DEV] = targets_ref[group * group_rows : (group + 1) * group_rows, :]
        out_ref[group, :, POINTS_DEV : POINTS_DEV + BLOCK] = extra_ref[...]


def split(value, pieces):
    found = []
    for _ in range(pieces):
        piece = value.astype(bf16).astype(f32)
        found.append(piece)
        value = value - piece
    return found


def point_factors(extra, half):
    row = lax.broadcasted_iota(jnp.int32, (ROWS, BLOCK), 0)
    coords = pltpu.roll(extra, 4, 0) if half else extra
    coords = jnp.where(row < 3, (coords - 0.5) * (1.0 / support_radius), 0.0)
    first, second, third = split(coords, 3)
    norm = jnp.sum(coords * coords, axis=0, keepdims=True)
    norm_pieces = split(jnp.broadcast_to(norm, (ROWS, BLOCK)), 3)
    zero = jnp.zeros((ROWS, BLOCK), f32)
    norms = jnp.where(
        row == 0, norm_pieces[0], jnp.where(row == 1, norm_pieces[1], jnp.where(row == 2, norm_pieces[2], zero))
    )
    ones = jnp.where(row < 3, 1.0, 0.0).astype(f32)
    left = jnp.concatenate([first, first, second, second, first, third, norms, ones], axis=0)
    right = jnp.concatenate(
        [-2.0 * piece for piece in (first, second, first, second, third, first)] + [ones, norms], axis=0
    )
    return left, right


def form_tile(left, right, times):
    square = jnp.maximum(jnp.dot(left, right, preferred_element_type=f32), 1e-30)
    remain = jnp.maximum(1.0 - square * lax.rsqrt(square), 0.0)
    remain_two = remain * remain
    tile = remain_two * remain_two * (1.25 * times - times * remain)
    head = tile.astype(bf16)
    return head, (tile - head.astype(f32)).astype(bf16)


def add_diagonal(vector_ref, total_ref, block, head, tail):
    vector = vector_ref[block]
    total_ref[block] += jnp.dot(vector, head, preferred_element_type=f32) + jnp.dot(
        vector, tail, preferred_element_type=f32
    )


def add_products(vector_ref, total_ref, row_block, col_block, row_to, head, tail):
    over_cols = (((1,), (1,)), ((), ()))
    row_vector, col_vector = vector_ref[row_block], vector_ref[col_block]
    to_cols = jnp.dot(row_vector, head, preferred_element_type=f32) + jnp.dot(
        row_vector, tail, preferred_element_type=f32
    )
    to_rows = lax.dot_general(col_vector, head, over_cols, preferred_element_type=f32) + lax.dot_general(
        col_vector, tail, over_cols, preferred_element_type=f32
    )
    total_ref[col_block] += to_cols
    total_ref[row_to] += to_rows


def add_mixed_products(vector_ref, total_ref, side_ref, row_block, col_block, head, tail):
    over_cols = (((1,), (1,)), ((), ()))
    row_vector, col_vector = vector_ref[row_block], vector_ref[col_block]
    total_ref[col_block] += jnp.dot(row_vector, head, preferred_element_type=f32) + jnp.dot(
        row_vector, tail, preferred_element_type=f32
    )
    total_ref[row_block] += lax.dot_general(col_vector, head, over_cols, preferred_element_type=f32)
    side_ref[row_block] += lax.dot_general(tail, col_vector, over_cols, preferred_element_type=f32)


def store_pieces(vector_ref, block, value, with_ones):
    parts = split(value, 2)
    if with_ones:
        row = lax.broadcasted_iota(jnp.int32, (2 * ROWS, BLOCK), 0)
        parts.append(jnp.where(row == 0, 1.0, 0.0).astype(f32))
    vector_ref[block] = jnp.concatenate(parts, axis=0).astype(bf16)


def global_blocks(n_col, source, group, core):
    row_ids = source[group, 3:4, POINTS_DEV : POINTS_DEV + LANES].astype(jnp.int32)
    col_ids = source[group, 7:8, POINTS_DEV : POINTS_DEV + LANES].astype(jnp.int32)
    count = row_ids[:, LANES - 1 :]
    row, col = 2 * (group // n_col) + core, group % n_col
    in_use = lax.broadcasted_iota(jnp.int32, (1, LANES), 1) < count
    row_block = row * (n_col * BLOCK_DEV) + row_ids
    col_block = ((col_ids >> 1) * n_col + col) * BLOCK_DEV + (col_ids & 1)
    return jnp.minimum(row_block, col_block), jnp.maximum(row_block, col_block), in_use


def merged_list(n_dev, n_col, core, sources, keys_ref, times_ref):
    blocks = n_dev * BLOCK_DEV
    block_id = lax.broadcasted_iota(jnp.int32, (blocks, LANES), 0)
    smaller, larger = [], []
    for source, source_core in sources:
        for group in range(n_dev // 2):
            low, high, in_use = global_blocks(n_col, source, group, source_core)
            smaller.append(jnp.where((block_id == low) & in_use, 1.0, 0.0))
            larger.append(jnp.where((block_id == high) & in_use, 1.0, 0.0))
    over_lanes = (((1,), (1,)), ((), ()))
    times = lax.dot_general(
        jnp.concatenate(larger, axis=1).astype(bf16),
        jnp.concatenate(smaller, axis=1).astype(bf16),
        over_lanes,
        preferred_element_type=f32,
    )
    high_id = lax.broadcasted_iota(jnp.int32, (blocks, blocks), 0)
    low_id = lax.broadcasted_iota(jnp.int32, (blocks, blocks), 1)
    present = jnp.where((times > 0.0) & (high_id > low_id), 1.0, 0.0)
    before = jnp.where(high_id > low_id, 1.0, 0.0).astype(bf16)
    present_low = present.astype(bf16)
    in_column = jnp.dot(before, present_low, preferred_element_type=f32)
    column_sums = jnp.sum(present, axis=0, keepdims=True)
    column_starts = lax.dot_general(
        jnp.broadcast_to(column_sums, (ROWS, blocks)).astype(bf16), before, over_lanes, preferred_element_type=f32
    )[0:1]
    place = (in_column + column_starts).astype(jnp.int32)
    mine = (present > 0.0) & ((place & 1) == core)
    slot = jnp.where(mine, place >> 1, -1)
    value = (low_id * blocks + high_id).astype(f32) + float(blocks * blocks) * times
    lane = lax.broadcasted_iota(jnp.int32, (blocks, LISTED), 1)
    values = jnp.zeros((blocks, LISTED), f32)
    for low in range(blocks):
        values = values + jnp.where(lane == slot[:, low : low + 1], value[:, low : low + 1], 0.0)
    listed = jnp.sum(values, axis=0, keepdims=True).astype(jnp.int32)
    held = jnp.sum(jnp.where(mine, 1.0, 0.0), axis=1, keepdims=True)
    held = jnp.sum(held, axis=0, keepdims=True).astype(jnp.int32)
    first_lane = lax.broadcasted_iota(jnp.int32, (1, LISTED), 1)
    keys_ref[...] = jnp.where(first_lane == LISTED - 1, held, lax.rem(listed, blocks * blocks))
    times_ref[...] = lax.div(listed, blocks * blocks).astype(f32)


def read_key(list_ref, slot, blocks):
    key = list_ref[0, slot]
    row_block, col_block = lax.div(key, blocks), lax.rem(key, blocks)
    return row_block, col_block, jnp.where(row_block == col_block, blocks, row_block)


def assemble_group(n_col, group, sources, base_ref, vector_ref, left_ref, right_ref):
    for source, source_core in sources:
        device = (2 * (group // n_col) + source_core) * n_col + lax.rem(group, n_col)
        extra = source[group, :, POINTS_DEV : POINTS_DEV + BLOCK]
        for half in range(BLOCK_DEV):
            block = BLOCK_DEV * device + half
            values = source[group, :, half * BLOCK : (half + 1) * BLOCK]
            base_ref[block] = values
            store_pieces(vector_ref, block, values, True)
            left, right = point_factors(extra, half)
            left_ref[block] = left.T.astype(bf16)
            right_ref[block] = right.astype(bf16)


def finish_first(total_ref, partial_ref, blocks):
    for block in range(blocks):
        partial_ref[block] = total_ref[block, 0:ROWS] + total_ref[block, ROWS : 2 * ROWS]
        partial_ref[blocks + block // ROWS, block % ROWS : block % ROWS + 1, :] = total_ref[
            block, 2 * ROWS : 2 * ROWS + 1
        ]


def form_stored_kernel(
    n_row,
    n_col,
    mine_ref,
    other_ref,
    list_ref,
    base_ref,
    partial_ref,
    tiles_ref,
    times_ref,
    keys_vector,
    times_vector,
    list_sems,
    vector_ref,
    total_ref,
    left_ref,
    right_ref,
    sems,
    even_ref,
    odd_ref,
):
    n_dev = n_row * n_col
    blocks = n_dev * BLOCK_DEV
    core = lax.rem(lax.axis_index("row"), 2)
    sources = ((mine_ref, core), (other_ref, 1 - core))
    def assemble(group, carry):
        assemble_group(n_col, group, sources, base_ref, vector_ref, left_ref, right_ref)
        return carry

    lax.fori_loop(0, n_dev // 2, assemble, 0, unroll=4)
    total_ref[...] = jnp.zeros_like(total_ref)
    merged_list(n_dev, n_col, core, sources, keys_vector, times_vector)
    keys_copy = pltpu.make_async_copy(keys_vector, list_ref, list_sems.at[0])
    times_copy = pltpu.make_async_copy(times_vector, times_ref, list_sems.at[1])
    keys_copy.start()
    times_copy.start()

    odd_ref[WRITE_SLOTS - 1, HALF - 1] = jnp.zeros(odd_ref.shape[2:], bf16)
    diagonal = blocks // 2
    diagonal_turns = diagonal // TURN

    def diagonal_block(slot):
        return 2 * slot + core

    def entry_at(turn, place, size=TURN):
        return turn * TURN + place % 2 * (size // 2) + place // 2

    def copies(turn, size=TURN):
        place_slot = lax.rem(turn, WRITE_SLOTS)
        return [
            pltpu.make_async_copy(
                buffer_ref.at[place_slot, pl.ds(0, size // 2)],
                tiles_ref.at[pl.ds(turn * TURN + odd * (size // 2), size // 2)],
                sems.at[place_slot, odd],
            )
            for odd, buffer_ref in enumerate((even_ref, odd_ref))
        ]

    def wait_turn(turn, size=TURN):
        for copy in copies(turn, size):
            copy.wait()

    def form(turn, place, row_block, col_block, times):
        head, tail = form_tile(left_ref[row_block], right_ref[col_block], times)
        buffer_ref = odd_ref if place % 2 else even_ref
        buffer_ref[lax.rem(turn, WRITE_SLOTS), place // 2, 0] = head
        buffer_ref[lax.rem(turn, WRITE_SLOTS), place // 2, 1] = tail

    def kept_tile(turn, place):
        buffer_ref, place_slot = odd_ref if place % 2 else even_ref, lax.rem(turn, WRITE_SLOTS)
        return buffer_ref[place_slot, place // 2, 0], buffer_ref[place_slot, place // 2, 1]

    def multiply(turn, place, size):
        slot = entry_at(turn, place, size)
        row_block, col_block, _ = read_key(list_ref, jnp.maximum(slot - diagonal, 0), blocks)
        on_diagonal = slot < diagonal
        row_block = jnp.where(on_diagonal, diagonal_block(slot), row_block)
        col_block = jnp.where(on_diagonal, diagonal_block(slot), col_block)
        row_to = jnp.where(on_diagonal, blocks, row_block)
        add_products(vector_ref, total_ref, row_block, col_block, row_to, *kept_tile(turn, place))

    def run_diagonal(turn, carry):
        pl.when(turn >= WRITE_SLOTS)(lambda: wait_turn(turn - WRITE_SLOTS))
        for place in range(TURN):
            block = diagonal_block(entry_at(turn, place))
            form(turn, place, block, block, 1.0)
            if place:
                before, tile = entry_at(turn, place - 1), kept_tile(turn, place - 1)
            else:
                before, tile = jnp.maximum(turn * TURN - 1, 0), kept_tile(turn + 1, TURN - 1)
            add_diagonal(vector_ref, total_ref, diagonal_block(before), *tile)
        for copy in copies(turn):
            copy.start()
        return carry

    def run_turn(turn, size):
        wait_turn(turn - WRITE_SLOTS)
        for place in range(size):
            entry = entry_at(turn, place, size) - diagonal
            row_block, col_block, _ = read_key(list_ref, entry, blocks)
            form(turn, place, row_block, col_block, times_ref[0, entry])
            multiply(*((turn, place - 1, size) if place else (turn - 1, TURN - 1, TURN)))
        for copy in copies(turn, size):
            copy.start()

    def run_full(turn, carry):
        run_turn(turn, TURN)
        return carry

    lax.fori_loop(0, diagonal_turns, run_diagonal, 0)
    keys_copy.wait()
    times_copy.wait()
    held = list_ref[0, LISTED - 1]
    turns = diagonal_turns + (held + TURN - HALF - 1) // TURN
    with_half = held > (turns - diagonal_turns) * TURN
    lax.fori_loop(diagonal_turns, turns, run_full, 0)

    @pl.when(with_half)
    def _():
        run_turn(turns, HALF)
        multiply(turns, HALF - 1, HALF)
        wait_turn(turns, HALF)

    @pl.when(jnp.logical_not(with_half))
    def _():
        multiply(turns - 1, TURN - 1, TURN)
        wait_turn(turns - 2)

    finish_first(total_ref, partial_ref, blocks)
    wait_turn(turns - 1)


def form_kernel(
    n_row, n_col, mine_ref, other_ref, list_ref, base_ref, partial_ref, left_ref, right_ref, meta_ref, meta_sems, vector_ref, total_ref
):
    n_dev = n_row * n_col
    blocks = n_dev * BLOCK_DEV
    core = lax.rem(lax.axis_index("row"), 2)
    sources = ((mine_ref, core), (other_ref, 1 - core))
    meta_copies = [
        pltpu.make_async_copy(
            source.at[:, :, POINTS_DEV : POINTS_DEV + LANES], meta_ref.at[source_core], meta_sems.at[index]
        )
        for index, (source, source_core) in enumerate(sources)
    ]
    for copy in meta_copies:
        copy.start()

    def assemble(group, carry):
        assemble_group(n_col, group, sources, base_ref, vector_ref, left_ref, right_ref)
        return carry

    lax.fori_loop(0, n_dev // 2, assemble, 0)
    total_ref[...] = jnp.zeros_like(total_ref)
    for copy in meta_copies:
        copy.wait()

    def read_device(device, carry):
        seen, held = carry
        row = device // n_col
        col = lax.rem(device, n_col)
        source_core, group = lax.rem(row, 2), (row // 2) * n_col + col
        count = meta_ref[source_core, group, 3, LANES - 1].astype(jnp.int32)
        first = lax.rem(seen + core, 2)
        taken = (count - first + 1) // 2

        def read_entry(index, carry):
            slot = first + 2 * index
            row_id = meta_ref[source_core, group, 3, slot].astype(jnp.int32)
            col_id = meta_ref[source_core, group, 7, slot].astype(jnp.int32)
            row_block = row * (n_col * BLOCK_DEV) + row_id
            col_block = ((col_id // BLOCK_DEV) * n_col + col) * BLOCK_DEV + lax.rem(col_id, BLOCK_DEV)
            list_ref[0, held + index] = row_block * blocks + col_block
            return carry

        lax.fori_loop(0, taken, read_entry, 0)
        return seen + count, held + taken

    _, held = lax.fori_loop(0, n_dev, read_device, (0, 0))
    list_ref[0, list_ref.shape[1] - 1] = held
    apply_formed(list_ref, (left_ref, right_ref), vector_ref, total_ref, blocks)
    finish_first(total_ref, partial_ref, blocks)


def apply_formed(list_ref, factor_refs, vector_ref, total_ref, blocks):
    def run_entry(entry, carry):
        row_block, col_block, row_to = read_key(list_ref, entry, blocks)
        head, tail = form_tile(factor_refs[0][row_block], factor_refs[1][col_block], 1.0)
        add_products(vector_ref, total_ref, row_block, col_block, row_to, head, tail)
        return carry

    lax.fori_loop(0, list_ref[0, list_ref.shape[1] - 1], run_entry, 0)


def read_copy(first, count, tiles_ref, buffer_ref, sems):
    span = pl.ds(first, count)
    return pltpu.make_async_copy(tiles_ref.at[span], buffer_ref.at[span], sems.at[first // HALF])


def start_reads(list_ref, tiles_ref, buffer_ref, sems, blocks):
    def start(turn, carry):
        read_copy(turn * TURN, TURN, tiles_ref, buffer_ref, sems).start()
        return carry

    diagonal = blocks // 2
    held = diagonal + list_ref[0, LISTED - 1]
    full = (held + TURN - HALF - 1) // TURN
    lax.fori_loop(diagonal // TURN, full, start, 0)
    pl.when(held > full * TURN)(lambda: read_copy(full * TURN, HALF, tiles_ref, buffer_ref, sems).start())
    read_copy(0, diagonal, tiles_ref, buffer_ref, sems).start()


def apply_stored(list_ref, tiles_ref, buffer_ref, sems, side_ref, vector_ref, total_ref, blocks):
    held = list_ref[0, LISTED - 1]
    core = lax.rem(lax.axis_index("row"), 2)
    diagonal = blocks // 2

    def run_entries(first, count):
        read_copy(diagonal + first, count, tiles_ref, buffer_ref, sems).wait()
        for place in range(count):
            row_block, col_block, _ = read_key(list_ref, first + place, blocks)
            slot = diagonal + first + place
            head, tail = buffer_ref[slot, 0], buffer_ref[slot, 1]
            add_mixed_products(vector_ref, total_ref, side_ref, row_block, col_block, head, tail)

    def run_full(turn, carry):
        run_entries(turn * TURN, TURN)
        return carry

    def run_diagonal(turn, carry):
        for place in range(TURN):
            slot = turn * TURN + place
            add_diagonal(vector_ref, total_ref, 2 * slot + core, buffer_ref[slot, 0], buffer_ref[slot, 1])
        return carry

    full = (held + HALF - 1) // TURN
    lax.fori_loop(0, full, run_full, 0)
    pl.when(held > full * TURN)(lambda: run_entries(full * TURN, HALF))
    read_copy(0, diagonal, tiles_ref, buffer_ref, sems).wait()
    lax.fori_loop(0, diagonal // TURN, run_diagonal, 0)


def apply_tiles(stored, value_ref, list_ref, held_refs, partial_ref, scratch):
    blocks = value_ref.shape[0]
    vector_ref, total_ref = scratch[:2]

    def put_block(block, carry):
        store_pieces(vector_ref, block, value_ref[block], False)
        return carry

    lax.fori_loop(0, blocks, put_block, 0, unroll=32)
    if stored:
        side_ref = scratch[4]
        apply_stored(list_ref, held_refs[0], *scratch[2:5], vector_ref, total_ref, blocks)
        place = lax.broadcasted_iota(jnp.int32, (ROWS, 2 * ROWS), 0)
        piece = lax.broadcasted_iota(jnp.int32, (ROWS, 2 * ROWS), 1)
        both_pieces = jnp.where((piece == place) | (piece == place + ROWS), 1.0, 0.0).astype(bf16)

        def finish_block(block, carry):
            turned = lax.dot_general(
                both_pieces, side_ref[block].astype(bf16), (((1,), (1,)), ((), ())), preferred_element_type=f32
            )
            partial_ref[block] = total_ref[block, 0:ROWS] + total_ref[block, ROWS : 2 * ROWS] + turned
            return carry

        lax.fori_loop(0, blocks, finish_block, 0, unroll=32)
    else:
        apply_formed(list_ref, held_refs, vector_ref, total_ref, blocks)
        partial_ref[...] = total_ref[0:blocks, 0:ROWS] + total_ref[0:blocks, ROWS : 2 * ROWS]


def row_sum(value):
    return jnp.sum(jnp.sum(value, axis=0, keepdims=True), axis=2, keepdims=True)


def first_step_kernel(stored, list_ref, mine_ref, other_ref, base_ref, *rest):
    count = 1 if stored else 2
    held, rest = rest[:count], rest[count:]
    residual_ref, direction_ref, partial_ref, scalars_ref, *scratch = rest
    if stored:
        start_reads(list_ref, held[0], scratch[2], scratch[3], base_ref.shape[0])
        scratch[4][...] = jnp.zeros_like(scratch[4])
    scratch[1][...] = jnp.zeros_like(scratch[1])
    blocks = base_ref.shape[0]
    largest = jnp.max(mine_ref[blocks:] + other_ref[blocks:])
    base = base_ref[...]
    applied = ridge_shift * base + (mine_ref[0:blocks] + other_ref[0:blocks]) / largest
    norm_now = row_sum(base * base)
    step_size = norm_now / row_sum(base * applied)
    residual = base - step_size * applied
    norm_next = row_sum(residual * residual)
    direction = residual + (norm_next / norm_now) * base
    residual_ref[...] = residual
    direction_ref[...] = direction
    scalars_ref[0] = jnp.broadcast_to(step_size[0], (ROWS, LANES))
    scalars_ref[1] = jnp.broadcast_to(norm_next[0], (ROWS, LANES))
    scalars_ref[2] = jnp.full((ROWS, LANES), largest, f32)
    apply_tiles(stored, direction_ref, list_ref, held, partial_ref, scratch)


def next_step_kernel(
    stored, n_row, n_col, list_ref, mine_ref, other_ref, base_ref, residual_ref, direction_ref, scalars_ref, *rest
):
    count = 1 if stored else 2
    held, rest = rest[:count], rest[count:]
    weights_out, residual_out, direction_out, kept_ref, sent_ref, scalars_out, *scratch = rest
    partial_ref = scratch.pop()
    if stored:
        start_reads(list_ref, held[0], scratch[2], scratch[3], base_ref.shape[0])
        scratch[4][...] = jnp.zeros_like(scratch[4])
    scratch[1][...] = jnp.zeros_like(scratch[1])
    step_before = scalars_ref[0:1, :, 0:1]
    norm_now = scalars_ref[1:2, :, 0:1]
    largest = scalars_ref[2:3, :, 0:1]
    direction = direction_ref[...]
    applied = ridge_shift * direction + (mine_ref[...] + other_ref[...]) / largest
    step_size = norm_now / row_sum(direction * applied)
    weights_out[...] = step_before * base_ref[...] + step_size * direction
    residual = residual_ref[...] - step_size * applied
    norm_next = row_sum(residual * residual)
    residual_out[...] = residual
    direction_out[...] = residual + (norm_next / norm_now) * direction
    scalars_out[0] = scalars_ref[0]
    scalars_out[1] = jnp.broadcast_to(norm_next[0], (ROWS, LANES))
    scalars_out[2] = scalars_ref[2]
    apply_tiles(stored, direction_out, list_ref, held, partial_ref, scratch)
    core = lax.rem(lax.axis_index("row"), 2)
    row_blocks = n_col * BLOCK_DEV
    product = row_sum(direction_out[...] * partial_ref[...])[0]
    for pair in range(n_row // 2):
        taken = slice(pair * row_blocks, (pair + 1) * row_blocks)
        kept_ref[taken] = partial_ref[pl.ds((2 * pair + core) * row_blocks, row_blocks)]
        sent_ref[taken] = partial_ref[pl.ds((2 * pair + 1 - core) * row_blocks, row_blocks)]
    kept_ref[kept_ref.shape[0] - 1] = jnp.broadcast_to(product, (ROWS, BLOCK))
    sent_ref[sent_ref.shape[0] - 1] = jnp.broadcast_to(product, (ROWS, BLOCK))


def last_step_kernel(
    n_row, n_col, mine_ref, other_ref, weights_ref, residual_ref, direction_ref, scalars_ref, out_ref
):
    norm_now = scalars_ref[1:2, :, 0:1]
    largest = scalars_ref[2:3, :, 0:1]
    direction = direction_ref[...]
    last = mine_ref.shape[0] - 1
    product = (mine_ref[last:, :, 0:1] + other_ref[last:, :, 0:1]) / largest
    step_size = norm_now / (ridge_shift * row_sum(direction * direction) + product)
    core = lax.rem(lax.axis_index("row"), 2)
    row_blocks = n_col * BLOCK_DEV
    for pair in range(n_row // 2):
        span = pl.ds((2 * pair + core) * row_blocks, row_blocks)
        own = slice(pair * row_blocks, (pair + 1) * row_blocks)
        direction = direction_ref[span]
        applied = ridge_shift * direction + (mine_ref[own] + other_ref[own]) / largest
        weights = weights_ref[span] + step_size * direction
        residual = residual_ref[span] - step_size * applied
        for col in range(n_col):
            start = (pair * n_col + col) * 2 * BLOCK_DEV
            taken = slice(col * BLOCK_DEV, (col + 1) * BLOCK_DEV)
            out_ref[start : start + BLOCK_DEV] = weights[taken]
            out_ref[start + BLOCK_DEV : start + 2 * BLOCK_DEV] = residual[taken]


def unpack_kernel(groups, group_rows, received_ref, weights_ref, residual_ref):
    for group in range(groups):
        rows = slice(group * group_rows, (group + 1) * group_rows)
        for index, target in enumerate((weights_ref, residual_ref)):
            for half in range(BLOCK_DEV):
                target[rows, half * BLOCK : (half + 1) * BLOCK] = received_ref[
                    (2 * group + index) * BLOCK_DEV + half, 0:group_rows
                ]


def call(kernel, out_shape, *args, scratch=(), in_spaces=None, out_spaces=None, vmem=16):
    spaces = in_spaces or [pltpu.VMEM] * len(args)
    outs = out_spaces or jax.tree.map(lambda _: pltpu.VMEM, out_shape)
    return pl.pallas_call(
        kernel,
        out_shape=out_shape,
        in_specs=[pl.BlockSpec(memory_space=space) for space in spaces],
        out_specs=jax.tree.map(lambda space: pl.BlockSpec(memory_space=space), outs),
        scratch_shapes=list(scratch),
        compiler_params=pltpu.CompilerParams(vmem_limit_bytes=vmem * 2**20),
    )(*args)


def local(positions, targets, pairs, counts):
    n_row = lax.axis_size("row")
    n_col = lax.axis_size("col")
    n_dev = n_row * n_col
    blocks = n_dev * BLOCK_DEV
    entries = pairs.shape[1]
    groups = n_dev // 2
    group_rows = targets.shape[0] // groups
    room = -(-(n_dev * entries // 2) // TURN) * TURN
    stored = room <= STORED_MAX and blocks % (2 * TURN) == 0
    same_core = [
        [row * n_col + col for row in range(core, n_row, 2) for col in range(n_col)] for core in range(2)
    ]
    siblings = [(index, index ^ 1) for index in range(n_row)]
    shape = jax.ShapeDtypeStruct
    kept = pltpu.VMEM if stored else shape
    vmem = 56 if stored else 58
    field = kept((blocks, ROWS, BLOCK), f32)
    scalars = kept((3, ROWS, LANES), f32)

    def resident(array):
        return pltpu.with_memory_space_constraint(array, pltpu.VMEM) if stored else array

    def from_sibling(array):
        return resident(lax.ppermute(array, "row", siblings))

    def among_cores(array):
        return resident(
            lax.all_to_all(array, ("row", "col"), 0, 0, axis_index_groups=same_core, tiled=True)
        )

    packed = call(
        functools.partial(pack_kernel, n_row, n_col),
        kept((groups, ROWS, POINTS_DEV + BLOCK), f32),
        targets,
        positions,
        pairs,
        counts,
        in_spaces=[pl.ANY] * 4,
        scratch=[
            pltpu.VMEM(targets.shape, f32),
            pltpu.VMEM(positions.shape, f32),
            pltpu.VMEM(pairs.shape, jnp.int32),
            pltpu.SMEM(counts.shape, jnp.int32),
            pltpu.VMEM((ROWS, BLOCK), f32),
            pltpu.SemaphoreType.DMA((4,)),
        ],
        vmem=60,
    )
    mine = among_cores(resident(packed))
    other = from_sibling(mine)

    factors = [((blocks, BLOCK, PIECE_DEPTH), bf16), ((blocks, PIECE_DEPTH, BLOCK), bf16)]
    factor_scratch = [pltpu.VMEM(*factor) for factor in factors]
    first_partial = kept((blocks + -(-blocks // ROWS), ROWS, BLOCK), f32)
    first_scratch = [
        pltpu.VMEM((blocks, 4 * ROWS, BLOCK), bf16),
        pltpu.VMEM((blocks + 1, 4 * ROWS, BLOCK), f32),
    ]
    step_scratch = [
        pltpu.VMEM((blocks, 2 * ROWS, BLOCK), bf16),
        pltpu.VMEM((blocks + 1, 2 * ROWS, BLOCK), f32),
    ]
    if stored:
        listed, base, partial, *held = call(
            functools.partial(form_stored_kernel, n_row, n_col),
            [shape((1, LISTED), jnp.int32), field, first_partial, shape((room, 2, BLOCK, BLOCK), bf16)],
            mine,
            other,
            out_spaces=[pltpu.SMEM, pltpu.VMEM, pltpu.VMEM, pl.ANY],
            scratch=[
                pltpu.SMEM((1, LISTED), f32),
                pltpu.VMEM((1, LISTED), jnp.int32),
                pltpu.VMEM((1, LISTED), f32),
                pltpu.SemaphoreType.DMA((2,)),
                *first_scratch,
                *factor_scratch,
                pltpu.SemaphoreType.DMA((WRITE_SLOTS, 2)),
                *[pltpu.VMEM((WRITE_SLOTS, HALF, 2, BLOCK, BLOCK), bf16)] * 2,
            ],
            vmem=vmem,
        )
        held_spaces = [pl.ANY]
        step_scratch += [
            pltpu.VMEM((room, 2, BLOCK, BLOCK), bf16),
            pltpu.SemaphoreType.DMA((room // HALF,)),
            pltpu.VMEM((blocks, BLOCK, 2 * ROWS), f32),
        ]
    else:
        listed, base, partial, *held = call(
            functools.partial(form_kernel, n_row, n_col),
            [shape((1, room + 1), jnp.int32), field, first_partial, *(shape(*factor) for factor in factors)],
            mine,
            other,
            out_spaces=[pltpu.SMEM] + [pltpu.VMEM] * 4,
            scratch=[
                pltpu.SMEM((2, n_dev // 2, ROWS, LANES), f32),
                pltpu.SemaphoreType.DMA((2,)),
                *first_scratch,
            ],
            vmem=vmem,
        )
        held_spaces = [pltpu.VMEM] * 2
    base, partial = resident(base), resident(partial)

    def step(kernel, out_shape, *args, more_scratch=()):
        outs = call(
            kernel,
            out_shape,
            listed,
            *args,
            *held,
            in_spaces=[pltpu.SMEM] + [pltpu.VMEM] * len(args) + held_spaces,
            scratch=[*step_scratch, *more_scratch],
            vmem=vmem,
        )
        return [resident(out) for out in outs]

    residual, direction, partial, numbers = step(
        functools.partial(first_step_kernel, stored), (field, field, field, scalars), partial, from_sibling(partial), base
    )
    half_field = kept((blocks // 2 + 1, ROWS, BLOCK), f32)
    weights, residual, direction, partial, sent, numbers = step(
        functools.partial(next_step_kernel, stored, n_row, n_col),
        (field, field, field, half_field, half_field, scalars),
        partial,
        from_sibling(partial),
        base,
        residual,
        direction,
        numbers,
        more_scratch=[pltpu.VMEM((blocks, ROWS, BLOCK), f32)],
    )
    result = call(
        functools.partial(last_step_kernel, n_row, n_col),
        field,
        partial,
        from_sibling(sent),
        weights,
        residual,
        direction,
        numbers,
    )
    home = among_cores(resident(result))
    out = shape(targets.shape, f32)
    return call(functools.partial(unpack_kernel, groups, group_rows), (out, out), home)


def solution(mesh):
    placed = (
        P(None, ("groups", "row", "col")),
        P(None, ("groups", "row", "col")),
        P(None, ("groups", "row", "col")),
        P(("groups", "row", "col")),
    )
    return jax.shard_map(
        local,
        mesh=mesh,
        in_specs=placed,
        out_specs=(P(None, ("groups", "row", "col")), P(None, ("groups", "row", "col"))),
        check_vma=False,
    )
```

```python
import functools

import jax
import jax.numpy as jnp
from jax import lax
from jax.experimental import pallas as pl
from jax.experimental.pallas import tpu as pltpu
from jax.sharding import PartitionSpec as P

BLOCK = 256
BLOCK_DEV = 2
LANES = 128
POINTS_DEV = BLOCK * BLOCK_DEV
ROWS = 8
PIECE_DEPTH = 64
TURN = 8
HALF = TURN // 2
STORED_MAX = 192
LISTED = 256
WRITE_SLOTS = 2

support_radius = 0.5
ridge_shift = 1.5
f32 = jnp.float32
bf16 = jnp.bfloat16


def pack_kernel(
    n_row, n_col, targets_in, positions_in, pairs_in, counts_in, out_ref, targets_ref, positions_ref, pairs_ref, counts_ref, extra_ref, sems
):
    copies = [
        pltpu.make_async_copy(source, kept, sems.at[index])
        for index, (source, kept) in enumerate(
            (
                (positions_in, positions_ref),
                (pairs_in, pairs_ref),
                (counts_in, counts_ref),
                (targets_in, targets_ref),
            )
        )
    ]
    for copy in copies:
        copy.start()
    for copy in copies[:3]:
        copy.wait()
    entries = pairs_ref.shape[1]
    groups = n_row // 2 * n_col
    group_rows = targets_ref.shape[0] // groups
    lane = lax.broadcasted_iota(jnp.int32, (1, BLOCK), 1)
    for half in range(BLOCK_DEV):
        extra_ref[4 * half : 4 * half + 3, :] = positions_ref[:, half * BLOCK : (half + 1) * BLOCK]
    extra_ref[3:4, :] = jnp.where(lane == LANES - 1, counts_ref[0], 0).astype(f32)
    extra_ref[7:8, :] = jnp.zeros((1, BLOCK), f32)
    extra_ref[3:4, 0:entries] = pairs_ref[0:1, :].astype(f32)
    extra_ref[7:8, 0:entries] = pairs_ref[1:2, :].astype(f32)
    copies[3].wait()
    for group in range(groups):
        if group_rows < ROWS:
            out_ref[group, :, 0:POINTS_DEV] = jnp.zeros((ROWS, POINTS_DEV), f32)
        out_ref[group, 0:group_rows, 0:POINTS_DEV] = targets_ref[group * group_rows : (group + 1) * group_rows, :]
        out_ref[group, :, POINTS_DEV : POINTS_DEV + BLOCK] = extra_ref[...]


def split(value, pieces):
    found = []
    for _ in range(pieces):
        piece = value.astype(bf16).astype(f32)
        found.append(piece)
        value = value - piece
    return found


def point_factors(extra, half):
    row = lax.broadcasted_iota(jnp.int32, (ROWS, BLOCK), 0)
    coords = pltpu.roll(extra, 4, 0) if half else extra
    coords = jnp.where(row < 3, (coords - 0.5) * (1.0 / support_radius), 0.0)
    first, second, third = split(coords, 3)
    norm = jnp.sum(coords * coords, axis=0, keepdims=True)
    norm_pieces = split(jnp.broadcast_to(norm, (ROWS, BLOCK)), 3)
    zero = jnp.zeros((ROWS, BLOCK), f32)
    norms = jnp.where(
        row == 0, norm_pieces[0], jnp.where(row == 1, norm_pieces[1], jnp.where(row == 2, norm_pieces[2], zero))
    )
    ones = jnp.where(row < 3, 1.0, 0.0).astype(f32)
    left = jnp.concatenate([first, first, second, second, first, third, norms, ones], axis=0)
    right = jnp.concatenate(
        [-2.0 * piece for piece in (first, second, first, second, third, first)] + [ones, norms], axis=0
    )
    return left, right


def form_tile(left, right, times):
    square = jnp.maximum(jnp.dot(left, right, preferred_element_type=f32), 1e-30)
    remain = jnp.maximum(1.0 - square * lax.rsqrt(square), 0.0)
    remain_two = remain * remain
    tile = remain_two * remain_two * (1.25 * times - times * remain)
    head = tile.astype(bf16)
    return head, (tile - head.astype(f32)).astype(bf16)


def add_diagonal(vector_ref, total_ref, block, head, tail):
    vector = vector_ref[block]
    total_ref[block] += jnp.dot(vector, head, preferred_element_type=f32) + jnp.dot(
        vector, tail, preferred_element_type=f32
    )


def add_products(vector_ref, total_ref, row_block, col_block, row_to, head, tail):
    over_cols = (((1,), (1,)), ((), ()))
    row_vector, col_vector = vector_ref[row_block], vector_ref[col_block]
    to_cols = jnp.dot(row_vector, head, preferred_element_type=f32) + jnp.dot(
        row_vector, tail, preferred_element_type=f32
    )
    to_rows = lax.dot_general(col_vector, head, over_cols, preferred_element_type=f32) + lax.dot_general(
        col_vector, tail, over_cols, preferred_element_type=f32
    )
    total_ref[col_block] += to_cols
    total_ref[row_to] += to_rows


def add_mixed_products(vector_ref, total_ref, side_ref, row_block, col_block, head, tail):
    over_cols = (((1,), (1,)), ((), ()))
    row_vector, col_vector = vector_ref[row_block], vector_ref[col_block]
    total_ref[col_block] += jnp.dot(row_vector, head, preferred_element_type=f32) + jnp.dot(
        row_vector, tail, preferred_element_type=f32
    )
    total_ref[row_block] += lax.dot_general(col_vector, head, over_cols, preferred_element_type=f32)
    side_ref[row_block] += lax.dot_general(tail, col_vector, over_cols, preferred_element_type=f32)


def store_pieces(vector_ref, block, value, with_ones):
    parts = split(value, 2)
    if with_ones:
        row = lax.broadcasted_iota(jnp.int32, (2 * ROWS, BLOCK), 0)
        parts.append(jnp.where(row == 0, 1.0, 0.0).astype(f32))
    vector_ref[block] = jnp.concatenate(parts, axis=0).astype(bf16)


def global_blocks(n_col, source, group, core):
    row_ids = source[group, 3:4, POINTS_DEV : POINTS_DEV + LANES].astype(jnp.int32)
    col_ids = source[group, 7:8, POINTS_DEV : POINTS_DEV + LANES].astype(jnp.int32)
    count = row_ids[:, LANES - 1 :]
    row, col = 2 * (group // n_col) + core, group % n_col
    in_use = lax.broadcasted_iota(jnp.int32, (1, LANES), 1) < count
    row_block = row * (n_col * BLOCK_DEV) + row_ids
    col_block = ((col_ids >> 1) * n_col + col) * BLOCK_DEV + (col_ids & 1)
    return jnp.minimum(row_block, col_block), jnp.maximum(row_block, col_block), in_use


def merged_list(n_dev, n_col, core, sources, keys_ref, times_ref):
    blocks = n_dev * BLOCK_DEV
    block_id = lax.broadcasted_iota(jnp.int32, (blocks, LANES), 0)
    smaller, larger = [], []
    for source, source_core in sources:
        for group in range(n_dev // 2):
            low, high, in_use = global_blocks(n_col, source, group, source_core)
            smaller.append(jnp.where((block_id == low) & in_use, 1.0, 0.0))
            larger.append(jnp.where((block_id == high) & in_use, 1.0, 0.0))
    over_lanes = (((1,), (1,)), ((), ()))
    times = lax.dot_general(
        jnp.concatenate(larger, axis=1).astype(bf16),
        jnp.concatenate(smaller, axis=1).astype(bf16),
        over_lanes,
        preferred_element_type=f32,
    )
    high_id = lax.broadcasted_iota(jnp.int32, (blocks, blocks), 0)
    low_id = lax.broadcasted_iota(jnp.int32, (blocks, blocks), 1)
    present = jnp.where((times > 0.0) & (high_id > low_id), 1.0, 0.0)
    before = jnp.where(high_id > low_id, 1.0, 0.0).astype(bf16)
    present_low = present.astype(bf16)
    in_column = jnp.dot(before, present_low, preferred_element_type=f32)
    column_sums = jnp.sum(present, axis=0, keepdims=True)
    column_starts = lax.dot_general(
        jnp.broadcast_to(column_sums, (ROWS, blocks)).astype(bf16), before, over_lanes, preferred_element_type=f32
    )[0:1]
    place = (in_column + column_starts).astype(jnp.int32)
    mine = (present > 0.0) & ((place & 1) == core)
    slot = jnp.where(mine, place >> 1, -1)
    value = (low_id * blocks + high_id).astype(f32) + float(blocks * blocks) * times
    lane = lax.broadcasted_iota(jnp.int32, (blocks, LISTED), 1)
    values = jnp.zeros((blocks, LISTED), f32)
    for low in range(blocks):
        values = values + jnp.where(lane == slot[:, low : low + 1], value[:, low : low + 1], 0.0)
    listed = jnp.sum(values, axis=0, keepdims=True).astype(jnp.int32)
    held = jnp.sum(jnp.where(mine, 1.0, 0.0), axis=1, keepdims=True)
    held = jnp.sum(held, axis=0, keepdims=True).astype(jnp.int32)
    first_lane = lax.broadcasted_iota(jnp.int32, (1, LISTED), 1)
    keys_ref[...] = jnp.where(first_lane == LISTED - 1, held, lax.rem(listed, blocks * blocks))
    times_ref[...] = lax.div(listed, blocks * blocks).astype(f32)


def read_key(list_ref, slot, blocks):
    key = list_ref[0, slot]
    row_block, col_block = lax.div(key, blocks), lax.rem(key, blocks)
    return row_block, col_block, jnp.where(row_block == col_block, blocks, row_block)


def assemble_group(n_col, group, sources, base_ref, vector_ref, left_ref, right_ref):
    for source, source_core in sources:
        device = (2 * (group // n_col) + source_core) * n_col + lax.rem(group, n_col)
        extra = source[group, :, POINTS_DEV : POINTS_DEV + BLOCK]
        for half in range(BLOCK_DEV):
            block = BLOCK_DEV * device + half
            values = source[group, :, half * BLOCK : (half + 1) * BLOCK]
            base_ref[block] = values
            store_pieces(vector_ref, block, values, True)
            left, right = point_factors(extra, half)
            left_ref[block] = left.T.astype(bf16)
            right_ref[block] = right.astype(bf16)


def finish_first(total_ref, partial_ref, blocks):
    for block in range(blocks):
        partial_ref[block] = total_ref[block, 0:ROWS] + total_ref[block, ROWS : 2 * ROWS]
        partial_ref[blocks + block // ROWS, block % ROWS : block % ROWS + 1, :] = total_ref[
            block, 2 * ROWS : 2 * ROWS + 1
        ]


def form_stored_kernel(
    n_row,
    n_col,
    mine_ref,
    other_ref,
    list_ref,
    base_ref,
    partial_ref,
    diagonal_ref,
    tiles_ref,
    times_ref,
    keys_vector,
    times_vector,
    list_sems,
    vector_ref,
    total_ref,
    left_ref,
    right_ref,
    sems,
    even_ref,
    odd_ref,
):
    n_dev = n_row * n_col
    blocks = n_dev * BLOCK_DEV
    core = lax.rem(lax.axis_index("row"), 2)
    sources = ((mine_ref, core), (other_ref, 1 - core))
    def assemble(group, carry):
        assemble_group(n_col, group, sources, base_ref, vector_ref, left_ref, right_ref)
        return carry

    lax.fori_loop(0, n_dev // 2, assemble, 0, unroll=4)
    total_ref[...] = jnp.zeros_like(total_ref)
    merged_list(n_dev, n_col, core, sources, keys_vector, times_vector)
    keys_copy = pltpu.make_async_copy(keys_vector, list_ref, list_sems.at[0])
    times_copy = pltpu.make_async_copy(times_vector, times_ref, list_sems.at[1])
    keys_copy.start()
    times_copy.start()

    odd_ref[WRITE_SLOTS - 1, HALF - 1] = jnp.zeros(odd_ref.shape[2:], bf16)
    diagonal = blocks // 2
    diagonal_turns = diagonal // TURN

    def diagonal_block(slot):
        return 2 * slot + core

    def entry_at(turn, place, size=TURN):
        return turn * TURN + place % 2 * (size // 2) + place // 2

    def copies(turn, size=TURN, kept_ref=tiles_ref):
        place_slot = lax.rem(turn, WRITE_SLOTS)
        return [
            pltpu.make_async_copy(
                buffer_ref.at[place_slot, pl.ds(0, size // 2)],
                kept_ref.at[pl.ds(turn * TURN + odd * (size // 2), size // 2)],
                sems.at[place_slot, odd],
            )
            for odd, buffer_ref in enumerate((even_ref, odd_ref))
        ]

    def wait_turn(turn, size=TURN):
        for copy in copies(turn, size):
            copy.wait()

    def form(turn, place, row_block, col_block, times):
        head, tail = form_tile(left_ref[row_block], right_ref[col_block], times)
        buffer_ref = odd_ref if place % 2 else even_ref
        buffer_ref[lax.rem(turn, WRITE_SLOTS), place // 2, 0] = head
        buffer_ref[lax.rem(turn, WRITE_SLOTS), place // 2, 1] = tail

    def kept_tile(turn, place):
        buffer_ref, place_slot = odd_ref if place % 2 else even_ref, lax.rem(turn, WRITE_SLOTS)
        return buffer_ref[place_slot, place // 2, 0], buffer_ref[place_slot, place // 2, 1]

    def multiply(turn, place, size):
        slot = entry_at(turn, place, size)
        row_block, col_block, _ = read_key(list_ref, jnp.maximum(slot - diagonal, 0), blocks)
        on_diagonal = slot < diagonal
        row_block = jnp.where(on_diagonal, diagonal_block(slot), row_block)
        col_block = jnp.where(on_diagonal, diagonal_block(slot), col_block)
        row_to = jnp.where(on_diagonal, blocks, row_block)
        add_products(vector_ref, total_ref, row_block, col_block, row_to, *kept_tile(turn, place))

    def run_diagonal(turn, carry):
        pl.when(turn >= WRITE_SLOTS)(lambda: wait_turn(turn - WRITE_SLOTS))
        for place in range(TURN):
            block = diagonal_block(entry_at(turn, place))
            form(turn, place, block, block, 1.0)
            if place:
                before, tile = entry_at(turn, place - 1), kept_tile(turn, place - 1)
            else:
                before, tile = jnp.maximum(turn * TURN - 1, 0), kept_tile(turn + 1, TURN - 1)
            add_diagonal(vector_ref, total_ref, diagonal_block(before), *tile)
        for copy in copies(turn, TURN, diagonal_ref):
            copy.start()
        return carry

    def run_turn(turn, size):
        wait_turn(turn - WRITE_SLOTS)
        for place in range(size):
            entry = entry_at(turn, place, size) - diagonal
            row_block, col_block, _ = read_key(list_ref, entry, blocks)
            form(turn, place, row_block, col_block, times_ref[0, entry])
            multiply(*((turn, place - 1, size) if place else (turn - 1, TURN - 1, TURN)))
        for copy in copies(turn, size):
            copy.start()

    def run_full(turn, carry):
        run_turn(turn, TURN)
        return carry

    lax.fori_loop(0, diagonal_turns, run_diagonal, 0)
    keys_copy.wait()
    times_copy.wait()
    held = list_ref[0, LISTED - 1]
    turns = diagonal_turns + (held + TURN - HALF - 1) // TURN
    with_half = held > (turns - diagonal_turns) * TURN
    lax.fori_loop(diagonal_turns, turns, run_full, 0)

    @pl.when(with_half)
    def _():
        run_turn(turns, HALF)
        multiply(turns, HALF - 1, HALF)
        wait_turn(turns, HALF)

    @pl.when(jnp.logical_not(with_half))
    def _():
        multiply(turns - 1, TURN - 1, TURN)
        wait_turn(turns - 2)

    finish_first(total_ref, partial_ref, blocks)
    wait_turn(turns - 1)


def form_kernel(
    n_row, n_col, mine_ref, other_ref, list_ref, base_ref, partial_ref, left_ref, right_ref, meta_ref, meta_sems, vector_ref, total_ref
):
    n_dev = n_row * n_col
    blocks = n_dev * BLOCK_DEV
    core = lax.rem(lax.axis_index("row"), 2)
    sources = ((mine_ref, core), (other_ref, 1 - core))
    meta_copies = [
        pltpu.make_async_copy(
            source.at[:, :, POINTS_DEV : POINTS_DEV + LANES], meta_ref.at[source_core], meta_sems.at[index]
        )
        for index, (source, source_core) in enumerate(sources)
    ]
    for copy in meta_copies:
        copy.start()

    def assemble(group, carry):
        assemble_group(n_col, group, sources, base_ref, vector_ref, left_ref, right_ref)
        return carry

    lax.fori_loop(0, n_dev // 2, assemble, 0)
    total_ref[...] = jnp.zeros_like(total_ref)
    for copy in meta_copies:
        copy.wait()

    def read_device(device, carry):
        seen, held = carry
        row = device // n_col
        col = lax.rem(device, n_col)
        source_core, group = lax.rem(row, 2), (row // 2) * n_col + col
        count = meta_ref[source_core, group, 3, LANES - 1].astype(jnp.int32)
        first = lax.rem(seen + core, 2)
        taken = (count - first + 1) // 2

        def read_entry(index, carry):
            slot = first + 2 * index
            row_id = meta_ref[source_core, group, 3, slot].astype(jnp.int32)
            col_id = meta_ref[source_core, group, 7, slot].astype(jnp.int32)
            row_block = row * (n_col * BLOCK_DEV) + row_id
            col_block = ((col_id // BLOCK_DEV) * n_col + col) * BLOCK_DEV + lax.rem(col_id, BLOCK_DEV)
            list_ref[0, held + index] = row_block * blocks + col_block
            return carry

        lax.fori_loop(0, taken, read_entry, 0)
        return seen + count, held + taken

    _, held = lax.fori_loop(0, n_dev, read_device, (0, 0))
    list_ref[0, list_ref.shape[1] - 1] = held
    apply_formed(list_ref, (left_ref, right_ref), vector_ref, total_ref, blocks)
    finish_first(total_ref, partial_ref, blocks)


def apply_formed(list_ref, factor_refs, vector_ref, total_ref, blocks):
    def run_entry(entry, carry):
        row_block, col_block, row_to = read_key(list_ref, entry, blocks)
        head, tail = form_tile(factor_refs[0][row_block], factor_refs[1][col_block], 1.0)
        add_products(vector_ref, total_ref, row_block, col_block, row_to, head, tail)
        return carry

    lax.fori_loop(0, list_ref[0, list_ref.shape[1] - 1], run_entry, 0)


def read_copy(first, count, diagonal, tiles_ref, buffer_ref, sems):
    return pltpu.make_async_copy(
        tiles_ref.at[pl.ds(diagonal + first, count)], buffer_ref.at[pl.ds(first, count)], sems.at[first // HALF]
    )


def start_reads(list_ref, tiles_ref, buffer_ref, sems, blocks):
    diagonal = blocks // 2

    def start(turn, carry):
        read_copy(turn * TURN, TURN, diagonal, tiles_ref, buffer_ref, sems).start()
        return carry

    held = list_ref[0, LISTED - 1]
    full = (held + TURN - HALF - 1) // TURN
    lax.fori_loop(0, full, start, 0)
    pl.when(held > full * TURN)(lambda: read_copy(full * TURN, HALF, diagonal, tiles_ref, buffer_ref, sems).start())


def apply_stored(
    list_ref, diagonal_ref, tiles_ref, buffer_ref, sems, side_ref, vector_ref, total_ref, blocks
):
    held = list_ref[0, LISTED - 1]
    core = lax.rem(lax.axis_index("row"), 2)
    diagonal = blocks // 2

    def run_entries(first, count):
        read_copy(first, count, diagonal, tiles_ref, buffer_ref, sems).wait()
        for place in range(count):
            row_block, col_block, _ = read_key(list_ref, first + place, blocks)
            head, tail = buffer_ref[first + place, 0], buffer_ref[first + place, 1]
            add_mixed_products(vector_ref, total_ref, side_ref, row_block, col_block, head, tail)

    def run_full(turn, carry):
        run_entries(turn * TURN, TURN)
        return carry

    def run_diagonal(turn, carry):
        for place in range(TURN):
            slot = turn * TURN + place
            add_diagonal(vector_ref, total_ref, 2 * slot + core, diagonal_ref[slot, 0], diagonal_ref[slot, 1])
        return carry

    lax.fori_loop(0, diagonal // TURN, run_diagonal, 0)
    full = (held + HALF - 1) // TURN
    lax.fori_loop(0, full, run_full, 0)
    pl.when(held > full * TURN)(lambda: run_entries(full * TURN, HALF))


def apply_tiles(stored, value_ref, list_ref, held_refs, partial_ref, scratch):
    blocks = value_ref.shape[0]
    vector_ref, total_ref = scratch[:2]

    def put_block(block, carry):
        store_pieces(vector_ref, block, value_ref[block], False)
        return carry

    lax.fori_loop(0, blocks, put_block, 0, unroll=32)
    if stored:
        side_ref = scratch[4]
        apply_stored(list_ref, *held_refs, *scratch[2:5], vector_ref, total_ref, blocks)
        place = lax.broadcasted_iota(jnp.int32, (ROWS, 2 * ROWS), 0)
        piece = lax.broadcasted_iota(jnp.int32, (ROWS, 2 * ROWS), 1)
        both_pieces = jnp.where((piece == place) | (piece == place + ROWS), 1.0, 0.0).astype(bf16)

        def finish_block(block, carry):
            turned = lax.dot_general(
                both_pieces, side_ref[block].astype(bf16), (((1,), (1,)), ((), ())), preferred_element_type=f32
            )
            partial_ref[block] = total_ref[block, 0:ROWS] + total_ref[block, ROWS : 2 * ROWS] + turned
            return carry

        lax.fori_loop(0, blocks, finish_block, 0, unroll=32)
    else:
        apply_formed(list_ref, held_refs, vector_ref, total_ref, blocks)
        partial_ref[...] = total_ref[0:blocks, 0:ROWS] + total_ref[0:blocks, ROWS : 2 * ROWS]


def row_sum(value):
    return jnp.sum(jnp.sum(value, axis=0, keepdims=True), axis=2, keepdims=True)


def first_step_kernel(stored, list_ref, mine_ref, other_ref, base_ref, *rest):
    held, rest = rest[:2], rest[2:]
    residual_ref, direction_ref, partial_ref, scalars_ref, *scratch = rest
    if stored:
        start_reads(list_ref, held[1], scratch[2], scratch[3], base_ref.shape[0])
        scratch[4][...] = jnp.zeros_like(scratch[4])
    scratch[1][...] = jnp.zeros_like(scratch[1])
    blocks = base_ref.shape[0]
    largest = jnp.max(mine_ref[blocks:] + other_ref[blocks:])
    base = base_ref[...]
    applied = ridge_shift * base + (mine_ref[0:blocks] + other_ref[0:blocks]) / largest
    norm_now = row_sum(base * base)
    step_size = norm_now / row_sum(base * applied)
    residual = base - step_size * applied
    norm_next = row_sum(residual * residual)
    direction = residual + (norm_next / norm_now) * base
    residual_ref[...] = residual
    direction_ref[...] = direction
    scalars_ref[0] = jnp.broadcast_to(step_size[0], (ROWS, LANES))
    scalars_ref[1] = jnp.broadcast_to(norm_next[0], (ROWS, LANES))
    scalars_ref[2] = jnp.full((ROWS, LANES), largest, f32)
    apply_tiles(stored, direction_ref, list_ref, held, partial_ref, scratch)


def next_step_kernel(
    stored, n_row, n_col, list_ref, mine_ref, other_ref, base_ref, residual_ref, direction_ref, scalars_ref, *rest
):
    held, rest = rest[:2], rest[2:]
    weights_out, residual_out, direction_out, kept_ref, sent_ref, scalars_out, *scratch = rest
    partial_ref = scratch.pop()
    if stored:
        start_reads(list_ref, held[1], scratch[2], scratch[3], base_ref.shape[0])
        scratch[4][...] = jnp.zeros_like(scratch[4])
    scratch[1][...] = jnp.zeros_like(scratch[1])
    step_before = scalars_ref[0:1, :, 0:1]
    norm_now = scalars_ref[1:2, :, 0:1]
    largest = scalars_ref[2:3, :, 0:1]
    direction = direction_ref[...]
    applied = ridge_shift * direction + (mine_ref[...] + other_ref[...]) / largest
    step_size = norm_now / row_sum(direction * applied)
    weights_out[...] = step_before * base_ref[...] + step_size * direction
    residual = residual_ref[...] - step_size * applied
    norm_next = row_sum(residual * residual)
    residual_out[...] = residual
    direction_out[...] = residual + (norm_next / norm_now) * direction
    scalars_out[0] = scalars_ref[0]
    scalars_out[1] = jnp.broadcast_to(norm_next[0], (ROWS, LANES))
    scalars_out[2] = scalars_ref[2]
    apply_tiles(stored, direction_out, list_ref, held, partial_ref, scratch)
    core = lax.rem(lax.axis_index("row"), 2)
    row_blocks = n_col * BLOCK_DEV
    product = row_sum(direction_out[...] * partial_ref[...])[0]
    for pair in range(n_row // 2):
        taken = slice(pair * row_blocks, (pair + 1) * row_blocks)
        kept_ref[taken] = partial_ref[pl.ds((2 * pair + core) * row_blocks, row_blocks)]
        sent_ref[taken] = partial_ref[pl.ds((2 * pair + 1 - core) * row_blocks, row_blocks)]
    kept_ref[kept_ref.shape[0] - 1] = jnp.broadcast_to(product, (ROWS, BLOCK))
    sent_ref[sent_ref.shape[0] - 1] = jnp.broadcast_to(product, (ROWS, BLOCK))


def last_step_kernel(
    n_row, n_col, mine_ref, other_ref, weights_ref, residual_ref, direction_ref, scalars_ref, out_ref
):
    norm_now = scalars_ref[1:2, :, 0:1]
    largest = scalars_ref[2:3, :, 0:1]
    direction = direction_ref[...]
    last = mine_ref.shape[0] - 1
    product = (mine_ref[last:, :, 0:1] + other_ref[last:, :, 0:1]) / largest
    step_size = norm_now / (ridge_shift * row_sum(direction * direction) + product)
    core = lax.rem(lax.axis_index("row"), 2)
    row_blocks = n_col * BLOCK_DEV
    for pair in range(n_row // 2):
        span = pl.ds((2 * pair + core) * row_blocks, row_blocks)
        own = slice(pair * row_blocks, (pair + 1) * row_blocks)
        direction = direction_ref[span]
        applied = ridge_shift * direction + (mine_ref[own] + other_ref[own]) / largest
        weights = weights_ref[span] + step_size * direction
        residual = residual_ref[span] - step_size * applied
        for col in range(n_col):
            start = (pair * n_col + col) * 2 * BLOCK_DEV
            taken = slice(col * BLOCK_DEV, (col + 1) * BLOCK_DEV)
            out_ref[start : start + BLOCK_DEV] = weights[taken]
            out_ref[start + BLOCK_DEV : start + 2 * BLOCK_DEV] = residual[taken]


def unpack_kernel(groups, group_rows, received_ref, weights_ref, residual_ref):
    for group in range(groups):
        rows = slice(group * group_rows, (group + 1) * group_rows)
        for index, target in enumerate((weights_ref, residual_ref)):
            for half in range(BLOCK_DEV):
                target[rows, half * BLOCK : (half + 1) * BLOCK] = received_ref[
                    (2 * group + index) * BLOCK_DEV + half, 0:group_rows
                ]


def call(kernel, out_shape, *args, scratch=(), in_spaces=None, out_spaces=None, vmem=16):
    spaces = in_spaces or [pltpu.VMEM] * len(args)
    outs = out_spaces or jax.tree.map(lambda _: pltpu.VMEM, out_shape)
    return pl.pallas_call(
        kernel,
        out_shape=out_shape,
        in_specs=[pl.BlockSpec(memory_space=space) for space in spaces],
        out_specs=jax.tree.map(lambda space: pl.BlockSpec(memory_space=space), outs),
        scratch_shapes=list(scratch),
        compiler_params=pltpu.CompilerParams(vmem_limit_bytes=vmem * 2**20),
    )(*args)


def local(positions, targets, pairs, counts):
    n_row = lax.axis_size("row")
    n_col = lax.axis_size("col")
    n_dev = n_row * n_col
    blocks = n_dev * BLOCK_DEV
    entries = pairs.shape[1]
    groups = n_dev // 2
    group_rows = targets.shape[0] // groups
    room = -(-(n_dev * entries // 2) // TURN) * TURN
    stored = room <= STORED_MAX and blocks % (2 * TURN) == 0
    same_core = [
        [row * n_col + col for row in range(core, n_row, 2) for col in range(n_col)] for core in range(2)
    ]
    siblings = [(index, index ^ 1) for index in range(n_row)]
    shape = jax.ShapeDtypeStruct
    kept = pltpu.VMEM if stored else shape
    vmem = 52 if stored else 58
    field = kept((blocks, ROWS, BLOCK), f32)
    scalars = kept((3, ROWS, LANES), f32)

    def resident(array):
        return pltpu.with_memory_space_constraint(array, pltpu.VMEM) if stored else array

    def from_sibling(array):
        return resident(lax.ppermute(array, "row", siblings))

    def among_cores(array):
        return resident(
            lax.all_to_all(array, ("row", "col"), 0, 0, axis_index_groups=same_core, tiled=True)
        )

    packed = call(
        functools.partial(pack_kernel, n_row, n_col),
        kept((groups, ROWS, POINTS_DEV + BLOCK), f32),
        targets,
        positions,
        pairs,
        counts,
        in_spaces=[pl.ANY] * 4,
        scratch=[
            pltpu.VMEM(targets.shape, f32),
            pltpu.VMEM(positions.shape, f32),
            pltpu.VMEM(pairs.shape, jnp.int32),
            pltpu.SMEM(counts.shape, jnp.int32),
            pltpu.VMEM((ROWS, BLOCK), f32),
            pltpu.SemaphoreType.DMA((4,)),
        ],
        vmem=60,
    )
    mine = among_cores(resident(packed))
    other = from_sibling(mine)

    factors = [((blocks, BLOCK, PIECE_DEPTH), bf16), ((blocks, PIECE_DEPTH, BLOCK), bf16)]
    factor_scratch = [pltpu.VMEM(*factor) for factor in factors]
    first_partial = kept((blocks + -(-blocks // ROWS), ROWS, BLOCK), f32)
    first_scratch = [
        pltpu.VMEM((blocks, 4 * ROWS, BLOCK), bf16),
        pltpu.VMEM((blocks + 1, 4 * ROWS, BLOCK), f32),
    ]
    step_scratch = [
        pltpu.VMEM((blocks, 2 * ROWS, BLOCK), bf16),
        pltpu.VMEM((blocks + 1, 2 * ROWS, BLOCK), f32),
    ]
    if stored:
        listed, base, partial, *held = call(
            functools.partial(form_stored_kernel, n_row, n_col),
            [
                shape((1, LISTED), jnp.int32),
                field,
                first_partial,
                kept((blocks // 2, 2, BLOCK, BLOCK), bf16),
                shape((room, 2, BLOCK, BLOCK), bf16),
            ],
            mine,
            other,
            out_spaces=[pltpu.SMEM, pltpu.VMEM, pltpu.VMEM, pltpu.VMEM, pl.ANY],
            scratch=[
                pltpu.SMEM((1, LISTED), f32),
                pltpu.VMEM((1, LISTED), jnp.int32),
                pltpu.VMEM((1, LISTED), f32),
                pltpu.SemaphoreType.DMA((2,)),
                *first_scratch,
                *factor_scratch,
                pltpu.SemaphoreType.DMA((WRITE_SLOTS, 2)),
                *[pltpu.VMEM((WRITE_SLOTS, HALF, 2, BLOCK, BLOCK), bf16)] * 2,
            ],
            vmem=vmem,
        )
        held = [resident(held[0]), held[1]]
        held_spaces = [pltpu.VMEM, pl.ANY]
        step_scratch += [
            pltpu.VMEM((room - blocks // 2, 2, BLOCK, BLOCK), bf16),
            pltpu.SemaphoreType.DMA((room // HALF,)),
            pltpu.VMEM((blocks, BLOCK, 2 * ROWS), f32),
        ]
    else:
        listed, base, partial, *held = call(
            functools.partial(form_kernel, n_row, n_col),
            [shape((1, room + 1), jnp.int32), field, first_partial, *(shape(*factor) for factor in factors)],
            mine,
            other,
            out_spaces=[pltpu.SMEM] + [pltpu.VMEM] * 4,
            scratch=[
                pltpu.SMEM((2, n_dev // 2, ROWS, LANES), f32),
                pltpu.SemaphoreType.DMA((2,)),
                *first_scratch,
            ],
            vmem=vmem,
        )
        held_spaces = [pltpu.VMEM] * 2
    base, partial = resident(base), resident(partial)

    def step(kernel, out_shape, *args, more_scratch=()):
        outs = call(
            kernel,
            out_shape,
            listed,
            *args,
            *held,
            in_spaces=[pltpu.SMEM] + [pltpu.VMEM] * len(args) + held_spaces,
            scratch=[*step_scratch, *more_scratch],
            vmem=vmem,
        )
        return [resident(out) for out in outs]

    residual, direction, partial, numbers = step(
        functools.partial(first_step_kernel, stored), (field, field, field, scalars), partial, from_sibling(partial), base
    )
    half_field = kept((blocks // 2 + 1, ROWS, BLOCK), f32)
    weights, residual, direction, partial, sent, numbers = step(
        functools.partial(next_step_kernel, stored, n_row, n_col),
        (field, field, field, half_field, half_field, scalars),
        partial,
        from_sibling(partial),
        base,
        residual,
        direction,
        numbers,
        more_scratch=[pltpu.VMEM((blocks, ROWS, BLOCK), f32)],
    )
    result = call(
        functools.partial(last_step_kernel, n_row, n_col),
        field,
        partial,
        from_sibling(sent),
        weights,
        residual,
        direction,
        numbers,
    )
    home = among_cores(resident(result))
    out = shape(targets.shape, f32)
    return call(functools.partial(unpack_kernel, groups, group_rows), (out, out), home)


def solution(mesh):
    placed = (
        P(None, ("groups", "row", "col")),
        P(None, ("groups", "row", "col")),
        P(None, ("groups", "row", "col")),
        P(("groups", "row", "col")),
    )
    return jax.shard_map(
        local,
        mesh=mesh,
        in_specs=placed,
        out_specs=(P(None, ("groups", "row", "col")), P(None, ("groups", "row", "col"))),
        check_vma=False,
    )
```

```python
import functools

import jax
import jax.numpy as jnp
from jax import lax
from jax.experimental import pallas as pl
from jax.experimental.pallas import tpu as pltpu
from jax.sharding import PartitionSpec as P

BLOCK = 256
BLOCK_DEV = 2
LANES = 128
POINTS_DEV = BLOCK * BLOCK_DEV
ROWS = 8
PIECE_DEPTH = 64
TURN = 8
HALF = TURN // 2
STORED_MAX = 192
LISTED = 256
WRITE_SLOTS = 2

support_radius = 0.5
ridge_shift = 1.5
f32 = jnp.float32
bf16 = jnp.bfloat16


def pack_kernel(
    n_row, n_col, targets_in, positions_in, pairs_in, counts_in, out_ref, targets_ref, positions_ref, pairs_ref, counts_ref, extra_ref, sems
):
    copies = [
        pltpu.make_async_copy(source, kept, sems.at[index])
        for index, (source, kept) in enumerate(
            (
                (positions_in, positions_ref),
                (pairs_in, pairs_ref),
                (counts_in, counts_ref),
                (targets_in, targets_ref),
            )
        )
    ]
    for copy in copies:
        copy.start()
    for copy in copies[:3]:
        copy.wait()
    entries = pairs_ref.shape[1]
    groups = n_row // 2 * n_col
    group_rows = targets_ref.shape[0] // groups
    lane = lax.broadcasted_iota(jnp.int32, (1, BLOCK), 1)
    for half in range(BLOCK_DEV):
        extra_ref[4 * half : 4 * half + 3, :] = positions_ref[:, half * BLOCK : (half + 1) * BLOCK]
    extra_ref[3:4, :] = jnp.where(lane == LANES - 1, counts_ref[0], 0).astype(f32)
    extra_ref[7:8, :] = jnp.zeros((1, BLOCK), f32)
    extra_ref[3:4, 0:entries] = pairs_ref[0:1, :].astype(f32)
    extra_ref[7:8, 0:entries] = pairs_ref[1:2, :].astype(f32)
    copies[3].wait()
    for group in range(groups):
        if group_rows < ROWS:
            out_ref[group, :, 0:POINTS_DEV] = jnp.zeros((ROWS, POINTS_DEV), f32)
        out_ref[group, 0:group_rows, 0:POINTS_DEV] = targets_ref[group * group_rows : (group + 1) * group_rows, :]
        out_ref[group, :, POINTS_DEV : POINTS_DEV + BLOCK] = extra_ref[...]


def split(value, pieces):
    found = []
    for _ in range(pieces):
        piece = value.astype(bf16).astype(f32)
        found.append(piece)
        value = value - piece
    return found


def point_factors(extra, half):
    row = lax.broadcasted_iota(jnp.int32, (ROWS, BLOCK), 0)
    coords = pltpu.roll(extra, 4, 0) if half else extra
    coords = jnp.where(row < 3, (coords - 0.5) * (1.0 / support_radius), 0.0)
    first, second, third = split(coords, 3)
    norm = jnp.sum(coords * coords, axis=0, keepdims=True)
    norm_pieces = split(jnp.broadcast_to(norm, (ROWS, BLOCK)), 3)
    zero = jnp.zeros((ROWS, BLOCK), f32)
    norms = jnp.where(
        row == 0, norm_pieces[0], jnp.where(row == 1, norm_pieces[1], jnp.where(row == 2, norm_pieces[2], zero))
    )
    ones = jnp.where(row < 3, 1.0, 0.0).astype(f32)
    left = jnp.concatenate([first, first, second, second, first, third, norms, ones], axis=0)
    right = jnp.concatenate(
        [-2.0 * piece for piece in (first, second, first, second, third, first)] + [ones, norms], axis=0
    )
    return left, right


def form_tile(left, right, times):
    square = jnp.maximum(jnp.dot(left, right, preferred_element_type=f32), 1e-30)
    remain = jnp.maximum(1.0 - square * lax.rsqrt(square), 0.0)
    remain_two = remain * remain
    tile = remain_two * remain_two * (1.25 * times - times * remain)
    head = tile.astype(bf16)
    return head, (tile - head.astype(f32)).astype(bf16)


def add_diagonal(vector_ref, total_ref, block, head, tail):
    vector = vector_ref[block]
    total_ref[block] += jnp.dot(vector, head, preferred_element_type=f32) + jnp.dot(
        vector, tail, preferred_element_type=f32
    )


def add_products(vector_ref, total_ref, row_block, col_block, row_to, head, tail):
    over_cols = (((1,), (1,)), ((), ()))
    row_vector, col_vector = vector_ref[row_block], vector_ref[col_block]
    to_cols = jnp.dot(row_vector, head, preferred_element_type=f32) + jnp.dot(
        row_vector, tail, preferred_element_type=f32
    )
    to_rows = lax.dot_general(col_vector, head, over_cols, preferred_element_type=f32) + lax.dot_general(
        col_vector, tail, over_cols, preferred_element_type=f32
    )
    total_ref[col_block] += to_cols
    total_ref[row_to] += to_rows


def add_mixed_products(vector_ref, total_ref, side_ref, row_block, col_block, head, tail):
    over_cols = (((1,), (1,)), ((), ()))
    row_vector, col_vector = vector_ref[row_block], vector_ref[col_block]
    total_ref[col_block] += jnp.dot(row_vector, head, preferred_element_type=f32) + jnp.dot(
        row_vector, tail, preferred_element_type=f32
    )
    total_ref[row_block] += lax.dot_general(col_vector, head, over_cols, preferred_element_type=f32)
    side_ref[row_block] += lax.dot_general(tail, col_vector, over_cols, preferred_element_type=f32)


def store_pieces(vector_ref, block, value, with_ones):
    parts = split(value, 2)
    if with_ones:
        row = lax.broadcasted_iota(jnp.int32, (2 * ROWS, BLOCK), 0)
        parts.append(jnp.where(row == 0, 1.0, 0.0).astype(f32))
    vector_ref[block] = jnp.concatenate(parts, axis=0).astype(bf16)


def global_blocks(n_col, source, group, core):
    row_ids = source[group, 3:4, POINTS_DEV : POINTS_DEV + LANES].astype(jnp.int32)
    col_ids = source[group, 7:8, POINTS_DEV : POINTS_DEV + LANES].astype(jnp.int32)
    count = row_ids[:, LANES - 1 :]
    row, col = 2 * (group // n_col) + core, group % n_col
    in_use = lax.broadcasted_iota(jnp.int32, (1, LANES), 1) < count
    row_block = row * (n_col * BLOCK_DEV) + row_ids
    col_block = ((col_ids >> 1) * n_col + col) * BLOCK_DEV + (col_ids & 1)
    return jnp.minimum(row_block, col_block), jnp.maximum(row_block, col_block), in_use


def merged_list(n_dev, n_col, core, sources, keys_ref, times_ref):
    blocks = n_dev * BLOCK_DEV
    block_id = lax.broadcasted_iota(jnp.int32, (blocks, LANES), 0)
    smaller, larger = [], []
    for source, source_core in sources:
        for group in range(n_dev // 2):
            low, high, in_use = global_blocks(n_col, source, group, source_core)
            smaller.append(jnp.where((block_id == low) & in_use, 1.0, 0.0))
            larger.append(jnp.where((block_id == high) & in_use, 1.0, 0.0))
    over_lanes = (((1,), (1,)), ((), ()))
    times = lax.dot_general(
        jnp.concatenate(larger, axis=1).astype(bf16),
        jnp.concatenate(smaller, axis=1).astype(bf16),
        over_lanes,
        preferred_element_type=f32,
    )
    high_id = lax.broadcasted_iota(jnp.int32, (blocks, blocks), 0)
    low_id = lax.broadcasted_iota(jnp.int32, (blocks, blocks), 1)
    present = jnp.where((times > 0.0) & (high_id > low_id), 1.0, 0.0)
    before = jnp.where(high_id > low_id, 1.0, 0.0).astype(bf16)
    present_low = present.astype(bf16)
    in_column = jnp.dot(before, present_low, preferred_element_type=f32)
    column_sums = jnp.sum(present, axis=0, keepdims=True)
    column_starts = lax.dot_general(
        jnp.broadcast_to(column_sums, (ROWS, blocks)).astype(bf16), before, over_lanes, preferred_element_type=f32
    )[0:1]
    place = (in_column + column_starts).astype(jnp.int32)
    mine = (present > 0.0) & ((place & 1) == core)
    slot = jnp.where(mine, place >> 1, -1)
    value = (low_id * blocks + high_id).astype(f32) + float(blocks * blocks) * times
    lane = lax.broadcasted_iota(jnp.int32, (blocks, LISTED), 1)
    values = jnp.zeros((blocks, LISTED), f32)
    for low in range(blocks):
        values = values + jnp.where(lane == slot[:, low : low + 1], value[:, low : low + 1], 0.0)
    listed = jnp.sum(values, axis=0, keepdims=True).astype(jnp.int32)
    held = jnp.sum(jnp.where(mine, 1.0, 0.0), axis=1, keepdims=True)
    held = jnp.sum(held, axis=0, keepdims=True).astype(jnp.int32)
    first_lane = lax.broadcasted_iota(jnp.int32, (1, LISTED), 1)
    keys_ref[...] = jnp.where(first_lane == LISTED - 1, held, lax.rem(listed, blocks * blocks))
    times_ref[...] = lax.div(listed, blocks * blocks).astype(f32)


def read_key(list_ref, slot, blocks):
    key = list_ref[0, slot]
    row_block, col_block = lax.div(key, blocks), lax.rem(key, blocks)
    return row_block, col_block, jnp.where(row_block == col_block, blocks, row_block)


def assemble_group(n_col, group, sources, base_ref, vector_ref, left_ref, right_ref):
    for source, source_core in sources:
        device = (2 * (group // n_col) + source_core) * n_col + lax.rem(group, n_col)
        extra = source[group, :, POINTS_DEV : POINTS_DEV + BLOCK]
        for half in range(BLOCK_DEV):
            block = BLOCK_DEV * device + half
            values = source[group, :, half * BLOCK : (half + 1) * BLOCK]
            base_ref[block] = values
            store_pieces(vector_ref, block, values, True)
            left, right = point_factors(extra, half)
            left_ref[block] = left.T.astype(bf16)
            right_ref[block] = right.astype(bf16)


def finish_first(total_ref, partial_ref, blocks):
    for block in range(blocks):
        partial_ref[block] = total_ref[block, 0:ROWS] + total_ref[block, ROWS : 2 * ROWS]
        partial_ref[blocks + block // ROWS, block % ROWS : block % ROWS + 1, :] = total_ref[
            block, 2 * ROWS : 2 * ROWS + 1
        ]


def own_block(slot, core, n_col):
    group = slot // BLOCK_DEV
    device = (2 * (group // n_col) + core) * n_col + lax.rem(group, n_col)
    return BLOCK_DEV * device + lax.rem(slot, BLOCK_DEV)


def diagonal_kernel(
    mine_ref, diagonal_ref, own_total_ref, vector_ref, left_ref, right_ref, sems, even_ref, odd_ref
):
    def assemble(group, carry):
        extra = mine_ref[group, :, POINTS_DEV : POINTS_DEV + BLOCK]
        for half in range(BLOCK_DEV):
            slot = BLOCK_DEV * group + half
            store_pieces(vector_ref, slot, mine_ref[group, :, half * BLOCK : (half + 1) * BLOCK], True)
            left, right = point_factors(extra, half)
            left_ref[slot] = left.T.astype(bf16)
            right_ref[slot] = right.astype(bf16)
        return carry

    lax.fori_loop(0, mine_ref.shape[0], assemble, 0, unroll=4)
    own_total_ref[...] = jnp.zeros_like(own_total_ref)
    odd_ref[WRITE_SLOTS - 1, HALF - 1] = jnp.zeros(odd_ref.shape[2:], bf16)

    def copies(turn):
        place_slot = lax.rem(turn, WRITE_SLOTS)
        return [
            pltpu.make_async_copy(
                buffer_ref.at[place_slot],
                diagonal_ref.at[pl.ds(turn * TURN + odd * HALF, HALF)],
                sems.at[place_slot, odd],
            )
            for odd, buffer_ref in enumerate((even_ref, odd_ref))
        ]

    def wait_turn(turn):
        for copy in copies(turn):
            copy.wait()

    def slot_at(turn, place):
        return turn * TURN + place % 2 * HALF + place // 2

    def multiply(slot, place, place_slot):
        buffer_ref = odd_ref if place % 2 else even_ref
        head, tail = buffer_ref[place_slot, place // 2, 0], buffer_ref[place_slot, place // 2, 1]
        add_diagonal(vector_ref, own_total_ref, slot, head, tail)

    def run_turn(turn, carry):
        place_slot = lax.rem(turn, WRITE_SLOTS)
        pl.when(turn >= WRITE_SLOTS)(lambda: wait_turn(turn - WRITE_SLOTS))
        for place in range(TURN):
            slot = slot_at(turn, place)
            head, tail = form_tile(left_ref[slot], right_ref[slot], 1.0)
            buffer_ref = odd_ref if place % 2 else even_ref
            buffer_ref[place_slot, place // 2, 0] = head
            buffer_ref[place_slot, place // 2, 1] = tail
            if place:
                multiply(slot_at(turn, place - 1), place - 1, place_slot)
            else:
                multiply(jnp.maximum(turn * TURN - 1, 0), TURN - 1, WRITE_SLOTS - 1 - place_slot)
        for copy in copies(turn):
            copy.start()
        return carry

    turns = diagonal_ref.shape[0] // TURN
    lax.fori_loop(0, turns, run_turn, 0)
    multiply(turns * TURN - 1, TURN - 1, (turns - 1) % WRITE_SLOTS)
    for turn in range(max(turns - WRITE_SLOTS, 0), turns):
        wait_turn(turn)


def form_stored_kernel(
    n_row,
    n_col,
    mine_ref,
    other_ref,
    own_total_ref,
    list_ref,
    base_ref,
    partial_ref,
    tiles_ref,
    times_ref,
    keys_vector,
    times_vector,
    list_sems,
    vector_ref,
    total_ref,
    left_ref,
    right_ref,
    sems,
    even_ref,
    odd_ref,
):
    n_dev = n_row * n_col
    blocks = n_dev * BLOCK_DEV
    core = lax.rem(lax.axis_index("row"), 2)
    sources = ((mine_ref, core), (other_ref, 1 - core))
    merged_list(n_dev, n_col, core, sources, keys_vector, times_vector)
    keys_copy = pltpu.make_async_copy(keys_vector, list_ref, list_sems.at[0])
    times_copy = pltpu.make_async_copy(times_vector, times_ref, list_sems.at[1])
    keys_copy.start()
    times_copy.start()

    def assemble(group, carry):
        assemble_group(n_col, group, sources, base_ref, vector_ref, left_ref, right_ref)
        return carry

    lax.fori_loop(0, n_dev // 2, assemble, 0, unroll=4)
    total_ref[...] = jnp.zeros_like(total_ref)
    for slot in range(blocks // 2):
        total_ref[own_block(slot, core, n_col)] = own_total_ref[slot]
    odd_ref[WRITE_SLOTS - 1, HALF - 1] = jnp.zeros(odd_ref.shape[2:], bf16)
    diagonal = blocks // 2
    diagonal_turns = diagonal // TURN

    def entry_at(turn, place, size=TURN):
        return turn * TURN + place % 2 * (size // 2) + place // 2

    def copies(turn, size=TURN):
        place_slot = lax.rem(turn, WRITE_SLOTS)
        return [
            pltpu.make_async_copy(
                buffer_ref.at[place_slot, pl.ds(0, size // 2)],
                tiles_ref.at[pl.ds(turn * TURN + odd * (size // 2), size // 2)],
                sems.at[place_slot, odd],
            )
            for odd, buffer_ref in enumerate((even_ref, odd_ref))
        ]

    def wait_turn(turn, size=TURN):
        for copy in copies(turn, size):
            copy.wait()

    def form(turn, place, row_block, col_block, times):
        head, tail = form_tile(left_ref[row_block], right_ref[col_block], times)
        buffer_ref = odd_ref if place % 2 else even_ref
        buffer_ref[lax.rem(turn, WRITE_SLOTS), place // 2, 0] = head
        buffer_ref[lax.rem(turn, WRITE_SLOTS), place // 2, 1] = tail

    def kept_tile(turn, place):
        buffer_ref, place_slot = odd_ref if place % 2 else even_ref, lax.rem(turn, WRITE_SLOTS)
        return buffer_ref[place_slot, place // 2, 0], buffer_ref[place_slot, place // 2, 1]

    def multiply(turn, place, size):
        entry = jnp.maximum(entry_at(turn, place, size) - diagonal, 0)
        row_block, col_block, _ = read_key(list_ref, entry, blocks)
        add_products(vector_ref, total_ref, row_block, col_block, row_block, *kept_tile(turn, place))

    def run_turn(turn, size):
        pl.when(turn >= diagonal_turns + WRITE_SLOTS)(lambda: wait_turn(turn - WRITE_SLOTS))
        for place in range(size):
            entry = entry_at(turn, place, size) - diagonal
            row_block, col_block, _ = read_key(list_ref, entry, blocks)
            form(turn, place, row_block, col_block, times_ref[0, entry])
            multiply(*((turn, place - 1, size) if place else (turn - 1, TURN - 1, TURN)))
        for copy in copies(turn, size):
            copy.start()

    def run_full(turn, carry):
        run_turn(turn, TURN)
        return carry

    keys_copy.wait()
    times_copy.wait()
    held = list_ref[0, LISTED - 1]
    turns = diagonal_turns + (held + TURN - HALF - 1) // TURN
    with_half = held > (turns - diagonal_turns) * TURN
    lax.fori_loop(diagonal_turns, turns, run_full, 0)

    @pl.when(with_half)
    def _():
        run_turn(turns, HALF)
        multiply(turns, HALF - 1, HALF)
        wait_turn(turns, HALF)

    @pl.when(jnp.logical_not(with_half))
    def _():
        multiply(turns - 1, TURN - 1, TURN)
        pl.when(turns >= diagonal_turns + 2)(lambda: wait_turn(turns - 2))

    finish_first(total_ref, partial_ref, blocks)
    pl.when(turns > diagonal_turns)(lambda: wait_turn(turns - 1))


def form_kernel(
    n_row, n_col, mine_ref, other_ref, list_ref, base_ref, partial_ref, left_ref, right_ref, meta_ref, meta_sems, vector_ref, total_ref
):
    n_dev = n_row * n_col
    blocks = n_dev * BLOCK_DEV
    core = lax.rem(lax.axis_index("row"), 2)
    sources = ((mine_ref, core), (other_ref, 1 - core))
    meta_copies = [
        pltpu.make_async_copy(
            source.at[:, :, POINTS_DEV : POINTS_DEV + LANES], meta_ref.at[source_core], meta_sems.at[index]
        )
        for index, (source, source_core) in enumerate(sources)
    ]
    for copy in meta_copies:
        copy.start()

    def assemble(group, carry):
        assemble_group(n_col, group, sources, base_ref, vector_ref, left_ref, right_ref)
        return carry

    lax.fori_loop(0, n_dev // 2, assemble, 0)
    total_ref[...] = jnp.zeros_like(total_ref)
    for copy in meta_copies:
        copy.wait()

    def read_device(device, carry):
        seen, held = carry
        row = device // n_col
        col = lax.rem(device, n_col)
        source_core, group = lax.rem(row, 2), (row // 2) * n_col + col
        count = meta_ref[source_core, group, 3, LANES - 1].astype(jnp.int32)
        first = lax.rem(seen + core, 2)
        taken = (count - first + 1) // 2

        def read_entry(index, carry):
            slot = first + 2 * index
            row_id = meta_ref[source_core, group, 3, slot].astype(jnp.int32)
            col_id = meta_ref[source_core, group, 7, slot].astype(jnp.int32)
            row_block = row * (n_col * BLOCK_DEV) + row_id
            col_block = ((col_id // BLOCK_DEV) * n_col + col) * BLOCK_DEV + lax.rem(col_id, BLOCK_DEV)
            list_ref[0, held + index] = row_block * blocks + col_block
            return carry

        lax.fori_loop(0, taken, read_entry, 0)
        return seen + count, held + taken

    _, held = lax.fori_loop(0, n_dev, read_device, (0, 0))
    list_ref[0, list_ref.shape[1] - 1] = held
    apply_formed(list_ref, (left_ref, right_ref), vector_ref, total_ref, blocks)
    finish_first(total_ref, partial_ref, blocks)


def apply_formed(list_ref, factor_refs, vector_ref, total_ref, blocks):
    def run_entry(entry, carry):
        row_block, col_block, row_to = read_key(list_ref, entry, blocks)
        head, tail = form_tile(factor_refs[0][row_block], factor_refs[1][col_block], 1.0)
        add_products(vector_ref, total_ref, row_block, col_block, row_to, head, tail)
        return carry

    lax.fori_loop(0, list_ref[0, list_ref.shape[1] - 1], run_entry, 0)


def read_copy(first, count, diagonal, tiles_ref, buffer_ref, sems):
    return pltpu.make_async_copy(
        tiles_ref.at[pl.ds(diagonal + first, count)], buffer_ref.at[pl.ds(first, count)], sems.at[first // HALF]
    )


def start_reads(list_ref, tiles_ref, buffer_ref, sems, blocks):
    diagonal = blocks // 2

    def start(turn, carry):
        read_copy(turn * TURN, TURN, diagonal, tiles_ref, buffer_ref, sems).start()
        return carry

    held = list_ref[0, LISTED - 1]
    full = (held + TURN - HALF - 1) // TURN
    lax.fori_loop(0, full, start, 0)
    pl.when(held > full * TURN)(lambda: read_copy(full * TURN, HALF, diagonal, tiles_ref, buffer_ref, sems).start())


def apply_stored(
    list_ref, diagonal_ref, tiles_ref, buffer_ref, sems, side_ref, vector_ref, total_ref, blocks
):
    held = list_ref[0, LISTED - 1]
    core = lax.rem(lax.axis_index("row"), 2)
    diagonal = blocks // 2

    def run_entries(first, count):
        read_copy(first, count, diagonal, tiles_ref, buffer_ref, sems).wait()
        for place in range(count):
            row_block, col_block, _ = read_key(list_ref, first + place, blocks)
            head, tail = buffer_ref[first + place, 0], buffer_ref[first + place, 1]
            add_mixed_products(vector_ref, total_ref, side_ref, row_block, col_block, head, tail)

    def run_full(turn, carry):
        run_entries(turn * TURN, TURN)
        return carry

    def run_diagonal(turn, carry):
        for place in range(TURN):
            slot = turn * TURN + place
            block = own_block(slot, core, lax.axis_size("col"))
            add_diagonal(vector_ref, total_ref, block, diagonal_ref[slot, 0], diagonal_ref[slot, 1])
        return carry

    lax.fori_loop(0, diagonal // TURN, run_diagonal, 0)
    full = (held + HALF - 1) // TURN
    lax.fori_loop(0, full, run_full, 0)
    pl.when(held > full * TURN)(lambda: run_entries(full * TURN, HALF))


def apply_tiles(stored, value_ref, list_ref, held_refs, partial_ref, scratch):
    blocks = value_ref.shape[0]
    vector_ref, total_ref = scratch[:2]

    def put_block(block, carry):
        store_pieces(vector_ref, block, value_ref[block], False)
        return carry

    lax.fori_loop(0, blocks, put_block, 0, unroll=32)
    if stored:
        side_ref = scratch[4]
        apply_stored(list_ref, *held_refs, *scratch[2:5], vector_ref, total_ref, blocks)
        place = lax.broadcasted_iota(jnp.int32, (ROWS, 2 * ROWS), 0)
        piece = lax.broadcasted_iota(jnp.int32, (ROWS, 2 * ROWS), 1)
        both_pieces = jnp.where((piece == place) | (piece == place + ROWS), 1.0, 0.0).astype(bf16)

        def finish_block(block, carry):
            turned = lax.dot_general(
                both_pieces, side_ref[block].astype(bf16), (((1,), (1,)), ((), ())), preferred_element_type=f32
            )
            partial_ref[block] = total_ref[block, 0:ROWS] + total_ref[block, ROWS : 2 * ROWS] + turned
            return carry

        lax.fori_loop(0, blocks, finish_block, 0, unroll=32)
    else:
        apply_formed(list_ref, held_refs, vector_ref, total_ref, blocks)
        partial_ref[...] = total_ref[0:blocks, 0:ROWS] + total_ref[0:blocks, ROWS : 2 * ROWS]


def row_sum(value):
    return jnp.sum(jnp.sum(value, axis=0, keepdims=True), axis=2, keepdims=True)


def first_step_kernel(stored, list_ref, mine_ref, other_ref, base_ref, *rest):
    held, rest = rest[:2], rest[2:]
    residual_ref, direction_ref, partial_ref, scalars_ref, *scratch = rest
    if stored:
        start_reads(list_ref, held[1], scratch[2], scratch[3], base_ref.shape[0])
        scratch[4][...] = jnp.zeros_like(scratch[4])
    scratch[1][...] = jnp.zeros_like(scratch[1])
    blocks = base_ref.shape[0]
    largest = jnp.max(mine_ref[blocks:] + other_ref[blocks:])
    base = base_ref[...]
    applied = ridge_shift * base + (mine_ref[0:blocks] + other_ref[0:blocks]) / largest
    norm_now = row_sum(base * base)
    step_size = norm_now / row_sum(base * applied)
    residual = base - step_size * applied
    norm_next = row_sum(residual * residual)
    direction = residual + (norm_next / norm_now) * base
    residual_ref[...] = residual
    direction_ref[...] = direction
    scalars_ref[0] = jnp.broadcast_to(step_size[0], (ROWS, LANES))
    scalars_ref[1] = jnp.broadcast_to(norm_next[0], (ROWS, LANES))
    scalars_ref[2] = jnp.full((ROWS, LANES), largest, f32)
    apply_tiles(stored, direction_ref, list_ref, held, partial_ref, scratch)


def next_step_kernel(
    stored, n_row, n_col, list_ref, mine_ref, other_ref, base_ref, residual_ref, direction_ref, scalars_ref, *rest
):
    held, rest = rest[:2], rest[2:]
    weights_out, residual_out, direction_out, kept_ref, sent_ref, scalars_out, *scratch = rest
    partial_ref = scratch.pop()
    if stored:
        start_reads(list_ref, held[1], scratch[2], scratch[3], base_ref.shape[0])
        scratch[4][...] = jnp.zeros_like(scratch[4])
    scratch[1][...] = jnp.zeros_like(scratch[1])
    step_before = scalars_ref[0:1, :, 0:1]
    norm_now = scalars_ref[1:2, :, 0:1]
    largest = scalars_ref[2:3, :, 0:1]
    direction = direction_ref[...]
    applied = ridge_shift * direction + (mine_ref[...] + other_ref[...]) / largest
    step_size = norm_now / row_sum(direction * applied)
    weights_out[...] = step_before * base_ref[...] + step_size * direction
    residual = residual_ref[...] - step_size * applied
    norm_next = row_sum(residual * residual)
    residual_out[...] = residual
    direction_out[...] = residual + (norm_next / norm_now) * direction
    scalars_out[0] = scalars_ref[0]
    scalars_out[1] = jnp.broadcast_to(norm_next[0], (ROWS, LANES))
    scalars_out[2] = scalars_ref[2]
    apply_tiles(stored, direction_out, list_ref, held, partial_ref, scratch)
    core = lax.rem(lax.axis_index("row"), 2)
    row_blocks = n_col * BLOCK_DEV
    product = row_sum(direction_out[...] * partial_ref[...])[0]
    for pair in range(n_row // 2):
        taken = slice(pair * row_blocks, (pair + 1) * row_blocks)
        kept_ref[taken] = partial_ref[pl.ds((2 * pair + core) * row_blocks, row_blocks)]
        sent_ref[taken] = partial_ref[pl.ds((2 * pair + 1 - core) * row_blocks, row_blocks)]
    kept_ref[kept_ref.shape[0] - 1] = jnp.broadcast_to(product, (ROWS, BLOCK))
    sent_ref[sent_ref.shape[0] - 1] = jnp.broadcast_to(product, (ROWS, BLOCK))


def last_step_kernel(
    n_row, n_col, mine_ref, other_ref, weights_ref, residual_ref, direction_ref, scalars_ref, out_ref
):
    norm_now = scalars_ref[1:2, :, 0:1]
    largest = scalars_ref[2:3, :, 0:1]
    direction = direction_ref[...]
    last = mine_ref.shape[0] - 1
    product = (mine_ref[last:, :, 0:1] + other_ref[last:, :, 0:1]) / largest
    step_size = norm_now / (ridge_shift * row_sum(direction * direction) + product)
    core = lax.rem(lax.axis_index("row"), 2)
    row_blocks = n_col * BLOCK_DEV
    for pair in range(n_row // 2):
        span = pl.ds((2 * pair + core) * row_blocks, row_blocks)
        own = slice(pair * row_blocks, (pair + 1) * row_blocks)
        direction = direction_ref[span]
        applied = ridge_shift * direction + (mine_ref[own] + other_ref[own]) / largest
        weights = weights_ref[span] + step_size * direction
        residual = residual_ref[span] - step_size * applied
        for col in range(n_col):
            start = (pair * n_col + col) * 2 * BLOCK_DEV
            taken = slice(col * BLOCK_DEV, (col + 1) * BLOCK_DEV)
            out_ref[start : start + BLOCK_DEV] = weights[taken]
            out_ref[start + BLOCK_DEV : start + 2 * BLOCK_DEV] = residual[taken]


def unpack_kernel(groups, group_rows, received_ref, weights_ref, residual_ref):
    for group in range(groups):
        rows = slice(group * group_rows, (group + 1) * group_rows)
        for index, target in enumerate((weights_ref, residual_ref)):
            for half in range(BLOCK_DEV):
                target[rows, half * BLOCK : (half + 1) * BLOCK] = received_ref[
                    (2 * group + index) * BLOCK_DEV + half, 0:group_rows
                ]


def call(kernel, out_shape, *args, scratch=(), in_spaces=None, out_spaces=None, vmem=16, cost=None):
    spaces = in_spaces or [pltpu.VMEM] * len(args)
    outs = out_spaces or jax.tree.map(lambda _: pltpu.VMEM, out_shape)
    return pl.pallas_call(
        kernel,
        out_shape=out_shape,
        in_specs=[pl.BlockSpec(memory_space=space) for space in spaces],
        out_specs=jax.tree.map(lambda space: pl.BlockSpec(memory_space=space), outs),
        scratch_shapes=list(scratch),
        cost_estimate=cost,
        compiler_params=pltpu.CompilerParams(vmem_limit_bytes=vmem * 2**20),
    )(*args)


def local(positions, targets, pairs, counts):
    n_row = lax.axis_size("row")
    n_col = lax.axis_size("col")
    n_dev = n_row * n_col
    blocks = n_dev * BLOCK_DEV
    entries = pairs.shape[1]
    groups = n_dev // 2
    group_rows = targets.shape[0] // groups
    room = -(-(n_dev * entries // 2) // TURN) * TURN
    stored = room <= STORED_MAX and blocks % (2 * TURN) == 0
    same_core = [
        [row * n_col + col for row in range(core, n_row, 2) for col in range(n_col)] for core in range(2)
    ]
    siblings = [(index, index ^ 1) for index in range(n_row)]
    shape = jax.ShapeDtypeStruct
    kept = pltpu.VMEM if stored else shape
    vmem = 52 if stored else 58
    field = kept((blocks, ROWS, BLOCK), f32)
    scalars = kept((3, ROWS, LANES), f32)

    def resident(array):
        return pltpu.with_memory_space_constraint(array, pltpu.VMEM) if stored else array

    def from_sibling(array):
        return resident(lax.ppermute(array, "row", siblings))

    def among_cores(array):
        return resident(
            lax.all_to_all(array, ("row", "col"), 0, 0, axis_index_groups=same_core, tiled=True)
        )

    packed = call(
        functools.partial(pack_kernel, n_row, n_col),
        kept((groups, ROWS, POINTS_DEV + BLOCK), f32),
        targets,
        positions,
        pairs,
        counts,
        in_spaces=[pl.ANY] * 4,
        scratch=[
            pltpu.VMEM(targets.shape, f32),
            pltpu.VMEM(positions.shape, f32),
            pltpu.VMEM(pairs.shape, jnp.int32),
            pltpu.SMEM(counts.shape, jnp.int32),
            pltpu.VMEM((ROWS, BLOCK), f32),
            pltpu.SemaphoreType.DMA((4,)),
        ],
        vmem=60,
    )
    mine = among_cores(resident(packed))
    other = from_sibling(mine)

    factors = [((blocks, BLOCK, PIECE_DEPTH), bf16), ((blocks, PIECE_DEPTH, BLOCK), bf16)]
    factor_scratch = [pltpu.VMEM(*factor) for factor in factors]
    first_partial = kept((blocks + -(-blocks // ROWS), ROWS, BLOCK), f32)
    first_scratch = [
        pltpu.VMEM((blocks, 4 * ROWS, BLOCK), bf16),
        pltpu.VMEM((blocks + 1, 4 * ROWS, BLOCK), f32),
    ]
    step_scratch = [
        pltpu.VMEM((blocks, 2 * ROWS, BLOCK), bf16),
        pltpu.VMEM((blocks + 1, 2 * ROWS, BLOCK), f32),
    ]
    if stored:
        pair_buffers = [
            pltpu.SemaphoreType.DMA((WRITE_SLOTS, 2)),
            *[pltpu.VMEM((WRITE_SLOTS, HALF, 2, BLOCK, BLOCK), bf16)] * 2,
        ]
        own = blocks // 2
        diagonal_tiles, own_total = call(
            diagonal_kernel,
            [kept((own, 2, BLOCK, BLOCK), bf16), kept((own, 4 * ROWS, BLOCK), f32)],
            mine,
            scratch=[
                pltpu.VMEM((own, 4 * ROWS, BLOCK), bf16),
                *[pltpu.VMEM((own, *factor[1:]), kind) for factor, kind in factors],
                *pair_buffers,
            ],
            vmem=24,
            cost=pl.CostEstimate(flops=10**9, bytes_accessed=10**6, transcendentals=0),
        )
        listed, base, partial, tiles = call(
            functools.partial(form_stored_kernel, n_row, n_col),
            [
                shape((1, LISTED), jnp.int32),
                field,
                first_partial,
                shape((room, 2, BLOCK, BLOCK), bf16),
            ],
            mine,
            other,
            resident(own_total),
            out_spaces=[pltpu.SMEM, pltpu.VMEM, pltpu.VMEM, pl.ANY],
            scratch=[
                pltpu.SMEM((1, LISTED), f32),
                pltpu.VMEM((1, LISTED), jnp.int32),
                pltpu.VMEM((1, LISTED), f32),
                pltpu.SemaphoreType.DMA((2,)),
                *first_scratch,
                *factor_scratch,
                *pair_buffers,
            ],
            vmem=vmem,
        )
        held = [resident(diagonal_tiles), tiles]
        held_spaces = [pltpu.VMEM, pl.ANY]
        step_scratch += [
            pltpu.VMEM((room - blocks // 2, 2, BLOCK, BLOCK), bf16),
            pltpu.SemaphoreType.DMA((room // HALF,)),
            pltpu.VMEM((blocks, BLOCK, 2 * ROWS), f32),
        ]
    else:
        listed, base, partial, *held = call(
            functools.partial(form_kernel, n_row, n_col),
            [shape((1, room + 1), jnp.int32), field, first_partial, *(shape(*factor) for factor in factors)],
            mine,
            other,
            out_spaces=[pltpu.SMEM] + [pltpu.VMEM] * 4,
            scratch=[
                pltpu.SMEM((2, n_dev // 2, ROWS, LANES), f32),
                pltpu.SemaphoreType.DMA((2,)),
                *first_scratch,
            ],
            vmem=vmem,
        )
        held_spaces = [pltpu.VMEM] * 2
    base, partial = resident(base), resident(partial)

    def step(kernel, out_shape, *args, more_scratch=()):
        outs = call(
            kernel,
            out_shape,
            listed,
            *args,
            *held,
            in_spaces=[pltpu.SMEM] + [pltpu.VMEM] * len(args) + held_spaces,
            scratch=[*step_scratch, *more_scratch],
            vmem=vmem,
        )
        return [resident(out) for out in outs]

    residual, direction, partial, numbers = step(
        functools.partial(first_step_kernel, stored), (field, field, field, scalars), partial, from_sibling(partial), base
    )
    half_field = kept((blocks // 2 + 1, ROWS, BLOCK), f32)
    weights, residual, direction, partial, sent, numbers = step(
        functools.partial(next_step_kernel, stored, n_row, n_col),
        (field, field, field, half_field, half_field, scalars),
        partial,
        from_sibling(partial),
        base,
        residual,
        direction,
        numbers,
        more_scratch=[pltpu.VMEM((blocks, ROWS, BLOCK), f32)],
    )
    result = call(
        functools.partial(last_step_kernel, n_row, n_col),
        field,
        partial,
        from_sibling(sent),
        weights,
        residual,
        direction,
        numbers,
    )
    home = among_cores(resident(result))
    out = shape(targets.shape, f32)
    return call(functools.partial(unpack_kernel, groups, group_rows), (out, out), home)


def solution(mesh):
    placed = (
        P(None, ("groups", "row", "col")),
        P(None, ("groups", "row", "col")),
        P(None, ("groups", "row", "col")),
        P(("groups", "row", "col")),
    )
    return jax.shard_map(
        local,
        mesh=mesh,
        in_specs=placed,
        out_specs=(P(None, ("groups", "row", "col")), P(None, ("groups", "row", "col"))),
        check_vma=False,
    )
```
